32 devices in a mesh: groups: 2 (over y), tensor: 4 (over z), dp: 4 (over x, core).
Axes of the slice: x: 2, y: 2, z: 4, core: 2. Of those that a mesh axis runs over, the one named last changes fastest.
Arguments:
- inputs: bfloat16 [8192, 4096], P(('groups', 'dp'), 'tensor'), parts along dimension 0, may hold values from -6 to 6
- gate_pre: bfloat16 [8192, 14336], P(('groups', 'dp'), 'tensor'), parts along dimension 0, may hold values from -6 to 6
- grad_out: bfloat16 [8192, 4096], P(('groups', 'dp'), 'tensor'), parts along dimension 0, may hold values from -2 to 2
- w_down: bfloat16 [14336, 4096], P('tensor'), may hold values from -0.046875 to 0.046875
- proj_in: bfloat16 [4096, 64], P('tensor'), may hold values from -0.09375 to 0.09375
- proj_out: bfloat16 [14336, 64], P('tensor'), may hold values from -0.046875 to 0.046875
- hessian: float32 [8192, 4096], P(('groups', 'tensor', 'dp')), parts along dimension 0, may hold values from -3 to 3
- queries: float32 [512, 4096], P('groups', ('tensor', 'dp')), parts along dimension 0, may hold values from -0.09375 to 0.09375
Outputs:
- updated: float32 [8192, 4096], P(('groups', 'tensor', 'dp')), parts along dimension 0
- scores: float32 [16, 256], P(('groups', 'dp')), parts along dimension 0
The draws below stay inside these ranges and needn't reach their ends.
There are 2 independent parts, one for each index of `groups`. The reference program is written for one: setup_inputs(seed, part) draws one part's arguments, and reference() takes and returns one part's arrays. A program takes and returns all parts, laid end to end along the dimension named above; an argument that names none is the same for every part. Nothing has to cross between parts.
All inputs are finite; a program needn't handle non-finite values.
Results may differ from the reference program's by a relative error of at most 0.0039.
Values may be sent and summed in bfloat16 or wider, within the bound.
No kernel may reach another device: no remote copies, remote signals or barrier semaphores. Data moves between devices by JAX's collectives and lax.ppermute only.
A program may use at most 128 MiB of HBM per device.

```python
import jax
import jax.numpy as jnp
from jax import lax

D = 4096
FF = 14336
PROJ = 64
QUERIES = 256
LEN = 512
TOKENS = 4096
EXAMPLES = 8
KK = 4096


def level_of(own_key, dims, shards, low, top_value):
    factor_of = 1.0
    for axis_at, shards_of in shards:
        steps = jax.random.uniform(jax.random.fold_in(jax.random.fold_in(own_key, 6), axis_at), (shards_of,), jnp.float32, low / len(shards), top_value / len(shards))
        factor_of = factor_of * jnp.repeat(jnp.exp(steps), dims[axis_at] // shards_of).reshape((-1,) + (1,) * (len(dims) - 1 - axis_at))
    return factor_of


def centred(own_key, shape, deviation, limit, split=(), dtype=jnp.bfloat16):
    array = jax.random.normal(own_key, shape, jnp.float32) * deviation
    if len(split) > 0:
        array = level_of(own_key, shape, split, -0.22, 0.18) * array
    return jnp.clip(array, min=-limit, max=limit).astype(dtype)


def setup_inputs(seed: int = 0, part: int = 0) -> dict:
    splits = jax.random.split(jax.random.key(seed), 9)
    own_keys = jax.random.split(jax.random.fold_in(splits[8], part), 9)
    inputs = centred(own_keys[0], (TOKENS, D), 1.0, 6.0, ((0, 4), (1, 4)))
    gate_pre = centred(own_keys[1], (TOKENS, FF), 1.0, 6.0, ((0, 4), (1, 4)))
    grad_out = centred(own_keys[2], (TOKENS, D), 0.25, 2.0, ((0, 4), (1, 4)))
    w_down = centred(splits[3], (FF, D), FF ** -0.5, 0.046875, ((0, 4),))
    proj_in = centred(splits[4], (D, PROJ), D ** -0.5, 0.09375, ((0, 4),))
    proj_out = centred(splits[5], (FF, PROJ), FF ** -0.5, 0.046875, ((0, 4),))
    hessian = centred(own_keys[6], (KK, KK), 0.5, 3.0, ((0, 16),), jnp.float32)
    queries = centred(own_keys[7], (QUERIES, KK), KK ** -0.5, 0.09375, ((1, 16),), jnp.float32)
    return {"inputs": inputs, "gate_pre": gate_pre, "grad_out": grad_out, "w_down": w_down, "proj_in": proj_in, "proj_out": proj_out, "hessian": hessian, "queries": queries}


def reference(inputs, gate_pre, grad_out, w_down, proj_in, proj_out, hessian, queries):
    hidden_grad = jnp.dot(grad_out, w_down.T, preferred_element_type=jnp.float32)
    up_grad = (hidden_grad * jax.nn.silu(gate_pre.astype(jnp.float32))).astype(jnp.bfloat16)
    in_proj = jnp.dot(inputs, proj_in, preferred_element_type=jnp.float32)
    out_proj = jnp.dot(up_grad, proj_out, preferred_element_type=jnp.float32)
    left_proj = in_proj.reshape(EXAMPLES, LEN, PROJ)
    right_proj = out_proj.reshape(EXAMPLES, LEN, PROJ)
    example_grads = jnp.einsum("sti,stj->sij", left_proj, right_proj, precision=lax.Precision.HIGHEST).reshape(EXAMPLES, PROJ * PROJ)
    updated = hessian + jnp.dot(example_grads.T, example_grads, precision=lax.Precision.HIGHEST) / EXAMPLES
    scores = jnp.dot(example_grads, queries.T, precision=lax.Precision.HIGHEST)
    return updated, scores
```

```python
import jax
import jax.numpy as jnp
from jax import lax
from jax.sharding import PartitionSpec as P

PROJ = 64
LEN = 512
HIGHEST = lax.Precision.HIGHEST


def on_device(inputs, gate_pre, grad_out, w_down, proj_in, proj_out, hessian, queries):
    tokens = grad_out.shape[0]
    in_part = jnp.dot(inputs, proj_in, preferred_element_type=jnp.float32)
    in_proj = lax.psum(in_part, "tensor")

    sizes = []
    for start in range(0, tokens, LEN):
        last = start + LEN >= tokens
        sizes += [LEN // 2, LEN // 4, LEN // 4] if last else [LEN // 2, LEN // 2]
    grads = [jnp.zeros((PROJ, PROJ), jnp.float32) for _ in range(tokens // LEN)]
    at = 0
    for size in sizes:
        rows = slice(at, at + size)
        block = lax.all_gather(grad_out[rows], "tensor", axis=1, tiled=True)
        hidden_grad = lax.dot_general(
            block, w_down, (((1,), (1,)), ((), ())), preferred_element_type=jnp.float32
        )
        up_grad = (hidden_grad * jax.nn.silu(gate_pre[rows].astype(jnp.float32))).astype(jnp.bfloat16)
        out_part = jnp.dot(up_grad, proj_out, preferred_element_type=jnp.float32)
        grads[at // LEN] += lax.dot_general(
            in_proj[rows], out_part, (((0,), (0,)), ((), ())), precision=HIGHEST
        )
        at += size
    local_grads = jnp.stack(grads).reshape(-1, PROJ * PROJ)
    parts = lax.all_gather(local_grads, ("tensor", "dp"), axis=0, tiled=True)
    all_grads = parts.reshape(lax.axis_size("tensor"), -1, PROJ * PROJ).sum(0)

    row_count = hessian.shape[0]
    row_start = lax.axis_index(("tensor", "dp")) * row_count
    mine = lax.dynamic_slice_in_dim(all_grads, row_start, row_count, 1)
    updated = hessian + jnp.dot(mine.T, all_grads, precision=HIGHEST) / all_grads.shape[0]
    score_part = jnp.dot(mine, queries.T, precision=HIGHEST)
    scores = lax.psum(score_part, ("tensor", "dp"))
    count = local_grads.shape[0]
    scores = lax.dynamic_slice_in_dim(scores, lax.axis_index("dp") * count, count, 0)
    return (updated, scores)


def solution(mesh):
    return jax.shard_map(
        on_device,
        mesh=mesh,
        in_specs=(
            P(("groups", "dp"), "tensor"),
            P(("groups", "dp"), "tensor"),
            P(("groups", "dp"), "tensor"),
            P("tensor", None),
            P("tensor", None),
            P("tensor", None),
            P(("groups", "tensor", "dp"), None),
            P("groups", ("tensor", "dp")),
        ),
        out_specs=(P(("groups", "tensor", "dp"), None), P(("groups", "dp"), None)),
        check_vma=False,
    )
```

```python
import functools

import jax
import jax.numpy as jnp
from jax import lax
from jax.experimental import pallas as pl
from jax.experimental.pallas import tpu as pltpu
from jax.sharding import PartitionSpec as P

PROJ = 64
LEN = 512
HIGHEST = lax.Precision.HIGHEST
NT = (((1,), (1,)), ((), ()))
TILE = 512
VMEM_BYTES = 40 * 2**20


def silu(v):
    return 0.5 * v * (1.0 + jnp.tanh(0.5 * v))


def dot_nt(a, b):
    return lax.dot_general(a, b, NT, preferred_element_type=jnp.float32)


def cost(flops, moved):
    return pl.CostEstimate(flops=flops, bytes_accessed=moved, transcendentals=0)


def params():
    return pltpu.CompilerParams(vmem_limit_bytes=VMEM_BYTES)


def first_body(where_ref, own_ref, pair_ref, w_own_ref, w_pair_ref, acc_ref):
    acc_ref[...] = dot_nt(own_ref[...], w_own_ref[...]) + dot_nt(pair_ref[...], w_pair_ref[...])


def first_blocks(where, own, pair, w):
    rows, feats = own.shape
    hidden = w.shape[0]
    whole = pl.BlockSpec((rows, feats), lambda j, where: (0, 0))
    return pl.pallas_call(
        first_body,
        grid_spec=pltpu.PrefetchScalarGridSpec(
            num_scalar_prefetch=1,
            grid=(hidden // TILE,),
            in_specs=[
                whole,
                whole,
                pl.BlockSpec((TILE, feats), lambda j, where: (j, where[0])),
                pl.BlockSpec((TILE, feats), lambda j, where: (j, where[1])),
            ],
            out_specs=pl.BlockSpec((rows, TILE), lambda j, where: (0, j)),
        ),
        out_shape=jax.ShapeDtypeStruct((rows, hidden), jnp.float32),
        compiler_params=params(),
        cost_estimate=cost(4 * rows * feats * hidden, 4 * rows * hidden + 4 * feats * hidden),
        name="first_blocks",
    )(where, own, pair, w, w)


def second_body(where_ref, inner_ref, outer_ref, w_ref, old_ref, acc_ref, block):
    @pl.when(pl.program_id(0) == 0)
    def _():
        block[...] = jnp.where(where_ref[4] == 1, inner_ref[...], outer_ref[...])

    acc_ref[...] = old_ref[...] + dot_nt(block[...], w_ref[...])


def second_block(where, inner, outer, w, old):
    rows, feats = inner.shape
    hidden = w.shape[0]
    whole = pl.BlockSpec((rows, feats), lambda j, where: (0, 0))
    tile = pl.BlockSpec((rows, TILE), lambda j, where: (0, j))
    return pl.pallas_call(
        second_body,
        grid_spec=pltpu.PrefetchScalarGridSpec(
            num_scalar_prefetch=1,
            grid=(hidden // TILE,),
            in_specs=[
                whole,
                whole,
                pl.BlockSpec((TILE, feats), lambda j, where: (j, where[2])),
                tile,
            ],
            out_specs=tile,
            scratch_shapes=[pltpu.VMEM((rows, feats), jnp.bfloat16)],
        ),
        out_shape=jax.ShapeDtypeStruct((rows, hidden), jnp.float32),
        input_output_aliases={4: 0},
        compiler_params=params(),
        cost_estimate=cost(2 * rows * feats * hidden, 8 * rows * hidden + 2 * feats * hidden),
        name="second_block",
    )(where, inner, outer, w, old)


def last_body(
    where_ref, inner_ref, outer_ref, w_ref, old_ref, gate_ref, po_ref, left_ref, grads_in, early_ref, grads_ref, block, right
):
    step = pl.program_id(0)

    @pl.when(step == 0)
    def _():
        block[...] = jnp.where(where_ref[4] == 1, inner_ref[...], outer_ref[...])
        right[...] = jnp.zeros_like(right)

    hidden_grad = old_ref[...] + dot_nt(block[...], w_ref[...])
    up_grad = (hidden_grad * silu(gate_ref[...].astype(jnp.float32))).astype(jnp.bfloat16)
    right[...] += dot_nt(up_grad, po_ref[...])

    @pl.when(step == pl.num_programs(0) - 1)
    def _():
        grads_ref[...] = grads_in[...] + jnp.dot(
            left_ref[...], right[...], precision=HIGHEST, preferred_element_type=jnp.float32
        )


def last_block(where, inner, outer, at, w, old, gate, po_t, left_t, grads, early):
    size, feats = outer.shape
    hidden = w.shape[0]
    chunk = at // size
    tile = pl.BlockSpec((size, TILE), lambda j, where: (chunk, j))
    small = pl.BlockSpec((PROJ, PROJ), lambda j, where: (0, 0))
    return pl.pallas_call(
        last_body,
        grid_spec=pltpu.PrefetchScalarGridSpec(
            num_scalar_prefetch=1,
            grid=(hidden // TILE,),
            in_specs=[
                pl.BlockSpec((size, feats), lambda j, where: (chunk, 0)),
                pl.BlockSpec((size, feats), lambda j, where: (0, 0)),
                pl.BlockSpec((TILE, feats), lambda j, where: (j, where[3])),
                tile,
                tile,
                pl.BlockSpec((PROJ, TILE), lambda j, where: (0, j)),
                pl.BlockSpec((PROJ, size), lambda j, where: (0, chunk)),
                small,
                pl.BlockSpec(memory_space=pl.ANY),
            ],
            out_specs=small,
            scratch_shapes=[
                pltpu.VMEM((size, feats), jnp.bfloat16),
                pltpu.VMEM((size, PROJ), jnp.float32),
            ],
        ),
        out_shape=jax.ShapeDtypeStruct((PROJ, PROJ), jnp.float32),
        compiler_params=params(),
        cost_estimate=cost(2 * size * (feats + PROJ) * hidden, 6 * size * hidden + 2 * feats * hidden),
        name="last_block",
    )(where, inner, outer, w, old, gate, po_t, left_t, grads, early)


def pieces(a):
    high = a.astype(jnp.bfloat16)
    rest = a - high.astype(jnp.float32)
    middle = rest.astype(jnp.bfloat16)
    low = (rest - middle.astype(jnp.float32)).astype(jnp.bfloat16)
    return high, middle, low


def update_body(row_ref, scale, grads_ref, mine_ref, hessian_ref, out_ref):
    high, middle, low = pieces(mine_ref[...])
    left = jnp.concatenate([high, high, middle, middle, high, low], axis=0)
    high, middle, low = pieces(grads_ref[...])
    right = jnp.concatenate([high, middle, high, middle, low, high], axis=0)
    total = lax.dot_general(left, right, (((0,), (0,)), ((), ())), preferred_element_type=jnp.float32)
    out_ref[...] = hessian_ref[...] + total * scale


def update(row, grads, hessian):
    rows, columns = hessian.shape
    count = grads.shape[0]
    width = min(columns, 512)
    tile = pl.BlockSpec((rows, width), lambda j, row: (0, j))

    def body(row_ref, *refs):
        update_body(row_ref, 1.0 / count, *refs)

    return pl.pallas_call(
        body,
        grid_spec=pltpu.PrefetchScalarGridSpec(
            num_scalar_prefetch=1,
            grid=(columns // width,),
            in_specs=[
                pl.BlockSpec((count, width), lambda j, row: (0, j)),
                pl.BlockSpec((count, rows), lambda j, row: (0, row[0])),
                tile,
            ],
            out_specs=tile,
        ),
        out_shape=jax.ShapeDtypeStruct((rows, columns), jnp.float32),
        compiler_params=params(),
        cost_estimate=cost(2 * 48 * rows * columns, 8 * rows * columns),
        name="hessian_update",
    )(row, grads, grads, hessian)


def line_of_four(inputs, gate_pre, grad_out, w_down, proj_in, proj_out, early):
    send = functools.partial(lax.ppermute, axis_name="tensor")
    pairs = [(0, 1), (1, 0), (2, 3), (3, 2)]
    inner = [(1, 2), (2, 1)]
    outward = [(1, 0), (2, 3)]
    inward = [(0, 1), (3, 2)]
    tokens = grad_out.shape[0]
    z = lax.axis_index("tensor")
    low = z < 2
    middle = jnp.logical_and(z > 0, z < 3)
    where = jnp.stack(
        [z, z + 1 - 2 * (z % 2), jnp.where(low, 2, 1), jnp.where(low, 3, 0), middle.astype(z.dtype)]
    ).astype(jnp.int32)

    pair = send(grad_out, perm=pairs)
    far_middle_inner = send(grad_out, perm=inner)
    in_part = lax.dot_general(
        proj_in, inputs, (((0,), (1,)), ((), ())), preferred_element_type=jnp.float32
    )
    side = in_part + send(in_part, perm=inward)
    total = side + send(side, perm=inner)
    left_t = jnp.where(middle, total, send(total, perm=outward))

    far_middle_outer = send(far_middle_inner, perm=outward)
    far_end_inner = send(pair, perm=inner)
    acc = first_blocks(where, grad_out, pair, w_down)
    acc = second_block(where, far_middle_inner, far_middle_outer, w_down, acc)

    grads = [jnp.zeros((PROJ, PROJ), jnp.float32) for _ in range(tokens // LEN)]
    at = 0
    while at < tokens:
        size = 256 if at + 256 < tokens else 128
        far_end_outer = send(far_end_inner[at : at + size], perm=outward)
        grads[at // LEN] = last_block(
            where, far_end_inner, far_end_outer, at, w_down, acc, gate_pre, proj_out.T, left_t, grads[at // LEN], early
        )
        at += size
    return jnp.stack(grads).reshape(-1, PROJ * PROJ)


def any_line(inputs, gate_pre, grad_out, w_down, proj_in, proj_out, early):
    in_part = jnp.dot(inputs, proj_in, preferred_element_type=jnp.float32)
    in_proj = lax.psum(in_part, "tensor").reshape(-1, LEN, PROJ)
    gathered = lax.all_gather(grad_out, "tensor", axis=1, tiled=True)
    up_grad = (dot_nt(gathered, w_down) * silu(gate_pre.astype(jnp.float32))).astype(jnp.bfloat16)
    out_part = jnp.dot(up_grad, proj_out, preferred_element_type=jnp.float32).reshape(-1, LEN, PROJ)
    grads = jnp.einsum("sti,stj->sij", in_proj, out_part, precision=HIGHEST)
    return grads.reshape(-1, PROJ * PROJ)


def xor_parts(a, axis):
    size = lax.axis_size(axis)
    return [a] + [lax.ppermute(a, axis, [(i, i ^ s) for i in range(size)]) for s in range(1, size)]


def xor_sum(a, axis):
    terms = xor_parts(a, axis)
    while len(terms) > 1:
        terms = [terms[i] + terms[i + 1] for i in range(0, len(terms), 2)]
    return terms[0]


def gather_queries(queries):
    rows, width = queries.shape
    me = lax.axis_index("dp")
    whole = jnp.zeros((rows, width * lax.axis_size("dp")), queries.dtype)
    for s, part in enumerate(xor_parts(queries, "dp")):
        whole = lax.dynamic_update_slice_in_dim(whole, part, (me ^ s) * width, 1)
    return whole


def on_device(inputs, gate_pre, grad_out, w_down, proj_in, proj_out, hessian, queries):
    z_queries = gather_queries(queries)
    line = line_of_four if lax.axis_size("tensor") == 4 else any_line
    grads = line(inputs, gate_pre, grad_out, w_down, proj_in, proj_out, z_queries)
    grads = xor_sum(grads, "tensor")

    width = z_queries.shape[1]
    quarter = lax.dynamic_slice_in_dim(grads, lax.axis_index("tensor") * width, width, 1)
    scores = xor_sum(jnp.dot(quarter, z_queries.T, precision=HIGHEST), "tensor")

    all_grads = jnp.concatenate(xor_parts(grads, "dp"), axis=0)
    row_count = hessian.shape[0]
    at = lax.axis_index(("tensor", "dp"))
    if row_count % 128:
        mine = lax.dynamic_slice_in_dim(all_grads, at * row_count, row_count, 1)
        updated = hessian + jnp.dot(mine.T, all_grads, precision=HIGHEST) / all_grads.shape[0]
    else:
        updated = update(at.reshape(1).astype(jnp.int32), all_grads, hessian)
    return (updated, scores)


def solution(mesh):
    return jax.shard_map(
        on_device,
        mesh=mesh,
        in_specs=(
            P(("groups", "dp"), "tensor"),
            P(("groups", "dp"), "tensor"),
            P(("groups", "dp"), "tensor"),
            P("tensor", None),
            P("tensor", None),
            P("tensor", None),
            P(("groups", "tensor", "dp"), None),
            P("groups", ("tensor", "dp")),
        ),
        out_specs=(P(("groups", "tensor", "dp"), None), P(("groups", "dp"), None)),
        check_vma=False,
    )
```

```python
import functools

import jax
import jax.numpy as jnp
from jax import lax
from jax.experimental import pallas as pl
from jax.experimental.pallas import tpu as pltpu
from jax.sharding import PartitionSpec as P

PROJ = 64
LEN = 512
HIGHEST = lax.Precision.HIGHEST
NT = (((1,), (1,)), ((), ()))
TILE = 512
LAST_TILE = 896
VMEM_BYTES = 28 * 2**20
ANYWHERE = pl.BlockSpec(memory_space=pl.ANY)


def silu(v):
    return 0.5 * v * (1.0 + jnp.tanh(0.5 * v))


def dot(a, b):
    return jnp.dot(a, b, preferred_element_type=jnp.float32)


def dot_nt(a, b):
    return lax.dot_general(a, b, NT, preferred_element_type=jnp.float32)


def call(body, name, where, grid, operands, in_specs, out_specs, out_shapes, scratch, flops, after=(), aliases=None):
    def with_after(*refs):
        head = 1 + len(operands)
        body(*refs[:head], *refs[head + len(after) :])

    moved = sum(a.size * a.dtype.itemsize for a in operands) + sum(s.size * s.dtype.itemsize for s in out_shapes)
    return pl.pallas_call(
        with_after,
        grid_spec=pltpu.PrefetchScalarGridSpec(
            num_scalar_prefetch=1,
            grid=grid,
            in_specs=list(in_specs) + [ANYWHERE] * len(after),
            out_specs=out_specs,
            scratch_shapes=scratch,
        ),
        out_shape=out_shapes,
        input_output_aliases=aliases or {},
        compiler_params=pltpu.CompilerParams(vmem_limit_bytes=VMEM_BYTES),
        cost_estimate=pl.CostEstimate(flops=flops, bytes_accessed=min(moved, flops // 300), transcendentals=0),
        name=name,
    )(where, *operands, *after)


def fixed(shape):
    return pl.BlockSpec(shape, lambda j, where: (0, 0), pipeline_mode=pl.Buffered(1))


def own_body(where, own, w, gate, inputs, pi_t, *rest):
    *accs, gate_t, in_t, own_t = rest
    half = accs[0].shape[1]

    @pl.when(pl.program_id(0) == 0)
    def _():
        own_t[...] = own[...].T
        in_t[...] = dot_nt(pi_t[...], inputs[...])

    gate_t[...] = gate[...].T
    for h, acc in enumerate(accs):
        acc[...] = dot(w[...], own_t[:, h * half : (h + 1) * half])


def own_block(where, own, w, gate, inputs, pi_t, halves):
    tokens, feats = own.shape
    hidden = w.shape[0]
    half = tokens // halves
    acc = jax.ShapeDtypeStruct((hidden, half), jnp.float32)
    return call(
        own_body,
        "own_block",
        where,
        (hidden // TILE,),
        (own, w, gate, inputs, pi_t),
        [
            fixed(own.shape),
            pl.BlockSpec((TILE, feats), lambda j, where: (j, where[0])),
            pl.BlockSpec((tokens, TILE), lambda j, where: (0, j)),
            fixed(inputs.shape),
            fixed(pi_t.shape),
        ],
        [pl.BlockSpec((TILE, half), lambda j, where: (j, 0))] * halves
        + [
            pl.BlockSpec((TILE, tokens), lambda j, where: (j, 0)),
            pl.BlockSpec((PROJ, tokens), lambda j, where: (0, 0)),
        ],
        [acc] * halves
        + [
            jax.ShapeDtypeStruct((hidden, tokens), gate.dtype),
            jax.ShapeDtypeStruct((PROJ, tokens), jnp.float32),
        ],
        [pltpu.VMEM((feats, tokens), own.dtype)],
        2 * tokens * feats * hidden,
    )


def pair_body(where, pair, w, *rest):
    halves = (len(rest) - 1) // 2
    pair_t = rest[-1]
    half = rest[0].shape[1]

    @pl.when(pl.program_id(0) == 0)
    def _():
        pair_t[...] = pair[...].T

    for h in range(halves):
        rest[halves + h][...] = rest[h][...] + dot(w[...], pair_t[:, h * half : (h + 1) * half])


def pair_block(where, pair, w, accs, after):
    tokens, feats = pair.shape
    hidden = w.shape[0]
    tiles = [pl.BlockSpec((TILE, acc.shape[1]), lambda j, where: (j, 0)) for acc in accs]
    return call(
        pair_body,
        "pair_block",
        where,
        (hidden // TILE,),
        (pair, w, *accs),
        [fixed(pair.shape), pl.BlockSpec((TILE, feats), lambda j, where: (j, where[1]))] + tiles,
        tiles,
        [jax.ShapeDtypeStruct(acc.shape, acc.dtype) for acc in accs],
        [pltpu.VMEM((feats, tokens), pair.dtype)],
        2 * tokens * feats * hidden,
        after=after,
        aliases={3 + h: h for h in range(len(accs))},
    )


def select_transposed(where, inner, outer):
    return jnp.where(where[4] == 1, inner[...], outer[...]).T


def third_body(where, inner, outer, w, old, acc, block_t):
    @pl.when(pl.program_id(0) == 0)
    def _():
        block_t[...] = select_transposed(where, inner, outer)

    acc[...] = old[...] + dot(w[...], block_t[...])


def third_block(where, inner, outer, w, old):
    tokens, feats = inner.shape
    hidden = w.shape[0]
    tile = pl.BlockSpec((TILE, tokens), lambda j, where: (j, 0))
    (acc,) = call(
        third_body,
        "third_block",
        where,
        (hidden // TILE,),
        (inner, outer, w, old),
        [
            fixed(inner.shape),
            fixed(outer.shape),
            pl.BlockSpec((TILE, feats), lambda j, where: (j, where[2])),
            tile,
        ],
        [tile],
        [jax.ShapeDtypeStruct(old.shape, old.dtype)],
        [pltpu.VMEM((feats, tokens), inner.dtype)],
        2 * tokens * feats * hidden,
        aliases={4: 0},
    )
    return acc


def last_body(where, inner, outer, w, old, gate_t, po_t, left_t, grads_in, grads, block_t, right_t):
    step = pl.program_id(0)

    @pl.when(step == 0)
    def _():
        block_t[...] = select_transposed(where, inner, outer)
        right_t[...] = jnp.zeros_like(right_t)

    hidden_grad = old[...] + dot(w[...], block_t[...])
    up_grad = (hidden_grad * silu(gate_t[...].astype(jnp.float32))).astype(jnp.bfloat16)
    right_t[...] += dot(po_t[...], up_grad)

    @pl.when(step == pl.num_programs(0) - 1)
    def _():
        grads[...] = grads_in[...] + lax.dot_general(
            left_t[...], right_t[...], NT, precision=HIGHEST, preferred_element_type=jnp.float32
        )


def last_block(where, inner, outer, at, in_half, w, old, gate_t, po_t, left_t, grads):
    size, feats = outer.shape
    hidden = w.shape[0]
    chunk, half_chunk = at // size, in_half // size
    small = pl.BlockSpec((PROJ, PROJ), lambda j, where: (0, 0))
    (grads,) = call(
        last_body,
        "last_block",
        where,
        (hidden // LAST_TILE,),
        (inner, outer, w, old, gate_t, po_t, left_t, grads),
        [
            pl.BlockSpec((size, feats), lambda j, where: (half_chunk, 0), pipeline_mode=pl.Buffered(1)),
            fixed(outer.shape),
            pl.BlockSpec((LAST_TILE, feats), lambda j, where: (j, where[3])),
            pl.BlockSpec((LAST_TILE, size), lambda j, where: (j, half_chunk)),
            pl.BlockSpec((LAST_TILE, size), lambda j, where: (j, chunk)),
            pl.BlockSpec((PROJ, LAST_TILE), lambda j, where: (0, j)),
            pl.BlockSpec((PROJ, size), lambda j, where: (0, chunk)),
            small,
        ],
        [small],
        [jax.ShapeDtypeStruct((PROJ, PROJ), jnp.float32)],
        [pltpu.VMEM((feats, size), outer.dtype), pltpu.VMEM((PROJ, size), jnp.float32)],
        2 * size * (feats + PROJ) * hidden,
    )
    return grads


def pieces(a):
    high = a.astype(jnp.bfloat16)
    rest = a - high.astype(jnp.float32)
    middle = rest.astype(jnp.bfloat16)
    low = (rest - middle.astype(jnp.float32)).astype(jnp.bfloat16)
    return high, middle, low


def update_body(scale, row, grads, mine, hessian, out):
    high, middle, low = pieces(mine[...])
    left = jnp.concatenate([high, high, middle, middle, high, low], axis=0)
    high, middle, low = pieces(grads[...])
    right = jnp.concatenate([high, middle, high, middle, low, high], axis=0)
    total = lax.dot_general(left, right, (((0,), (0,)), ((), ())), preferred_element_type=jnp.float32)
    out[...] = hessian[...] + total * scale


def update(row, grads, hessian):
    rows, columns = hessian.shape
    count = grads.shape[0]
    width = min(columns, 512)
    tile = pl.BlockSpec((rows, width), lambda j, row: (0, j))
    (updated,) = call(
        functools.partial(update_body, 1.0 / count),
        "hessian_update",
        row,
        (columns // width,),
        (grads, grads, hessian),
        [
            pl.BlockSpec((count, width), lambda j, row: (0, j)),
            pl.BlockSpec((count, rows), lambda j, row: (0, row[0])),
            tile,
        ],
        [tile],
        [jax.ShapeDtypeStruct((rows, columns), jnp.float32)],
        [],
        2 * 48 * rows * columns,
    )
    return updated


def line_of_four(inputs, gate_pre, grad_out, w_down, proj_in, proj_out, early):
    send = functools.partial(lax.ppermute, axis_name="tensor")
    pairs = [(0, 1), (1, 0), (2, 3), (3, 2)]
    inner = [(1, 2), (2, 1)]
    outward = [(1, 0), (2, 3)]
    inward = [(0, 1), (3, 2)]
    tokens = grad_out.shape[0]
    halves = 2
    half = tokens // halves
    z = lax.axis_index("tensor")
    low = z < 2
    middle = jnp.logical_and(z > 0, z < 3)
    where = jnp.stack(
        [z, z + 1 - 2 * (z % 2), jnp.where(low, 2, 1), jnp.where(low, 3, 0), middle.astype(z.dtype)]
    ).astype(jnp.int32)

    def part(a, h):
        return a[h * half : (h + 1) * half]

    pair = send(grad_out, perm=pairs)
    mid_inner = [send(part(grad_out, h), perm=inner) for h in range(halves)]
    *accs, gate_t, in_part = own_block(where, grad_out, w_down, gate_pre, inputs, proj_in.T, halves)
    mid_outer = [send(a, perm=outward) for a in mid_inner]
    end_inner = [send(part(pair, h), perm=inner) for h in range(halves)]
    accs = pair_block(where, pair, w_down, accs, [early])

    side = in_part + send(in_part, perm=inward)
    total = side + send(side, perm=inner)
    left_t = jnp.where(middle, total, send(total, perm=outward))

    accs = [third_block(where, mid_inner[h], mid_outer[h], w_down, accs[h]) for h in range(halves)]

    grads = [jnp.zeros((PROJ, PROJ), jnp.float32) for _ in range(tokens // LEN)]
    for h in range(halves):
        at = 0
        while at < half:
            size = 256 if h + 1 < halves or at + 256 < half else 128
            end_outer = send(end_inner[h][at : at + size], perm=outward)
            whole_at = h * half + at
            s = whole_at // LEN
            grads[s] = last_block(
                where, end_inner[h], end_outer, whole_at, at, w_down, accs[h], gate_t, proj_out.T, left_t, grads[s]
            )
            at += size
    return jnp.stack(grads).reshape(-1, PROJ * PROJ)


def any_line(inputs, gate_pre, grad_out, w_down, proj_in, proj_out, early):
    in_part = jnp.dot(inputs, proj_in, preferred_element_type=jnp.float32)
    in_proj = lax.psum(in_part, "tensor").reshape(-1, LEN, PROJ)
    gathered = lax.all_gather(grad_out, "tensor", axis=1, tiled=True)
    up_grad = (dot_nt(gathered, w_down) * silu(gate_pre.astype(jnp.float32))).astype(jnp.bfloat16)
    out_part = jnp.dot(up_grad, proj_out, preferred_element_type=jnp.float32).reshape(-1, LEN, PROJ)
    grads = jnp.einsum("sti,stj->sij", in_proj, out_part, precision=HIGHEST)
    return grads.reshape(-1, PROJ * PROJ)


def swap(a, axis, bit):
    return lax.ppermute(a, axis, [(i, i ^ bit) for i in range(lax.axis_size(axis))])


def bits(axis):
    return [1 << b for b in range(lax.axis_size(axis).bit_length() - 1)]


def xor_sum(a, axis):
    for bit in bits(axis):
        a = a + swap(a, axis, bit)
    return a


def xor_gather(a, axis):
    for bit in bits(axis):
        a = jnp.concatenate([a, swap(a, axis, bit)], axis=0)
    return a


def gather_queries(queries):
    rows, width = queries.shape
    me = lax.axis_index("dp")
    whole = jnp.zeros((rows, width * lax.axis_size("dp")), queries.dtype)
    whole = lax.dynamic_update_slice_in_dim(whole, queries, me * width, 1)
    for s in range(1, lax.axis_size("dp")):
        whole = lax.dynamic_update_slice_in_dim(whole, swap(queries, "dp", s), (me ^ s) * width, 1)
    return whole


def on_device(inputs, gate_pre, grad_out, w_down, proj_in, proj_out, hessian, queries):
    z_queries = gather_queries(queries)
    line = line_of_four if lax.axis_size("tensor") == 4 else any_line
    grads = line(inputs, gate_pre, grad_out, w_down, proj_in, proj_out, z_queries)
    grads = xor_sum(grads, "tensor")
    all_grads = xor_gather(grads, "dp")

    width = z_queries.shape[1]
    quarter = lax.dynamic_slice_in_dim(grads, lax.axis_index("tensor") * width, width, 1)
    scores = xor_sum(jnp.dot(quarter, z_queries.T, precision=HIGHEST), "tensor")

    row_count = hessian.shape[0]
    at = lax.axis_index(("tensor", "dp"))
    if row_count % 128:
        mine = lax.dynamic_slice_in_dim(all_grads, at * row_count, row_count, 1)
        updated = hessian + jnp.dot(mine.T, all_grads, precision=HIGHEST) / all_grads.shape[0]
    else:
        updated = update(at.reshape(1).astype(jnp.int32), all_grads, hessian)
    return (updated, scores)


def solution(mesh):
    return jax.shard_map(
        on_device,
        mesh=mesh,
        in_specs=(
            P(("groups", "dp"), "tensor"),
            P(("groups", "dp"), "tensor"),
            P(("groups", "dp"), "tensor"),
            P("tensor", None),
            P("tensor", None),
            P("tensor", None),
            P(("groups", "tensor", "dp"), None),
            P("groups", ("tensor", "dp")),
        ),
        out_specs=(P(("groups", "tensor", "dp"), None), P(("groups", "dp"), None)),
        check_vma=False,
    )
```

```python
import functools

import jax
import jax.numpy as jnp
from jax import lax
from jax.experimental import pallas as pl
from jax.experimental.pallas import tpu as pltpu
from jax.sharding import PartitionSpec as P

PROJ = 64
LEN = 512
HIGHEST = lax.Precision.HIGHEST
NT = (((1,), (1,)), ((), ()))
TILE = 512
VMEM_BYTES = 56 * 2**20
ANYWHERE = pl.BlockSpec(memory_space=pl.ANY)


def silu(v):
    return 0.5 * v * (1.0 + jnp.tanh(0.5 * v))


def dot(a, b):
    return jnp.dot(a, b, preferred_element_type=jnp.float32)


def dot_nt(a, b):
    return lax.dot_general(a, b, NT, preferred_element_type=jnp.float32)


def call(body, name, where, grid, operands, in_specs, out_specs, out_shapes, scratch):
    return pl.pallas_call(
        body,
        grid_spec=pltpu.PrefetchScalarGridSpec(
            num_scalar_prefetch=1, grid=grid, in_specs=in_specs, out_specs=out_specs, scratch_shapes=scratch
        ),
        out_shape=out_shapes,
        compiler_params=pltpu.CompilerParams(vmem_limit_bytes=VMEM_BYTES),
        cost_estimate=pl.CostEstimate(flops=1000, bytes_accessed=1000, transcendentals=0),
        name=name,
    )(where, *operands)


def after(a, *others):
    return lax.optimization_barrier((a, *others))[0]


def fixed(shape):
    return pl.BlockSpec(shape, lambda j, where: (0, 0), pipeline_mode=pl.Buffered(1))


def prepare_body(where, gate, inputs, pi_t, gate_t, in_t):
    @pl.when(pl.program_id(0) == 0)
    def _():
        in_t[...] = dot_nt(pi_t[...], inputs[...])

    gate_t[...] = gate[...].T


def prepare(where, gate, inputs, pi_t):
    tokens, hidden = gate.shape
    return call(
        prepare_body,
        "prepare",
        where,
        (hidden // TILE,),
        (gate, inputs, pi_t),
        [
            pl.BlockSpec((tokens, TILE), lambda j, where: (0, j)),
            fixed(inputs.shape),
            fixed(pi_t.shape),
        ],
        [
            pl.BlockSpec((TILE, tokens), lambda j, where: (j, 0)),
            pl.BlockSpec((PROJ, tokens), lambda j, where: (0, 0)),
        ],
        [
            jax.ShapeDtypeStruct((hidden, tokens), gate.dtype),
            jax.ShapeDtypeStruct((PROJ, tokens), jnp.float32),
        ],
        [],
    )


def columns(where, i, width):
    return pl.ds(pl.multiple_of(where[i] * width, width), width)


def copies(sources, slots, sems):
    started = [pltpu.make_async_copy(src, slots.at[t], sems.at[t]) for t, src in enumerate(sources)]
    for copy in started:
        copy.start()
    return started


def select_transposed(where, inner, outer):
    return jnp.where(where[4] == 1, inner[...], outer[...]).T


def blocks_body(where, own, pair, inner, outer, w, acc, block_t, w_slots, acc_slots, w_sems, acc_sems):
    feats = own.shape[1]
    tiles = acc_slots.shape[0]
    rows = [pl.ds(t * TILE, TILE) for t in range(tiles)]
    reads = copies([w.at[rows[t], columns(where, i, feats)] for t in range(tiles) for i in range(3)], w_slots, w_sems)
    block_t[0] = own[...].T
    block_t[1] = pair[...].T
    block_t[2] = select_transposed(where, inner, outer)
    writes = []
    for t in range(tiles):
        total = None
        for i in range(3):
            reads[3 * t + i].wait()
            term = dot(w_slots[3 * t + i], block_t[i])
            total = term if total is None else total + term
        acc_slots[t] = total
        writes.append(pltpu.make_async_copy(acc_slots.at[t], acc.at[rows[t]], acc_sems.at[t]))
        writes[t].start()
    for write in writes:
        write.wait()


def three_blocks(where, own, pair, h, inner, outer, w):
    half, feats = inner.shape
    hidden = w.shape[0]
    tiles = hidden // TILE
    rows = pl.BlockSpec((half, feats), lambda j, where: (h, 0), pipeline_mode=pl.Buffered(1))
    (acc,) = call(
        blocks_body,
        "three_blocks",
        where,
        (1,),
        (own, pair, inner, outer, w),
        [rows, rows, fixed(inner.shape), fixed(outer.shape), ANYWHERE],
        [ANYWHERE],
        [jax.ShapeDtypeStruct((hidden, half), jnp.float32)],
        [
            pltpu.VMEM((3, feats, half), inner.dtype),
            pltpu.VMEM((3 * tiles, TILE, feats), w.dtype),
            pltpu.VMEM((tiles, TILE, half), jnp.float32),
            pltpu.SemaphoreType.DMA((3 * tiles,)),
            pltpu.SemaphoreType.DMA((tiles,)),
        ],
    )
    return acc


def last_body(
    at,
    in_half,
    where,
    inner,
    outer,
    w,
    old,
    gate_t,
    po_t,
    left_t,
    grads_in,
    grads,
    block,
    block_t,
    w_slots,
    old_slots,
    gate_slots,
    block_sems,
    w_sems,
    old_sems,
    gate_sems,
):
    size, feats = outer.shape
    tiles = w_slots.shape[0]
    rows = [pl.ds(t * TILE, TILE) for t in range(tiles)]
    blocks = copies([inner.at[pl.ds(in_half, size)], outer], block, block_sems)
    w_reads = copies([w.at[rows[t], columns(where, 3, feats)] for t in range(tiles)], w_slots, w_sems)
    old_reads = copies([old.at[rows[t], pl.ds(in_half, size)] for t in range(tiles)], old_slots, old_sems)
    gate_reads = copies([gate_t.at[rows[t], pl.ds(at, size)] for t in range(tiles)], gate_slots, gate_sems)
    for read in blocks:
        read.wait()
    block_t[...] = select_transposed(where, block.at[0], block.at[1])
    right_t = jnp.zeros((PROJ, size), jnp.float32)
    for t in range(tiles):
        w_reads[t].wait()
        term = dot(w_slots[t], block_t[...])
        old_reads[t].wait()
        gate_reads[t].wait()
        hidden_grad = old_slots[t] + term
        up_grad = (hidden_grad * silu(gate_slots[t].astype(jnp.float32))).astype(jnp.bfloat16)
        right_t += dot(po_t[:, t * TILE : (t + 1) * TILE], up_grad)
    grads[...] = grads_in[...] + lax.dot_general(
        left_t[...], right_t, NT, precision=HIGHEST, preferred_element_type=jnp.float32
    )


def last_block(where, inner, outer, at, in_half, w, old, gate_t, po_t, left_t, grads):
    size, feats = outer.shape
    hidden = w.shape[0]
    tiles = hidden // TILE
    chunk = at // size
    (grads,) = call(
        functools.partial(last_body, at, in_half),
        "last_block",
        where,
        (1,),
        (inner, outer, w, old, gate_t, po_t, left_t, grads),
        [ANYWHERE] * 5
        + [
            fixed(po_t.shape),
            pl.BlockSpec((PROJ, size), lambda j, where: (0, chunk), pipeline_mode=pl.Buffered(1)),
            fixed(grads.shape),
        ],
        [pl.BlockSpec((PROJ, PROJ), lambda j, where: (0, 0))],
        [jax.ShapeDtypeStruct((PROJ, PROJ), jnp.float32)],
        [
            pltpu.VMEM((2, size, feats), outer.dtype),
            pltpu.VMEM((feats, size), outer.dtype),
            pltpu.VMEM((tiles, TILE, feats), w.dtype),
            pltpu.VMEM((tiles, TILE, size), jnp.float32),
            pltpu.VMEM((tiles, TILE, size), gate_t.dtype),
            pltpu.SemaphoreType.DMA((2,)),
            pltpu.SemaphoreType.DMA((tiles,)),
            pltpu.SemaphoreType.DMA((tiles,)),
            pltpu.SemaphoreType.DMA((tiles,)),
        ],
    )
    return grads


def pieces(a):
    high = a.astype(jnp.bfloat16)
    rest = a - high.astype(jnp.float32)
    middle = rest.astype(jnp.bfloat16)
    low = (rest - middle.astype(jnp.float32)).astype(jnp.bfloat16)
    return high, middle, low


def update_body(scale, row, grads, mine, hessian, out, old, new, in_sems, out_sems):
    count, columns = grads.shape
    width = old.shape[2]
    parts = columns // width
    reads = [
        pltpu.make_async_copy(hessian.at[:, pl.ds(t * width, width)], old.at[t], in_sems.at[t]) for t in range(parts)
    ]
    writes = [
        pltpu.make_async_copy(new.at[t], out.at[:, pl.ds(t * width, width)], out_sems.at[t]) for t in range(parts)
    ]
    for read in reads:
        read.start()
    high, middle, low = pieces(mine[...])
    left = jnp.concatenate([high, high, middle, middle, high, low], axis=0).T
    for t in range(parts):
        high, middle, low = pieces(grads[:, t * width : (t + 1) * width])
        right = jnp.concatenate([high, middle, high, middle, low, high], axis=0)
        total = dot(left, right) * scale
        reads[t].wait()
        new[t] = old[t] + total
        writes[t].start()
    for write in writes:
        write.wait()


def update(row, grads, hessian):
    rows, columns = hessian.shape
    count = grads.shape[0]
    parts = 4
    width = columns // parts
    (updated,) = call(
        functools.partial(update_body, 1.0 / count),
        "hessian_update",
        row,
        (1,),
        (grads, grads, hessian),
        [
            fixed(grads.shape),
            pl.BlockSpec((count, rows), lambda j, row: (0, row[0]), pipeline_mode=pl.Buffered(1)),
            ANYWHERE,
        ],
        [ANYWHERE],
        [jax.ShapeDtypeStruct((rows, columns), jnp.float32)],
        [
            pltpu.VMEM((parts, rows, width), jnp.float32),
            pltpu.VMEM((parts, rows, width), jnp.float32),
            pltpu.SemaphoreType.DMA((parts,)),
            pltpu.SemaphoreType.DMA((parts,)),
        ],
    )
    return updated


def line_of_four(inputs, gate_pre, grad_out, w_down, proj_in, proj_out, early):
    send = functools.partial(lax.ppermute, axis_name="tensor")
    pairs = [(0, 1), (1, 0), (2, 3), (3, 2)]
    inner = [(1, 2), (2, 1)]
    outward = [(1, 0), (2, 3)]
    inward = [(0, 1), (3, 2)]
    tokens = grad_out.shape[0]
    halves = 2
    half = tokens // halves
    z = lax.axis_index("tensor")
    low = z < 2
    middle = jnp.logical_and(z > 0, z < 3)
    where = jnp.stack(
        [z, z + 1 - 2 * (z % 2), jnp.where(low, 2, 1), jnp.where(low, 3, 0), middle.astype(z.dtype)]
    ).astype(jnp.int32)

    def part(a, h):
        return a[h * half : (h + 1) * half]

    pair = send(grad_out, perm=pairs)
    mid_inner = [send(part(grad_out, 0), perm=inner)]
    gate_t, in_part = prepare(where, gate_pre, inputs, proj_in.T)
    mid_inner.append(send(part(after(grad_out, mid_inner[0]), 1), perm=inner))
    mid_outer = [send(mid_inner[0], perm=outward)]

    side = in_part + after(send(in_part, perm=inward), mid_inner[0])
    total = side + send(side, perm=inner)
    left_t = jnp.where(middle, total, send(total, perm=outward))

    pair = after(pair, total, early)
    end_inner = [send(part(pair, 0), perm=inner)]
    mid_outer.append(send(after(mid_inner[1], mid_outer[0]), perm=outward))

    accs = [three_blocks(where, after(grad_out, left_t), pair, 0, mid_inner[0], mid_outer[0], w_down)]
    end_inner.append(send(part(after(pair, end_inner[0], accs[0]), 1), perm=inner))
    accs.append(three_blocks(where, grad_out, pair, 1, mid_inner[1], mid_outer[1], w_down))

    sizes = [256] * (tokens // 256 - 1) + [128, 128]
    grads = [jnp.zeros((PROJ, PROJ), jnp.float32) for _ in range(tokens // LEN)]
    arrived = [mid_outer[0], mid_outer[1]]
    done = [accs[0], accs[0], accs[1]]
    start = 0
    for n, size in enumerate(sizes):
        h, at = divmod(start, half)
        end_outer = send(after(end_inner[h][at : at + size], arrived[n], done[n]), perm=outward)
        arrived.append(end_outer)
        s = start // LEN
        grads[s] = last_block(
            where, end_inner[h], end_outer, start, at, w_down, accs[h], gate_t, proj_out.T, left_t, grads[s]
        )
        done.append(grads[s])
        start += size
    return jnp.stack(grads).reshape(-1, PROJ * PROJ)


def any_line(inputs, gate_pre, grad_out, w_down, proj_in, proj_out, early):
    in_part = jnp.dot(inputs, proj_in, preferred_element_type=jnp.float32)
    in_proj = lax.psum(in_part, "tensor").reshape(-1, LEN, PROJ)
    gathered = lax.all_gather(grad_out, "tensor", axis=1, tiled=True)
    up_grad = (dot_nt(gathered, w_down) * silu(gate_pre.astype(jnp.float32))).astype(jnp.bfloat16)
    out_part = jnp.dot(up_grad, proj_out, preferred_element_type=jnp.float32).reshape(-1, LEN, PROJ)
    grads = jnp.einsum("sti,stj->sij", in_proj, out_part, precision=HIGHEST)
    return grads.reshape(-1, PROJ * PROJ)


def swap(a, axis, bit):
    return lax.ppermute(a, axis, [(i, i ^ bit) for i in range(lax.axis_size(axis))])


def bits(axis):
    return [1 << b for b in range(lax.axis_size(axis).bit_length() - 1)]


def xor_sum(a, axis):
    for bit in bits(axis):
        a = a + swap(a, axis, bit)
    return a


def xor_gather(a, axis):
    for bit in bits(axis):
        a = jnp.concatenate([a, swap(a, axis, bit)], axis=0)
    return a


def gather_queries(queries):
    rows, width = queries.shape
    me = lax.axis_index("dp")
    whole = jnp.zeros((rows, width * lax.axis_size("dp")), queries.dtype)
    whole = lax.dynamic_update_slice_in_dim(whole, queries, me * width, 1)
    for s in range(1, lax.axis_size("dp")):
        whole = lax.dynamic_update_slice_in_dim(whole, swap(queries, "dp", s), (me ^ s) * width, 1)
    return whole


def on_device(inputs, gate_pre, grad_out, w_down, proj_in, proj_out, hessian, queries):
    z_queries = gather_queries(queries)
    line = line_of_four if lax.axis_size("tensor") == 4 else any_line
    grads = line(inputs, gate_pre, grad_out, w_down, proj_in, proj_out, z_queries)
    grads = xor_sum(grads, "tensor")

    width = z_queries.shape[1]
    quarter = lax.dynamic_slice_in_dim(grads, lax.axis_index("tensor") * width, width, 1)
    scores = jnp.dot(quarter, z_queries.T, precision=HIGHEST)
    *first, last = bits("tensor")
    for bit in first:
        scores = scores + swap(scores, "tensor", bit)
    other_scores = swap(scores, "tensor", last)

    all_grads = after(xor_gather(grads, "dp"), scores)
    row_count = hessian.shape[0]
    at = lax.axis_index(("tensor", "dp"))
    if row_count % 128:
        mine = lax.dynamic_slice_in_dim(all_grads, at * row_count, row_count, 1)
        updated = hessian + jnp.dot(mine.T, all_grads, precision=HIGHEST) / all_grads.shape[0]
    else:
        updated = update(at.reshape(1).astype(jnp.int32), all_grads, hessian)
    updated, other_scores = lax.optimization_barrier((updated, other_scores))
    return (updated, scores + other_scores)


def solution(mesh):
    return jax.shard_map(
        on_device,
        mesh=mesh,
        in_specs=(
            P(("groups", "dp"), "tensor"),
            P(("groups", "dp"), "tensor"),
            P(("groups", "dp"), "tensor"),
            P("tensor", None),
            P("tensor", None),
            P("tensor", None),
            P(("groups", "tensor", "dp"), None),
            P("groups", ("tensor", "dp")),
        ),
        out_specs=(P(("groups", "tensor", "dp"), None), P(("groups", "dp"), None)),
        check_vma=False,
    )
```

```python
import functools

import jax
import jax.numpy as jnp
from jax import lax
from jax.experimental import pallas as pl
from jax.experimental.pallas import tpu as pltpu
from jax.sharding import PartitionSpec as P

PROJ = 64
LEN = 512
HIGHEST = lax.Precision.HIGHEST
NT = (((1,), (1,)), ((), ()))
TILE = 512
OWN_TILE = 256
ANYWHERE = pl.BlockSpec(memory_space=pl.ANY)
INSIDE = pl.BlockSpec(memory_space=pltpu.VMEM)
OUTSIDE = pl.BlockSpec(memory_space=pltpu.HBM)


def silu(v):
    return 0.5 * v * (1.0 + jnp.tanh(0.5 * v))


def dot(a, b):
    return jnp.dot(a, b, preferred_element_type=jnp.float32)


def dot_nt(a, b):
    return lax.dot_general(a, b, NT, preferred_element_type=jnp.float32)


def placed(a, spec):
    if spec is INSIDE or spec is OUTSIDE:
        return pltpu.with_memory_space_constraint(a, spec.memory_space)
    return a


def call(body, name, where, grid, operands, in_specs, out_specs, out_shapes, scratch, mib, aliases=None):
    return pl.pallas_call(
        body,
        grid_spec=pltpu.PrefetchScalarGridSpec(
            num_scalar_prefetch=1, grid=grid, in_specs=in_specs, out_specs=out_specs, scratch_shapes=scratch
        ),
        out_shape=out_shapes,
        compiler_params=pltpu.CompilerParams(vmem_limit_bytes=mib * 2**20),
        cost_estimate=pl.CostEstimate(flops=1000, bytes_accessed=1000, transcendentals=0),
        name=name,
        input_output_aliases=aliases or {},
    )(where, *[placed(a, spec) for a, spec in zip(operands, in_specs)])


def after(a, *others):
    return lax.optimization_barrier((a, *others))[0]


def fixed(shape):
    return pl.BlockSpec(shape, lambda j, where: (0, 0), pipeline_mode=pl.Buffered(1))


def tile_rows(t, size=TILE):
    return pl.ds(pl.multiple_of(t * size, size), size)


def columns(where, i, width):
    return pl.ds(pl.multiple_of(where[i] * width, width), width)


def own_body(where, own, gate, inputs, pi_t, w_far, w, acc, in_t, *rest):
    *gates_t, own_t, sems = rest
    step = pl.program_id(0)
    reads = [
        pltpu.make_async_copy(w_far.at[rows], w.at[rows], sems.at[t])
        for t in range(sems.shape[0])
        for rows in [pl.ds(t * OWN_TILE, OWN_TILE)]
    ]

    @pl.when(step == 0)
    def _():
        for read in reads:
            read.start()
        in_t[...] = dot_nt(pi_t[...], inputs[...])
        own_t[...] = own[...].T

    start = 0
    for gate_t in gates_t:
        size = gate_t.shape[1]
        gate_t[...] = gate[start : start + size, :].T
        start += size
    rows = tile_rows(step, OWN_TILE)
    pltpu.make_async_copy(w_far.at[rows], w.at[rows], sems.at[step]).wait()
    acc[rows, :] = dot(w[rows, columns(where, 0, own.shape[1])], own_t[...])


def own_block(where, own, gate, inputs, pi_t, w, sizes):
    tokens, hidden = gate.shape
    feats = own.shape[1]
    return call(
        own_body,
        "own_block",
        where,
        (hidden // OWN_TILE,),
        (own, gate, inputs, pi_t, w),
        [
            fixed(own.shape),
            pl.BlockSpec((tokens, OWN_TILE), lambda j, where: (0, j)),
            fixed(inputs.shape),
            fixed(pi_t.shape),
            OUTSIDE,
        ],
        [INSIDE, INSIDE, pl.BlockSpec((PROJ, tokens), lambda j, where: (0, 0))]
        + [pl.BlockSpec((OWN_TILE, size), lambda j, where: (j, 0)) for size in sizes],
        [
            pltpu.VMEM(w.shape, w.dtype),
            pltpu.VMEM((hidden, tokens), jnp.float32),
            jax.ShapeDtypeStruct((PROJ, tokens), jnp.float32),
        ]
        + [jax.ShapeDtypeStruct((hidden, size), gate.dtype) for size in sizes],
        [pltpu.VMEM((feats, tokens), own.dtype), pltpu.SemaphoreType.DMA((hidden // OWN_TILE,))],
        16,
    )


def add_body(which, where, *refs):
    *blocks, w, old, _, acc, token, block_t = refs
    token[...] = jnp.zeros_like(token)
    if len(blocks) == 1:
        block_t[...] = blocks[0][...].T
    else:
        block_t[...] = select_transposed(where, *blocks)

    @pl.loop(0, acc.shape[0] // TILE)
    def _(t):
        rows = tile_rows(t)
        acc[rows, :] = old[rows, :] + dot(w[rows, columns(where, which, block_t.shape[0])], block_t[...])


def add_block(where, which, blocks, w, old):
    tokens, feats = blocks[0].shape
    return call(
        functools.partial(add_body, which),
        f"add_block_{which}",
        where,
        (1,),
        (*blocks, w, old),
        [fixed(a.shape) for a in blocks] + [INSIDE, INSIDE],
        [INSIDE, INSIDE, pl.BlockSpec((8, 128), lambda j, where: (0, 0))],
        [
            pltpu.VMEM(w.shape, w.dtype),
            pltpu.VMEM(old.shape, old.dtype),
            jax.ShapeDtypeStruct((8, 128), jnp.float32),
        ],
        [pltpu.VMEM((feats, tokens), blocks[0].dtype)],
        16,
        aliases={len(blocks) + 1: 0, len(blocks) + 2: 1},
    )


def select_transposed(where, inner, outer):
    return jnp.where(where[4] == 1, inner[...], outer[...]).T


def last_body(start, where, inner, outer, w, old, gate_t, po_t, left_t, *rest):
    *grads_in, w_same, old_same, grads, block_t = rest
    size, feats = outer.shape
    tokens = pl.ds(start, size)
    block_t[...] = select_transposed(where, inner, outer)

    def step(t, right_t):
        rows = tile_rows(t)
        hidden_grad = old[rows, tokens] + dot(w[rows, columns(where, 3, feats)], block_t[...])
        up_grad = (hidden_grad * silu(gate_t[rows, :].astype(jnp.float32))).astype(jnp.bfloat16)
        return right_t + dot(po_t[:, rows], up_grad)

    right_t = lax.fori_loop(0, old.shape[0] // TILE, step, jnp.zeros((PROJ, size), jnp.float32))
    total = lax.dot_general(
        left_t[...], right_t, NT, precision=HIGHEST, preferred_element_type=jnp.float32
    )
    for earlier in grads_in:
        total = total + earlier[...]
    grads[...] = total


def last_block(where, inner, outer, start, w, old, gate_t, po_t, left_t, grads):
    size, feats = outer.shape
    chunk = start // size
    return call(
        functools.partial(last_body, start),
        "last_block",
        where,
        (1,),
        (inner, outer, w, old, gate_t, po_t, left_t, *grads),
        [
            INSIDE,
            INSIDE,
            INSIDE,
            INSIDE,
            fixed(gate_t.shape),
            fixed(po_t.shape),
            pl.BlockSpec((PROJ, size), lambda j, where: (0, chunk), pipeline_mode=pl.Buffered(1)),
            *[fixed(a.shape) for a in grads],
        ],
        [INSIDE, INSIDE, pl.BlockSpec((PROJ, PROJ), lambda j, where: (0, 0))],
        [
            pltpu.VMEM(w.shape, w.dtype),
            pltpu.VMEM(old.shape, old.dtype),
            jax.ShapeDtypeStruct((PROJ, PROJ), jnp.float32),
        ],
        [pltpu.VMEM((feats, size), outer.dtype)],
        16,
        aliases={3: 0, 4: 1},
    )


def small_kernel(body, name, where, *operands):
    (out,) = call(
        body,
        name,
        where,
        (1,),
        operands,
        [fixed(a.shape) for a in operands],
        [pl.BlockSpec(operands[0].shape, lambda j, where: (0, 0))],
        [jax.ShapeDtypeStruct(operands[0].shape, operands[0].dtype)],
        [],
        16,
    )
    return out


def sum_body(where, a, b, out):
    out[...] = a[...] + b[...]


def pick_body(where, a, b, out):
    out[...] = jnp.where(where[4] == 1, a[...], b[...])


def score_body(order, grads, *rest):
    *parts, out = rest
    total = None
    for s, part in enumerate(parts):
        width = part.shape[1]
        term = lax.dot_general(
            grads[:, columns(order, s, width)],
            part[...],
            NT,
            precision=HIGHEST,
            preferred_element_type=jnp.float32,
        )
        total = term if total is None else total + term
    out[...] = total


def score_parts(order, grads, parts):
    width = parts[0].shape[1]
    shape = (grads.shape[0], parts[0].shape[0])
    if width % 128:
        slices = [lax.dynamic_slice_in_dim(grads, order[s] * width, width, 1) for s in range(len(parts))]
        return jnp.dot(jnp.concatenate(slices, axis=1), jnp.concatenate(parts, axis=1).T, precision=HIGHEST)
    (scores,) = call(
        score_body,
        "scores",
        order,
        (1,),
        (grads, *parts),
        [fixed(grads.shape)] + [fixed(a.shape) for a in parts],
        [pl.BlockSpec(shape, lambda j, order: (0, 0))],
        [jax.ShapeDtypeStruct(shape, jnp.float32)],
        [],
        16,
    )
    return scores


def pieces(a):
    high = a.astype(jnp.bfloat16)
    rest = a - high.astype(jnp.float32)
    middle = rest.astype(jnp.bfloat16)
    low = (rest - middle.astype(jnp.float32)).astype(jnp.bfloat16)
    return high, middle, low


def update_body(scale, row, grads, mine, hessian, out, old, new, in_sems, out_sems):
    count, columns = grads.shape
    width = old.shape[2]
    parts = columns // width
    reads = [
        pltpu.make_async_copy(hessian.at[:, pl.ds(t * width, width)], old.at[t], in_sems.at[t]) for t in range(parts)
    ]
    writes = [
        pltpu.make_async_copy(new.at[t], out.at[:, pl.ds(t * width, width)], out_sems.at[t]) for t in range(parts)
    ]
    for read in reads:
        read.start()
    high, middle, low = pieces(mine[...])
    left = jnp.concatenate([high, high, middle, middle, high, low], axis=0).T
    for t in range(parts):
        high, middle, low = pieces(grads[:, t * width : (t + 1) * width])
        right = jnp.concatenate([high, middle, high, middle, low, high], axis=0)
        total = dot(left, right) * scale
        reads[t].wait()
        new[t] = old[t] + total
        writes[t].start()
    for write in writes:
        write.wait()


def update(row, grads, hessian):
    rows, columns = hessian.shape
    count = grads.shape[0]
    parts = 4
    width = columns // parts
    (updated,) = call(
        functools.partial(update_body, 1.0 / count),
        "hessian_update",
        row,
        (1,),
        (grads, grads, hessian),
        [
            fixed(grads.shape),
            pl.BlockSpec((count, rows), lambda j, row: (0, row[0]), pipeline_mode=pl.Buffered(1)),
            OUTSIDE,
        ],
        [ANYWHERE],
        [jax.ShapeDtypeStruct((rows, columns), jnp.float32)],
        [
            pltpu.VMEM((parts, rows, width), jnp.float32),
            pltpu.VMEM((parts, rows, width), jnp.float32),
            pltpu.SemaphoreType.DMA((parts,)),
            pltpu.SemaphoreType.DMA((parts,)),
        ],
        16,
    )
    return updated


def line_of_four(inputs, gate_pre, grad_out, w_down, proj_in, proj_out, early):
    send = functools.partial(lax.ppermute, axis_name="tensor")
    pairs = [(0, 1), (1, 0), (2, 3), (3, 2)]
    inner = [(1, 2), (2, 1)]
    outward = [(1, 0), (2, 3)]
    inward = [(0, 1), (3, 2)]
    across = [(0, 2), (3, 1)]
    tokens = grad_out.shape[0]
    z = lax.axis_index("tensor")
    low = z < 2
    middle = jnp.logical_and(z > 0, z < 3)
    where = jnp.stack(
        [z, z + 1 - 2 * (z % 2), jnp.where(low, 2, 1), jnp.where(low, 3, 0), middle.astype(z.dtype)]
    ).astype(jnp.int32)

    sizes = [256] * (tokens // 256 - 1) + [128, 128]
    starts = [sum(sizes[:n]) for n in range(len(sizes))]
    mid_inner = send(grad_out, perm=inner)
    pair = send(grad_out, perm=pairs)
    chunks = [grad_out[start : start + size] for start, size in zip(starts, sizes)]
    w, acc, in_part, *gates_t = own_block(
        where, after(grad_out, *chunks), gate_pre, inputs, proj_in.T, w_down, sizes
    )
    mid_outer = send(after(mid_inner, in_part), perm=outward)
    end_inner = [send(after(chunk, mid_inner, pair, in_part, *early), perm=across) for chunk in chunks]

    side = small_kernel(sum_body, "side", where, in_part, after(send(in_part, perm=inward), mid_inner))
    total = small_kernel(sum_body, "total", where, side, send(side, perm=inner))
    left_t = small_kernel(pick_body, "left", where, total, send(total, perm=outward))

    w, acc, first = add_block(where, 1, [pair], w, after(acc, side))
    w, acc, _ = add_block(where, 2, [mid_inner, mid_outer], w, acc)

    grads = [[] for _ in range(tokens // LEN)]
    arrived = [mid_outer, mid_outer]
    done = [first, first, first]
    for n, (start, size) in enumerate(zip(starts, sizes)):
        ready = [left_t, *end_inner] if n < 2 else []
        end_outer = send(after(end_inner[n], arrived[n], done[n], *ready), perm=outward)
        arrived.append(end_outer)
        s = start // LEN
        w, acc, total = last_block(
            where, end_inner[n], end_outer, start, w, acc, gates_t[n], proj_out.T, left_t, grads[s]
        )
        grads[s] = [total]
        done.append(total)
    grads = lax.optimization_barrier(tuple(total for total, in grads))
    return jnp.stack(grads).reshape(-1, PROJ * PROJ)


def any_line(inputs, gate_pre, grad_out, w_down, proj_in, proj_out, early):
    in_part = jnp.dot(inputs, proj_in, preferred_element_type=jnp.float32)
    in_proj = lax.psum(in_part, "tensor").reshape(-1, LEN, PROJ)
    gathered = lax.all_gather(grad_out, "tensor", axis=1, tiled=True)
    up_grad = (dot_nt(gathered, w_down) * silu(gate_pre.astype(jnp.float32))).astype(jnp.bfloat16)
    out_part = jnp.dot(up_grad, proj_out, preferred_element_type=jnp.float32).reshape(-1, LEN, PROJ)
    grads = jnp.einsum("sti,stj->sij", in_proj, out_part, precision=HIGHEST)
    return grads.reshape(-1, PROJ * PROJ)


def swap(a, axis, bit):
    return lax.ppermute(a, axis, [(i, i ^ bit) for i in range(lax.axis_size(axis))])


def bits(axis):
    return [1 << b for b in range(lax.axis_size(axis).bit_length() - 1)]


def xor_sum(a, axis):
    for bit in bits(axis):
        a = a + swap(a, axis, bit)
    return a


def xor_gather(a, axis):
    for bit in bits(axis):
        a = jnp.concatenate([a, swap(a, axis, bit)], axis=0)
    return a


def on_device(inputs, gate_pre, grad_out, w_down, proj_in, proj_out, hessian, queries):
    count = lax.axis_size("dp")
    parts = [queries] + [swap(queries, "dp", s) for s in range(1, count)]
    line = line_of_four if lax.axis_size("tensor") == 4 else any_line
    grads = line(inputs, gate_pre, grad_out, w_down, proj_in, proj_out, parts)
    grads = xor_sum(grads, "tensor")

    me = lax.axis_index("dp")
    order = lax.axis_index("tensor") * count + jnp.stack([me ^ s for s in range(count)])
    scores = score_parts(order.astype(jnp.int32), grads, parts)
    *first, last = bits("tensor")
    for bit in first:
        scores = scores + swap(scores, "tensor", bit)
    other_scores = swap(scores, "tensor", last)

    all_grads = after(xor_gather(grads, "dp"), scores)
    row_count = hessian.shape[0]
    at = lax.axis_index(("tensor", "dp"))
    if row_count % 128:
        mine = lax.dynamic_slice_in_dim(all_grads, at * row_count, row_count, 1)
        updated = hessian + jnp.dot(mine.T, all_grads, precision=HIGHEST) / all_grads.shape[0]
    else:
        updated = update(at.reshape(1).astype(jnp.int32), all_grads, hessian)
    updated, other_scores = lax.optimization_barrier((updated, other_scores))
    return (updated, scores + other_scores)


def solution(mesh):
    return jax.shard_map(
        on_device,
        mesh=mesh,
        in_specs=(
            P(("groups", "dp"), "tensor"),
            P(("groups", "dp"), "tensor"),
            P(("groups", "dp"), "tensor"),
            P("tensor", None),
            P("tensor", None),
            P("tensor", None),
            P(("groups", "tensor", "dp"), None),
            P("groups", ("tensor", "dp")),
        ),
        out_specs=(P(("groups", "tensor", "dp"), None), P(("groups", "dp"), None)),
        check_vma=False,
    )
```

```python
import functools

import jax
import jax.numpy as jnp
from jax import lax
from jax.experimental import pallas as pl
from jax.experimental.pallas import tpu as pltpu
from jax.sharding import PartitionSpec as P

PROJ = 64
LEN = 512
HIGHEST = lax.Precision.HIGHEST
NT = (((1,), (1,)), ((), ()))
TILE = 512
LIMIT = 16
ANYWHERE = pl.BlockSpec(memory_space=pl.ANY)
INSIDE = pl.BlockSpec(memory_space=pltpu.VMEM)
OUTSIDE = pl.BlockSpec(memory_space=pltpu.HBM)


def silu(v):
    return 0.5 * v * (1.0 + jnp.tanh(0.5 * v))


def dot(a, b):
    return jnp.dot(a, b, preferred_element_type=jnp.float32)


def dot_nt(a, b):
    return lax.dot_general(a, b, NT, preferred_element_type=jnp.float32)


def placed(a, spec):
    if spec is INSIDE or spec is OUTSIDE:
        return pltpu.with_memory_space_constraint(a, spec.memory_space)
    return a


def call(body, name, where, grid, operands, in_specs, out_specs, out_shapes, scratch, mib, aliases=None):
    return pl.pallas_call(
        body,
        grid_spec=pltpu.PrefetchScalarGridSpec(
            num_scalar_prefetch=1, grid=grid, in_specs=in_specs, out_specs=out_specs, scratch_shapes=scratch
        ),
        out_shape=out_shapes,
        compiler_params=pltpu.CompilerParams(vmem_limit_bytes=mib * 2**20),
        cost_estimate=pl.CostEstimate(flops=1000, bytes_accessed=1000, transcendentals=0),
        name=name,
        input_output_aliases=aliases or {},
    )(where, *[placed(a, spec) for a, spec in zip(operands, in_specs)])


def after(a, *others):
    return lax.optimization_barrier((a, *others))[0]


def fixed(shape):
    return pl.BlockSpec(shape, lambda j, where: (0, 0), pipeline_mode=pl.Buffered(1))


def tile_rows(t, size=TILE):
    return pl.ds(pl.multiple_of(t * size, size), size)


def columns(where, i, width):
    return pl.ds(pl.multiple_of(where[i] * width, width), width)


def own_body(where, own, inputs, pi_t, w, w_last, acc, kept, in_t):
    step = pl.program_id(0)

    @pl.when(step == 0)
    def _():
        in_t[...] = dot_nt(pi_t[...], inputs[...])

    here = tile_rows(step)
    kept[here, :] = w_last[...]
    acc[:, here] = dot_nt(own[...], w[...])


def own_block(where, own, inputs, pi_t, w):
    tokens, feats = own.shape
    hidden = w.shape[0]
    return call(
        own_body,
        "own_block",
        where,
        (hidden // TILE,),
        (own, inputs, pi_t, w, w),
        [
            fixed(own.shape),
            fixed(inputs.shape),
            fixed(pi_t.shape),
            pl.BlockSpec((TILE, feats), lambda j, where: (j, where[0])),
            pl.BlockSpec((TILE, feats), lambda j, where: (j, where[3])),
        ],
        [INSIDE, INSIDE, pl.BlockSpec((PROJ, tokens), lambda j, where: (0, 0))],
        [
            pltpu.VMEM((tokens, hidden), jnp.float32),
            pltpu.VMEM((hidden, feats), w.dtype),
            jax.ShapeDtypeStruct((PROJ, tokens), jnp.float32),
        ],
        [],
        LIMIT,
    )


def select(where, inner, outer):
    return jnp.where(where[4] == 1, inner[...], outer[...])


def add_body(where, *refs):
    *blocks, w, old, acc, token, block = refs
    step = pl.program_id(0)

    @pl.when(step == 0)
    def _():
        token[...] = jnp.zeros_like(token)
        block[...] = blocks[0][...] if len(blocks) == 1 else select(where, *blocks)

    here = tile_rows(step)
    acc[:, here] = old[:, here] + dot_nt(block[...], w[...])


def add_block(where, which, blocks, w, old):
    tokens, feats = blocks[0].shape
    return call(
        add_body,
        f"add_block_{which}",
        where,
        (w.shape[0] // TILE,),
        (*blocks, w, old),
        [fixed(a.shape) for a in blocks]
        + [pl.BlockSpec((TILE, feats), lambda j, where: (j, where[which])), INSIDE],
        [INSIDE, pl.BlockSpec((8, 128), lambda j, where: (0, 0))],
        [pltpu.VMEM(old.shape, old.dtype), jax.ShapeDtypeStruct((8, 128), jnp.float32)],
        [pltpu.VMEM((tokens, feats), blocks[0].dtype)],
        LIMIT,
        aliases={len(blocks) + 2: 0},
    )


def last_body(start, where, inner, outer, kept, old, gate, po_t, token, kept_same, old_same, right, block):
    size = outer.shape[0]
    step = pl.program_id(0)

    @pl.when(step == 0)
    def _():
        block[...] = select(where, inner, outer)
        right[...] = jnp.zeros_like(right)

    here = tile_rows(step)
    hidden_grad = old[pl.ds(start, size), here] + dot_nt(block[...], kept[here, :])
    up_grad = (hidden_grad * silu(gate[...].astype(jnp.float32))).astype(jnp.bfloat16)
    right[...] += dot_nt(up_grad, po_t[...])


def last_block(where, inner, outer, start, kept, old, gate, po_t, token):
    size, feats = outer.shape
    chunk = start // size
    return call(
        functools.partial(last_body, start),
        "last_block",
        where,
        (kept.shape[0] // TILE,),
        (inner, outer, kept, old, pltpu.with_memory_space_constraint(gate, pltpu.HBM), po_t, token),
        [
            pl.BlockSpec((size, feats), lambda j, where: (chunk, 0), pipeline_mode=pl.Buffered(1)),
            fixed(outer.shape),
            INSIDE,
            INSIDE,
            pl.BlockSpec((size, TILE), lambda j, where: (chunk, j)),
            pl.BlockSpec((PROJ, TILE), lambda j, where: (0, j)),
            ANYWHERE,
        ],
        [INSIDE, INSIDE, pl.BlockSpec((size, PROJ), lambda j, where: (0, 0))],
        [
            pltpu.VMEM(kept.shape, kept.dtype),
            pltpu.VMEM(old.shape, old.dtype),
            jax.ShapeDtypeStruct((size, PROJ), jnp.float32),
        ],
        [pltpu.VMEM((size, feats), outer.dtype)],
        LIMIT,
        aliases={3: 0, 4: 1},
    )


def outer_body(spans, where, left_t, *refs):
    *rights, grads = refs
    total = None
    for (start, size), right in zip(spans, rights):
        term = jnp.dot(
            left_t[:, start : start + size], right[...], precision=HIGHEST, preferred_element_type=jnp.float32
        )
        total = term if total is None else total + term
    grads[...] = total


def outer_products(where, left_t, spans, rights):
    (grads,) = call(
        functools.partial(outer_body, spans),
        "outer_products",
        where,
        (1,),
        (left_t, *rights),
        [fixed(left_t.shape)] + [fixed(a.shape) for a in rights],
        [pl.BlockSpec((PROJ, PROJ), lambda j, where: (0, 0))],
        [jax.ShapeDtypeStruct((PROJ, PROJ), jnp.float32)],
        [],
        LIMIT,
    )
    return grads


def small_kernel(body, name, where, *operands):
    (out,) = call(
        body,
        name,
        where,
        (1,),
        operands,
        [fixed(a.shape) for a in operands],
        [pl.BlockSpec(operands[0].shape, lambda j, where: (0, 0))],
        [jax.ShapeDtypeStruct(operands[0].shape, operands[0].dtype)],
        [],
        LIMIT,
    )
    return out


def sum_body(where, a, b, out):
    out[...] = a[...] + b[...]


def pick_body(where, a, b, out):
    out[...] = jnp.where(where[4] == 1, a[...], b[...])


def score_body(order, grads, *rest):
    *parts, out = rest
    total = None
    for s, part in enumerate(parts):
        width = part.shape[1]
        term = lax.dot_general(
            grads[:, columns(order, s, width)],
            part[...],
            NT,
            precision=HIGHEST,
            preferred_element_type=jnp.float32,
        )
        total = term if total is None else total + term
    out[...] = total


def score_parts(order, grads, parts):
    width = parts[0].shape[1]
    shape = (grads.shape[0], parts[0].shape[0])
    if width % 128:
        slices = [lax.dynamic_slice_in_dim(grads, order[s] * width, width, 1) for s in range(len(parts))]
        return jnp.dot(jnp.concatenate(slices, axis=1), jnp.concatenate(parts, axis=1).T, precision=HIGHEST)
    (scores,) = call(
        score_body,
        "scores",
        order,
        (1,),
        (grads, *parts),
        [fixed(grads.shape)] + [fixed(a.shape) for a in parts],
        [pl.BlockSpec(shape, lambda j, order: (0, 0))],
        [jax.ShapeDtypeStruct(shape, jnp.float32)],
        [],
        LIMIT,
    )
    return scores


def pieces(a):
    high = a.astype(jnp.bfloat16)
    rest = a - high.astype(jnp.float32)
    middle = rest.astype(jnp.bfloat16)
    low = (rest - middle.astype(jnp.float32)).astype(jnp.bfloat16)
    return high, middle, low


def update_body(scale, row, grads, mine, hessian, out, old, new, in_sems, out_sems):
    count, columns = grads.shape
    width = old.shape[2]
    parts = columns // width
    reads = [
        pltpu.make_async_copy(hessian.at[:, pl.ds(t * width, width)], old.at[t], in_sems.at[t]) for t in range(parts)
    ]
    writes = [
        pltpu.make_async_copy(new.at[t], out.at[:, pl.ds(t * width, width)], out_sems.at[t]) for t in range(parts)
    ]
    for read in reads:
        read.start()
    high, middle, low = pieces(mine[...])
    left = jnp.concatenate([high, high, middle, middle, high, low], axis=0).T
    for t in range(parts):
        high, middle, low = pieces(grads[:, t * width : (t + 1) * width])
        right = jnp.concatenate([high, middle, high, middle, low, high], axis=0)
        total = dot(left, right) * scale
        reads[t].wait()
        new[t] = old[t] + total
        writes[t].start()
    for write in writes:
        write.wait()


def update(row, grads, hessian):
    rows, columns = hessian.shape
    count = grads.shape[0]
    parts = 4
    width = columns // parts
    (updated,) = call(
        functools.partial(update_body, 1.0 / count),
        "hessian_update",
        row,
        (1,),
        (grads, grads, hessian),
        [
            fixed(grads.shape),
            pl.BlockSpec((count, rows), lambda j, row: (0, row[0]), pipeline_mode=pl.Buffered(1)),
            OUTSIDE,
        ],
        [ANYWHERE],
        [jax.ShapeDtypeStruct((rows, columns), jnp.float32)],
        [
            pltpu.VMEM((parts, rows, width), jnp.float32),
            pltpu.VMEM((parts, rows, width), jnp.float32),
            pltpu.SemaphoreType.DMA((parts,)),
            pltpu.SemaphoreType.DMA((parts,)),
        ],
        LIMIT,
    )
    return updated


def line_of_four(inputs, gate_pre, grad_out, w_down, proj_in, proj_out, early):
    send = functools.partial(lax.ppermute, axis_name="tensor")
    pairs = [(0, 1), (1, 0), (2, 3), (3, 2)]
    inner = [(1, 2), (2, 1)]
    outward = [(1, 0), (2, 3)]
    inward = [(0, 1), (3, 2)]
    across = [(0, 2), (3, 1)]
    tokens = grad_out.shape[0]
    z = lax.axis_index("tensor")
    low = z < 2
    middle = jnp.logical_and(z > 0, z < 3)
    where = jnp.stack(
        [z, z + 1 - 2 * (z % 2), jnp.where(low, 2, 1), jnp.where(low, 3, 0), middle.astype(z.dtype)]
    ).astype(jnp.int32)

    sizes = [256] * (tokens // 256 - 1) + [128, 128]
    starts = [sum(sizes[:n]) for n in range(len(sizes))]
    mid_inner = send(grad_out, perm=inner)
    pair = send(grad_out, perm=pairs)
    acc, kept, in_part = own_block(where, after(grad_out, *early), inputs, proj_in.T, w_down)
    mid_outer = send(after(mid_inner, in_part), perm=outward)
    end_inner = send(after(grad_out, mid_inner, pair, in_part), perm=across)
    side = small_kernel(sum_body, "side", where, in_part, send(after(in_part, mid_inner, pair), perm=inward))
    acc, first = add_block(where, 1, [pair], w_down, after(acc, side))
    total = small_kernel(sum_body, "total", where, side, send(side, perm=inner))
    left_t = small_kernel(pick_body, "left", where, total, send(total, perm=outward))

    acc, second = add_block(where, 2, [mid_inner, mid_outer], w_down, acc)
    arrived = [mid_outer, mid_outer]
    done = [after(first, total), after(first, total), second]
    rights = []
    for n, (start, size) in enumerate(zip(starts, sizes)):
        chunk = end_inner[start : start + size]
        end_outer = send(after(chunk, arrived[n], done[n]), perm=outward)
        arrived.append(end_outer)
        kept, acc, right = last_block(where, end_inner, end_outer, start, kept, acc, gate_pre, proj_out.T, second)
        rights.append(right)
        done.append(right)
    grads = []
    for s in range(tokens // LEN):
        mine = [n for n, start in enumerate(starts) if start // LEN == s]
        spans = [(starts[n], sizes[n]) for n in mine]
        grads.append(outer_products(where, left_t, spans, [rights[n] for n in mine]))
    return jnp.stack(grads).reshape(-1, PROJ * PROJ)


def any_line(inputs, gate_pre, grad_out, w_down, proj_in, proj_out, early):
    in_part = jnp.dot(inputs, proj_in, preferred_element_type=jnp.float32)
    in_proj = lax.psum(in_part, "tensor").reshape(-1, LEN, PROJ)
    gathered = lax.all_gather(grad_out, "tensor", axis=1, tiled=True)
    up_grad = (dot_nt(gathered, w_down) * silu(gate_pre.astype(jnp.float32))).astype(jnp.bfloat16)
    out_part = jnp.dot(up_grad, proj_out, preferred_element_type=jnp.float32).reshape(-1, LEN, PROJ)
    grads = jnp.einsum("sti,stj->sij", in_proj, out_part, precision=HIGHEST)
    return grads.reshape(-1, PROJ * PROJ)


def swap(a, axis, bit):
    return lax.ppermute(a, axis, [(i, i ^ bit) for i in range(lax.axis_size(axis))])


def bits(axis):
    return [1 << b for b in range(lax.axis_size(axis).bit_length() - 1)]


def xor_sum(a, axis):
    for bit in bits(axis):
        a = a + swap(a, axis, bit)
    return a


def xor_gather(a, axis):
    for bit in bits(axis):
        a = jnp.concatenate([a, swap(a, axis, bit)], axis=0)
    return a


def on_device(inputs, gate_pre, grad_out, w_down, proj_in, proj_out, hessian, queries):
    count = lax.axis_size("dp")
    parts = [queries] + [swap(queries, "dp", s) for s in range(1, count)]
    line = line_of_four if lax.axis_size("tensor") == 4 else any_line
    grads = line(inputs, gate_pre, grad_out, w_down, proj_in, proj_out, parts)
    grads = xor_sum(grads, "tensor")

    me = lax.axis_index("dp")
    order = lax.axis_index("tensor") * count + jnp.stack([me ^ s for s in range(count)])
    scores = score_parts(order.astype(jnp.int32), grads, parts)
    *first, last = bits("tensor")
    for bit in first:
        scores = scores + swap(scores, "tensor", bit)
    other_scores = swap(scores, "tensor", last)

    all_grads = after(xor_gather(grads, "dp"), scores)
    row_count = hessian.shape[0]
    at = lax.axis_index(("tensor", "dp"))
    if row_count % 128:
        mine = lax.dynamic_slice_in_dim(all_grads, at * row_count, row_count, 1)
        updated = hessian + jnp.dot(mine.T, all_grads, precision=HIGHEST) / all_grads.shape[0]
    else:
        updated = update(at.reshape(1).astype(jnp.int32), all_grads, hessian)
    updated, other_scores = lax.optimization_barrier((updated, other_scores))
    return (updated, scores + other_scores)


def solution(mesh):
    return jax.shard_map(
        on_device,
        mesh=mesh,
        in_specs=(
            P(("groups", "dp"), "tensor"),
            P(("groups", "dp"), "tensor"),
            P(("groups", "dp"), "tensor"),
            P("tensor", None),
            P("tensor", None),
            P("tensor", None),
            P(("groups", "tensor", "dp"), None),
            P("groups", ("tensor", "dp")),
        ),
        out_specs=(P(("groups", "tensor", "dp"), None), P(("groups", "dp"), None)),
        check_vma=False,
    )
```

```python
import functools

import jax
import jax.numpy as jnp
from jax import lax
from jax.experimental import pallas as pl
from jax.experimental.pallas import tpu as pltpu
from jax.sharding import PartitionSpec as P

PROJ = 64
LEN = 512
HIGHEST = lax.Precision.HIGHEST
NT = (((1,), (1,)), ((), ()))
TILE = 512
LIMIT = 16
ANYWHERE = pl.BlockSpec(memory_space=pl.ANY)
INSIDE = pl.BlockSpec(memory_space=pltpu.VMEM)
OUTSIDE = pl.BlockSpec(memory_space=pltpu.HBM)


def silu(v):
    return 0.5 * v * (1.0 + jnp.tanh(0.5 * v))


def dot(a, b):
    return jnp.dot(a, b, preferred_element_type=jnp.float32)


def dot_nt(a, b):
    return lax.dot_general(a, b, NT, preferred_element_type=jnp.float32)


def placed(a, spec):
    if spec is INSIDE or spec is OUTSIDE:
        return pltpu.with_memory_space_constraint(a, spec.memory_space)
    return a


def call(body, name, where, grid, operands, in_specs, out_specs, out_shapes, scratch, mib, aliases=None, flops=1000):
    return pl.pallas_call(
        body,
        grid_spec=pltpu.PrefetchScalarGridSpec(
            num_scalar_prefetch=1, grid=grid, in_specs=in_specs, out_specs=out_specs, scratch_shapes=scratch
        ),
        out_shape=out_shapes,
        compiler_params=pltpu.CompilerParams(vmem_limit_bytes=mib * 2**20),
        cost_estimate=pl.CostEstimate(flops=flops, bytes_accessed=1000, transcendentals=0),
        name=name,
        input_output_aliases=aliases or {},
    )(where, *[placed(a, spec) for a, spec in zip(operands, in_specs)])


def after(a, *others):
    return lax.optimization_barrier((a, *others))[0]


def fixed(shape):
    return pl.BlockSpec(shape, lambda j, where: (0, 0), pipeline_mode=pl.Buffered(1))


def tile_rows(t, size=TILE):
    return pl.ds(pl.multiple_of(t * size, size), size)


def columns(where, i, width):
    return pl.ds(pl.multiple_of(where[i] * width, width), width)


def input_body(where, inputs, pi_t, in_t):
    in_t[...] = dot_nt(pi_t[...], inputs[...])


def input_block(where, inputs, pi_t):
    shape = (pi_t.shape[0], inputs.shape[0])
    (in_t,) = call(
        input_body,
        "input_block",
        where,
        (1,),
        (inputs, pi_t),
        [fixed(inputs.shape), fixed(pi_t.shape)],
        [pl.BlockSpec(shape, lambda j, where: (0, 0))],
        [jax.ShapeDtypeStruct(shape, jnp.float32)],
        [],
        LIMIT,
    )
    return in_t


def own_body(where, own, w, w_last, acc, kept, token):
    here = tile_rows(pl.program_id(0))
    token[...] = jnp.zeros_like(token)
    kept[here, :] = w_last[...]
    acc[:, here] = dot_nt(own[...], w[...])


def own_block(where, own, w):
    tokens, feats = own.shape
    hidden = w.shape[0]
    return call(
        own_body,
        "own_block",
        where,
        (hidden // TILE,),
        (own, w, w),
        [
            fixed(own.shape),
            pl.BlockSpec((TILE, feats), lambda j, where: (j, where[0])),
            pl.BlockSpec((TILE, feats), lambda j, where: (j, where[3])),
        ],
        [INSIDE, INSIDE, pl.BlockSpec((8, 128), lambda j, where: (0, 0))],
        [
            pltpu.VMEM((tokens, hidden), jnp.float32),
            pltpu.VMEM((hidden, feats), w.dtype),
            jax.ShapeDtypeStruct((8, 128), jnp.float32),
        ],
        [],
        LIMIT,
    )


def select(where, inner, outer):
    return jnp.where(where[4] == 1, inner[...], outer[...])


def add_body(where, *refs):
    *blocks, w, old, _, acc, token, block = refs
    step = pl.program_id(0)

    @pl.when(step == 0)
    def _():
        token[...] = jnp.zeros_like(token)
        if len(blocks) == 1:
            block[...] = blocks[0][...]
        else:
            half = len(blocks) // 2
            size = blocks[0].shape[0]
            for h in range(half):
                block[h * size : (h + 1) * size, :] = select(where, blocks[h], blocks[half + h])

    here = tile_rows(step)
    acc[:, here] = old[:, here] + dot_nt(block[...], w[...])


def add_block(where, which, blocks, w, old, token, flops):
    tokens, feats = old.shape[0], blocks[0].shape[1]
    return call(
        add_body,
        f"add_block_{which}",
        where,
        (w.shape[0] // TILE,),
        (*blocks, w, old, token),
        [fixed(a.shape) for a in blocks]
        + [pl.BlockSpec((TILE, feats), lambda j, where: (j, where[which])), INSIDE, ANYWHERE],
        [INSIDE, pl.BlockSpec((8, 128), lambda j, where: (0, 0))],
        [pltpu.VMEM(old.shape, old.dtype), jax.ShapeDtypeStruct((8, 128), jnp.float32)],
        [pltpu.VMEM((tokens, feats), blocks[0].dtype)],
        LIMIT,
        aliases={len(blocks) + 2: 0},
        flops=flops,
    )


def last_body(start, where, inner, outer, kept, old, gate, po_t, token, kept_same, old_same, right, block):
    size = outer.shape[0]
    step = pl.program_id(0)

    @pl.when(step == 0)
    def _():
        block[...] = select(where, inner, outer)
        right[...] = jnp.zeros_like(right)

    here = tile_rows(step)
    hidden_grad = old[pl.ds(start, size), here] + dot_nt(block[...], kept[here, :])
    up_grad = (hidden_grad * silu(gate[...].astype(jnp.float32))).astype(jnp.bfloat16)
    right[...] += dot_nt(up_grad, po_t[...])


def last_block(where, inner, inner_at, outer, start, kept, old, gate, po_t, token):
    size, feats = outer.shape
    chunk, inner_chunk = start // size, inner_at // size
    return call(
        functools.partial(last_body, start),
        "last_block",
        where,
        (kept.shape[0] // TILE,),
        (inner, outer, kept, old, pltpu.with_memory_space_constraint(gate, pltpu.HBM), po_t, token),
        [
            pl.BlockSpec((size, feats), lambda j, where: (inner_chunk, 0), pipeline_mode=pl.Buffered(1)),
            fixed(outer.shape),
            INSIDE,
            INSIDE,
            pl.BlockSpec((size, TILE), lambda j, where: (chunk, j)),
            pl.BlockSpec((PROJ, TILE), lambda j, where: (0, j)),
            ANYWHERE,
        ],
        [INSIDE, INSIDE, pl.BlockSpec((size, PROJ), lambda j, where: (0, 0))],
        [
            pltpu.VMEM(kept.shape, kept.dtype),
            pltpu.VMEM(old.shape, old.dtype),
            jax.ShapeDtypeStruct((size, PROJ), jnp.float32),
        ],
        [pltpu.VMEM((size, feats), outer.dtype)],
        LIMIT,
        aliases={3: 0, 4: 1},
    )


def outer_body(where, total, sent, *refs):
    *rights, grads = refs
    left_t = select(where, total, sent)
    start = 0
    terms = [None] * grads.shape[0]
    for right in rights:
        size = right.shape[0]
        s = start // LEN
        term = jnp.dot(
            left_t[:, start : start + size], right[...], precision=HIGHEST, preferred_element_type=jnp.float32
        )
        terms[s] = term if terms[s] is None else terms[s] + term
        start += size
    for s, term in enumerate(terms):
        grads[s] = term


def outer_products(where, total, sent, rights):
    shape = (total.shape[1] // LEN, PROJ, PROJ)
    (grads,) = call(
        outer_body,
        "outer_products",
        where,
        (1,),
        (total, sent, *rights),
        [fixed(a.shape) for a in (total, sent, *rights)],
        [pl.BlockSpec(shape, lambda j, where: (0, 0, 0))],
        [jax.ShapeDtypeStruct(shape, jnp.float32)],
        [],
        LIMIT,
    )
    return grads


def small_kernel(body, name, where, *operands):
    (out,) = call(
        body,
        name,
        where,
        (1,),
        operands,
        [fixed(a.shape) for a in operands],
        [pl.BlockSpec(operands[0].shape, lambda j, where: (0, 0))],
        [jax.ShapeDtypeStruct(operands[0].shape, operands[0].dtype)],
        [],
        LIMIT,
    )
    return out


def sum_body(where, a, b, out):
    out[...] = a[...] + b[...]


def score_body(order, grads, *rest):
    *parts, out = rest
    total = None
    for s, part in enumerate(parts):
        width = part.shape[1]
        term = lax.dot_general(
            grads[:, columns(order, s, width)],
            part[...],
            NT,
            precision=HIGHEST,
            preferred_element_type=jnp.float32,
        )
        total = term if total is None else total + term
    out[...] = total


def score_parts(order, grads, parts):
    width = parts[0].shape[1]
    shape = (grads.shape[0], parts[0].shape[0])
    if width % 128:
        slices = [lax.dynamic_slice_in_dim(grads, order[s] * width, width, 1) for s in range(len(parts))]
        return jnp.dot(jnp.concatenate(slices, axis=1), jnp.concatenate(parts, axis=1).T, precision=HIGHEST)
    (scores,) = call(
        score_body,
        "scores",
        order,
        (1,),
        (grads, *[pltpu.with_memory_space_constraint(a, pltpu.HBM) for a in parts]),
        [fixed(grads.shape)] + [fixed(a.shape) for a in parts],
        [pl.BlockSpec(shape, lambda j, order: (0, 0))],
        [jax.ShapeDtypeStruct(shape, jnp.float32)],
        [],
        LIMIT,
    )
    return scores


def pieces(a):
    high = a.astype(jnp.bfloat16)
    rest = a - high.astype(jnp.float32)
    middle = rest.astype(jnp.bfloat16)
    low = (rest - middle.astype(jnp.float32)).astype(jnp.bfloat16)
    return high, middle, low


def update_body(scale, row, grads, mine, hessian, out, old, new, in_sems, out_sems):
    count, columns = grads.shape
    width = old.shape[2]
    parts = columns // width
    reads = [
        pltpu.make_async_copy(hessian.at[:, pl.ds(t * width, width)], old.at[t], in_sems.at[t]) for t in range(parts)
    ]
    writes = [
        pltpu.make_async_copy(new.at[t], out.at[:, pl.ds(t * width, width)], out_sems.at[t]) for t in range(parts)
    ]
    for read in reads:
        read.start()
    high, middle, low = pieces(mine[...])
    left = jnp.concatenate([high, high, middle, middle, high, low], axis=0).T
    for t in range(parts):
        high, middle, low = pieces(grads[:, t * width : (t + 1) * width])
        right = jnp.concatenate([high, middle, high, middle, low, high], axis=0)
        total = dot(left, right) * scale
        reads[t].wait()
        new[t] = old[t] + total
        writes[t].start()
    for write in writes:
        write.wait()


def update(row, grads, hessian):
    rows, columns = hessian.shape
    count = grads.shape[0]
    parts = 4
    width = columns // parts
    (updated,) = call(
        functools.partial(update_body, 1.0 / count),
        "hessian_update",
        row,
        (1,),
        (grads, grads, hessian),
        [
            fixed(grads.shape),
            pl.BlockSpec((count, rows), lambda j, row: (0, row[0]), pipeline_mode=pl.Buffered(1)),
            OUTSIDE,
        ],
        [ANYWHERE],
        [jax.ShapeDtypeStruct((rows, columns), jnp.float32)],
        [
            pltpu.VMEM((parts, rows, width), jnp.float32),
            pltpu.VMEM((parts, rows, width), jnp.float32),
            pltpu.SemaphoreType.DMA((parts,)),
            pltpu.SemaphoreType.DMA((parts,)),
        ],
        LIMIT,
    )
    return updated


def line_of_four(inputs, gate_pre, grad_out, w_down, proj_in, proj_out, early):
    send = functools.partial(lax.ppermute, axis_name="tensor")
    pairs = [(0, 1), (1, 0), (2, 3), (3, 2)]
    inner = [(1, 2), (2, 1)]
    outward = [(1, 0), (2, 3)]
    inward = [(0, 1), (3, 2)]
    across = [(0, 2), (3, 1)]
    tokens = grad_out.shape[0]
    z = lax.axis_index("tensor")
    low = z < 2
    middle = jnp.logical_and(z > 0, z < 3)
    where = jnp.stack(
        [z, z + 1 - 2 * (z % 2), jnp.where(low, 2, 1), jnp.where(low, 3, 0), middle.astype(z.dtype)]
    ).astype(jnp.int32)

    halves = [slice(0, tokens // 2), slice(tokens // 2, tokens)]
    pair = send(grad_out, perm=pairs)
    own = [grad_out[half] for half in halves]
    mid_inner = [send(a, perm=inner) for a in own]
    in_part = input_block(where, inputs, proj_in.T)
    from_end = send(after(in_part, mid_inner[0]), perm=inward)
    acc, kept, begun = own_block(where, after(grad_out, in_part, *early), w_down)
    side = small_kernel(sum_body, "side", where, in_part, after(from_end, begun))
    end_inner = [send(after(a, side), perm=across) for a in own]
    mid_outer = [send(after(a, begun), perm=outward) for a in mid_inner]
    total = small_kernel(sum_body, "total", where, side, send(side, perm=inner))
    sent = send(total, perm=outward)

    acc, first = add_block(where, 1, [pair], w_down, after(acc, mid_outer[0]), begun, 2 * grad_out.size * w_down.shape[0])
    acc, second = add_block(where, 2, mid_inner + mid_outer, w_down, acc, first, 1000)

    size = 256
    arrived = [total, total]
    done = [first, first, second]
    rights = []
    for n in range(tokens // size):
        h, at = divmod(n * size, tokens // 2)
        chunk = end_inner[h][at : at + size]
        end_outer = send(after(chunk, arrived[n], done[n]), perm=outward)
        arrived.append(end_outer)
        kept, acc, right = last_block(
            where, end_inner[h], at, end_outer, n * size, kept, acc, gate_pre, proj_out.T, second
        )
        rights.append(right)
        done.append(right)
    return outer_products(where, total, sent, rights).reshape(-1, PROJ * PROJ)


def any_line(inputs, gate_pre, grad_out, w_down, proj_in, proj_out, early):
    in_part = jnp.dot(inputs, proj_in, preferred_element_type=jnp.float32)
    in_proj = lax.psum(in_part, "tensor").reshape(-1, LEN, PROJ)
    gathered = lax.all_gather(grad_out, "tensor", axis=1, tiled=True)
    up_grad = (dot_nt(gathered, w_down) * silu(gate_pre.astype(jnp.float32))).astype(jnp.bfloat16)
    out_part = jnp.dot(up_grad, proj_out, preferred_element_type=jnp.float32).reshape(-1, LEN, PROJ)
    grads = jnp.einsum("sti,stj->sij", in_proj, out_part, precision=HIGHEST)
    return grads.reshape(-1, PROJ * PROJ)


def swap(a, axis, bit):
    return lax.ppermute(a, axis, [(i, i ^ bit) for i in range(lax.axis_size(axis))])


def bits(axis):
    return [1 << b for b in range(lax.axis_size(axis).bit_length() - 1)]


def xor_sum(a, axis):
    for bit in bits(axis):
        a = a + swap(a, axis, bit)
    return a


def xor_gather(a, axis):
    for bit in bits(axis):
        a = jnp.concatenate([a, swap(a, axis, bit)], axis=0)
    return a


def on_device(inputs, gate_pre, grad_out, w_down, proj_in, proj_out, hessian, queries):
    count = lax.axis_size("dp")
    parts = [queries] + [swap(queries, "dp", s) for s in range(1, count)]
    line = line_of_four if lax.axis_size("tensor") == 4 else any_line
    grads = line(inputs, gate_pre, grad_out, w_down, proj_in, proj_out, parts)
    grads = xor_sum(grads, "tensor")

    me = lax.axis_index("dp")
    order = lax.axis_index("tensor") * count + jnp.stack([me ^ s for s in range(count)])
    scores = score_parts(order.astype(jnp.int32), grads, parts)
    *first, last = bits("tensor")
    for bit in first:
        scores = scores + swap(scores, "tensor", bit)
    other_scores = swap(scores, "tensor", last)

    all_grads = after(xor_gather(grads, "dp"), scores)
    row_count = hessian.shape[0]
    at = lax.axis_index(("tensor", "dp"))
    if row_count % 128:
        mine = lax.dynamic_slice_in_dim(all_grads, at * row_count, row_count, 1)
        updated = hessian + jnp.dot(mine.T, all_grads, precision=HIGHEST) / all_grads.shape[0]
    else:
        updated = update(at.reshape(1).astype(jnp.int32), all_grads, hessian)
    updated, other_scores = lax.optimization_barrier((updated, other_scores))
    return (updated, scores + other_scores)


def solution(mesh):
    return jax.shard_map(
        on_device,
        mesh=mesh,
        in_specs=(
            P(("groups", "dp"), "tensor"),
            P(("groups", "dp"), "tensor"),
            P(("groups", "dp"), "tensor"),
            P("tensor", None),
            P("tensor", None),
            P("tensor", None),
            P(("groups", "tensor", "dp"), None),
            P("groups", ("tensor", "dp")),
        ),
        out_specs=(P(("groups", "tensor", "dp"), None), P(("groups", "dp"), None)),
        check_vma=False,
    )
```

```python
import functools

import jax
import jax.numpy as jnp
from jax import lax
from jax.experimental import pallas as pl
from jax.experimental.pallas import tpu as pltpu
from jax.sharding import PartitionSpec as P

PROJ = 64
LEN = 512
HIGHEST = lax.Precision.HIGHEST
NT = (((1,), (1,)), ((), ()))
TILE = 512
LIMIT = 16
ANYWHERE = pl.BlockSpec(memory_space=pl.ANY)
INSIDE = pl.BlockSpec(memory_space=pltpu.VMEM)
OUTSIDE = pl.BlockSpec(memory_space=pltpu.HBM)


def silu(v):
    return 0.5 * v * (1.0 + jnp.tanh(0.5 * v))


def dot(a, b):
    return jnp.dot(a, b, preferred_element_type=jnp.float32)


def dot_nt(a, b):
    return lax.dot_general(a, b, NT, preferred_element_type=jnp.float32)


def placed(a, spec):
    if spec is INSIDE or spec is OUTSIDE:
        return pltpu.with_memory_space_constraint(a, spec.memory_space)
    return a


def call(body, name, where, grid, operands, in_specs, out_specs, out_shapes, scratch, mib, aliases=None, flops=1000):
    return pl.pallas_call(
        body,
        grid_spec=pltpu.PrefetchScalarGridSpec(
            num_scalar_prefetch=1, grid=grid, in_specs=in_specs, out_specs=out_specs, scratch_shapes=scratch
        ),
        out_shape=out_shapes,
        compiler_params=pltpu.CompilerParams(vmem_limit_bytes=mib * 2**20),
        cost_estimate=pl.CostEstimate(flops=flops, bytes_accessed=1000, transcendentals=0),
        name=name,
        input_output_aliases=aliases or {},
    )(where, *[placed(a, spec) for a, spec in zip(operands, in_specs)])


def after(a, *others):
    return lax.optimization_barrier((a, *others))[0]


def fixed(shape):
    return pl.BlockSpec(shape, lambda j, where: (0, 0), pipeline_mode=pl.Buffered(1))


def tile_rows(t, size=TILE):
    return pl.ds(pl.multiple_of(t * size, size), size)


def columns(where, i, width):
    return pl.ds(pl.multiple_of(where[i] * width, width), width)


def input_body(where, inputs, pi_t, in_t):
    in_t[...] = dot_nt(pi_t[...], inputs[...])


def input_block(where, inputs, pi_t):
    shape = (pi_t.shape[0], inputs.shape[0])
    (in_t,) = call(
        input_body,
        "input_block",
        where,
        (1,),
        (inputs, pi_t),
        [fixed(inputs.shape), fixed(pi_t.shape)],
        [pl.BlockSpec(shape, lambda j, where: (0, 0))],
        [jax.ShapeDtypeStruct(shape, jnp.float32)],
        [],
        LIMIT,
    )
    return in_t


def own_body(where, own, w, w_last, acc, kept, token):
    here = tile_rows(pl.program_id(0))
    token[...] = jnp.zeros_like(token)
    kept[:, here] = w_last[...].T
    acc[:, here] = dot_nt(own[...], w[...])


def own_block(where, own, w):
    tokens, feats = own.shape
    hidden = w.shape[0]
    return call(
        own_body,
        "own_block",
        where,
        (hidden // TILE,),
        (own, w, w),
        [
            fixed(own.shape),
            pl.BlockSpec((TILE, feats), lambda j, where: (j, where[0])),
            pl.BlockSpec((TILE, feats), lambda j, where: (j, where[3])),
        ],
        [INSIDE, INSIDE, pl.BlockSpec((8, 128), lambda j, where: (0, 0))],
        [
            pltpu.VMEM((tokens, hidden), jnp.float32),
            pltpu.VMEM((feats, hidden), w.dtype),
            jax.ShapeDtypeStruct((8, 128), jnp.float32),
        ],
        [],
        LIMIT,
    )


def select(where, inner, outer):
    return jnp.where(where[4] == 1, inner[...], outer[...])


def add_body(where, *refs):
    *blocks, w, old, _, acc, token, block = refs
    step = pl.program_id(0)

    @pl.when(step == 0)
    def _():
        token[...] = jnp.zeros_like(token)
        if len(blocks) == 1:
            block[...] = blocks[0][...]
        else:
            half = len(blocks) // 2
            size = blocks[0].shape[0]
            for h in range(half):
                block[h * size : (h + 1) * size, :] = select(where, blocks[h], blocks[half + h])

    here = tile_rows(step)
    acc[:, here] = old[:, here] + dot_nt(block[...], w[...])


def add_block(where, which, blocks, w, old, token, flops):
    tokens, feats = old.shape[0], blocks[0].shape[1]
    return call(
        add_body,
        f"add_block_{which}",
        where,
        (w.shape[0] // TILE,),
        (*blocks, w, old, token),
        [fixed(a.shape) for a in blocks]
        + [pl.BlockSpec((TILE, feats), lambda j, where: (j, where[which])), INSIDE, ANYWHERE],
        [INSIDE, pl.BlockSpec((8, 128), lambda j, where: (0, 0))],
        [pltpu.VMEM(old.shape, old.dtype), jax.ShapeDtypeStruct((8, 128), jnp.float32)],
        [pltpu.VMEM((tokens, feats), blocks[0].dtype)],
        LIMIT,
        aliases={len(blocks) + 2: 0},
        flops=flops,
    )


def last_body(
    start, inner_at, where, inner, outer, kept, old, gate, po_t, _, kept_same, old_same, right, gates, po, gate_sems, po_sem
):
    size = outer.shape[0]
    hidden = kept.shape[1]
    tokens = pl.ds(start, size)
    spans = [pl.ds(t * TILE, TILE) for t in range(hidden // TILE)]
    po_read = pltpu.make_async_copy(po_t, po, po_sem)
    reads = [
        pltpu.make_async_copy(gate.at[tokens, span], gates.at[t], gate_sems.at[t]) for t, span in enumerate(spans)
    ]
    reads[0].start()
    po_read.start()
    for read in reads[1:]:
        read.start()
    block = select(where, inner.at[pl.ds(inner_at, size)], outer)
    total = jnp.zeros((size, PROJ), jnp.float32)
    for t, span in enumerate(spans):
        hidden_grad = old[tokens, span] + dot(block, kept[:, span])
        reads[t].wait()
        up_grad = (hidden_grad * silu(gates[t].astype(jnp.float32))).astype(jnp.bfloat16)
        if t == 0:
            po_read.wait()
        total = total + dot_nt(up_grad, po[:, span])
    right[...] = total


def last_block(where, inner, inner_at, outer, start, kept, old, gate, po_t, token):
    size = outer.shape[0]
    tiles = kept.shape[1] // TILE
    return call(
        functools.partial(last_body, start, inner_at),
        "last_block",
        where,
        (1,),
        (inner, outer, kept, old, gate, po_t, token),
        [INSIDE, INSIDE, INSIDE, INSIDE, OUTSIDE, ANYWHERE, ANYWHERE],
        [INSIDE, INSIDE, pl.BlockSpec((size, PROJ), lambda j, where: (0, 0))],
        [
            pltpu.VMEM(kept.shape, kept.dtype),
            pltpu.VMEM(old.shape, old.dtype),
            jax.ShapeDtypeStruct((size, PROJ), jnp.float32),
        ],
        [
            pltpu.VMEM((tiles, size, TILE), gate.dtype),
            pltpu.VMEM(po_t.shape, po_t.dtype),
            pltpu.SemaphoreType.DMA((tiles,)),
            pltpu.SemaphoreType.DMA,
        ],
        LIMIT,
        aliases={3: 0, 4: 1},
    )


def outer_body(where, total, sent, *refs):
    *rights, grads = refs
    left_t = select(where, total, sent)
    start = 0
    terms = [None] * grads.shape[0]
    for right in rights:
        size = right.shape[0]
        s = start // LEN
        term = jnp.dot(
            left_t[:, start : start + size], right[...], precision=HIGHEST, preferred_element_type=jnp.float32
        )
        terms[s] = term if terms[s] is None else terms[s] + term
        start += size
    for s, term in enumerate(terms):
        grads[s] = term


def outer_products(where, total, sent, rights):
    shape = (total.shape[1] // LEN, PROJ, PROJ)
    (grads,) = call(
        outer_body,
        "outer_products",
        where,
        (1,),
        (total, sent, *rights),
        [fixed(a.shape) for a in (total, sent, *rights)],
        [pl.BlockSpec(shape, lambda j, where: (0, 0, 0))],
        [jax.ShapeDtypeStruct(shape, jnp.float32)],
        [],
        LIMIT,
    )
    return grads


def small_kernel(body, name, where, *operands):
    (out,) = call(
        body,
        name,
        where,
        (1,),
        operands,
        [fixed(a.shape) for a in operands],
        [pl.BlockSpec(operands[0].shape, lambda j, where: (0, 0))],
        [jax.ShapeDtypeStruct(operands[0].shape, operands[0].dtype)],
        [],
        LIMIT,
    )
    return out


def sum_body(where, a, b, out):
    out[...] = a[...] + b[...]


def score_body(order, grads, *rest):
    *parts, out = rest
    total = None
    for s, part in enumerate(parts):
        width = part.shape[1]
        term = lax.dot_general(
            grads[:, columns(order, s, width)],
            part[...],
            NT,
            precision=HIGHEST,
            preferred_element_type=jnp.float32,
        )
        total = term if total is None else total + term
    out[...] = total


def score_parts(order, grads, parts):
    width = parts[0].shape[1]
    shape = (grads.shape[0], parts[0].shape[0])
    if width % 128:
        slices = [lax.dynamic_slice_in_dim(grads, order[s] * width, width, 1) for s in range(len(parts))]
        return jnp.dot(jnp.concatenate(slices, axis=1), jnp.concatenate(parts, axis=1).T, precision=HIGHEST)
    (scores,) = call(
        score_body,
        "scores",
        order,
        (1,),
        (grads, *[pltpu.with_memory_space_constraint(a, pltpu.HBM) for a in parts]),
        [fixed(grads.shape)] + [fixed(a.shape) for a in parts],
        [pl.BlockSpec(shape, lambda j, order: (0, 0))],
        [jax.ShapeDtypeStruct(shape, jnp.float32)],
        [],
        LIMIT,
    )
    return scores


def pieces(a):
    high = a.astype(jnp.bfloat16)
    rest = a - high.astype(jnp.float32)
    middle = rest.astype(jnp.bfloat16)
    low = (rest - middle.astype(jnp.float32)).astype(jnp.bfloat16)
    return high, middle, low


def update_body(scale, row, grads, mine, hessian, out, old, new, in_sems, out_sems):
    count, columns = grads.shape
    width = old.shape[2]
    parts = columns // width
    reads = [
        pltpu.make_async_copy(hessian.at[:, pl.ds(t * width, width)], old.at[t], in_sems.at[t]) for t in range(parts)
    ]
    writes = [
        pltpu.make_async_copy(new.at[t], out.at[:, pl.ds(t * width, width)], out_sems.at[t]) for t in range(parts)
    ]
    for read in reads:
        read.start()
    high, middle, low = pieces(mine[...])
    left = jnp.concatenate([high, high, middle, middle, high, low], axis=0).T
    for t in range(parts):
        high, middle, low = pieces(grads[:, t * width : (t + 1) * width])
        right = jnp.concatenate([high, middle, high, middle, low, high], axis=0)
        total = dot(left, right) * scale
        reads[t].wait()
        new[t] = old[t] + total
        writes[t].start()
    for write in writes:
        write.wait()


def update(row, grads, hessian):
    rows, columns = hessian.shape
    count = grads.shape[0]
    parts = 4
    width = columns // parts
    (updated,) = call(
        functools.partial(update_body, 1.0 / count),
        "hessian_update",
        row,
        (1,),
        (grads, grads, hessian),
        [
            fixed(grads.shape),
            pl.BlockSpec((count, rows), lambda j, row: (0, row[0]), pipeline_mode=pl.Buffered(1)),
            OUTSIDE,
        ],
        [ANYWHERE],
        [jax.ShapeDtypeStruct((rows, columns), jnp.float32)],
        [
            pltpu.VMEM((parts, rows, width), jnp.float32),
            pltpu.VMEM((parts, rows, width), jnp.float32),
            pltpu.SemaphoreType.DMA((parts,)),
            pltpu.SemaphoreType.DMA((parts,)),
        ],
        LIMIT,
    )
    return updated


def line_of_four(inputs, gate_pre, grad_out, w_down, proj_in, proj_out, early):
    send = functools.partial(lax.ppermute, axis_name="tensor")
    pairs = [(0, 1), (1, 0), (2, 3), (3, 2)]
    inner = [(1, 2), (2, 1)]
    outward = [(1, 0), (2, 3)]
    inward = [(0, 1), (3, 2)]
    tokens = grad_out.shape[0]
    z = lax.axis_index("tensor")
    low = z < 2
    middle = jnp.logical_and(z > 0, z < 3)
    where = jnp.stack(
        [z, z + 1 - 2 * (z % 2), jnp.where(low, 2, 1), jnp.where(low, 3, 0), middle.astype(z.dtype)]
    ).astype(jnp.int32)

    halves = [slice(0, tokens // 2), slice(tokens // 2, tokens)]
    pair = send(grad_out, perm=pairs)
    own = [grad_out[half] for half in halves]
    mid_inner = [send(a, perm=inner) for a in own]
    in_part = input_block(where, inputs, proj_in.T)
    from_end = send(after(in_part, mid_inner[0]), perm=inward)
    acc, kept, begun = own_block(where, after(grad_out, in_part, *early), w_down)
    mid_outer = [send(after(a, begun), perm=outward) for a in mid_inner]
    end_inner = [send(pair[half], perm=inner) for half in halves]
    side = small_kernel(sum_body, "side", where, in_part, after(from_end, begun, pair))
    total = small_kernel(sum_body, "total", where, side, send(side, perm=inner))
    sent = send(total, perm=outward)

    acc, first = add_block(where, 1, [pair], w_down, after(acc, mid_outer[0]), begun, 2 * grad_out.size * w_down.shape[0])
    acc, second = add_block(where, 2, mid_inner + mid_outer, w_down, acc, first, 1000)

    size = 256
    arrived = [total, total]
    done = [first, first, second]
    rights = []
    for n in range(tokens // size):
        h, at = divmod(n * size, tokens // 2)
        chunk = end_inner[h][at : at + size]
        end_outer = send(after(chunk, arrived[n], done[n]), perm=outward)
        arrived.append(end_outer)
        kept, acc, right = last_block(
            where, end_inner[h], at, end_outer, n * size, kept, acc, gate_pre, proj_out.T, second
        )
        rights.append(right)
        done.append(right)
    return outer_products(where, total, sent, rights).reshape(-1, PROJ * PROJ)


def any_line(inputs, gate_pre, grad_out, w_down, proj_in, proj_out, early):
    in_part = jnp.dot(inputs, proj_in, preferred_element_type=jnp.float32)
    in_proj = lax.psum(in_part, "tensor").reshape(-1, LEN, PROJ)
    gathered = lax.all_gather(grad_out, "tensor", axis=1, tiled=True)
    up_grad = (dot_nt(gathered, w_down) * silu(gate_pre.astype(jnp.float32))).astype(jnp.bfloat16)
    out_part = jnp.dot(up_grad, proj_out, preferred_element_type=jnp.float32).reshape(-1, LEN, PROJ)
    grads = jnp.einsum("sti,stj->sij", in_proj, out_part, precision=HIGHEST)
    return grads.reshape(-1, PROJ * PROJ)


def swap(a, axis, bit):
    return lax.ppermute(a, axis, [(i, i ^ bit) for i in range(lax.axis_size(axis))])


def bits(axis):
    return [1 << b for b in range(lax.axis_size(axis).bit_length() - 1)]


def xor_sum(a, axis):
    for bit in bits(axis):
        a = a + swap(a, axis, bit)
    return a


def xor_gather(a, axis):
    for bit in bits(axis):
        a = jnp.concatenate([a, swap(a, axis, bit)], axis=0)
    return a


def on_device(inputs, gate_pre, grad_out, w_down, proj_in, proj_out, hessian, queries):
    count = lax.axis_size("dp")
    parts = [queries] + [swap(queries, "dp", s) for s in range(1, count)]
    line = line_of_four if lax.axis_size("tensor") == 4 else any_line
    grads = line(inputs, gate_pre, grad_out, w_down, proj_in, proj_out, parts)
    grads = xor_sum(grads, "tensor")

    me = lax.axis_index("dp")
    order = lax.axis_index("tensor") * count + jnp.stack([me ^ s for s in range(count)])
    scores = score_parts(order.astype(jnp.int32), grads, parts)
    *first, last = bits("tensor")
    for bit in first:
        scores = scores + swap(scores, "tensor", bit)
    other_scores = swap(scores, "tensor", last)

    all_grads = after(xor_gather(grads, "dp"), scores)
    row_count = hessian.shape[0]
    at = lax.axis_index(("tensor", "dp"))
    if row_count % 128:
        mine = lax.dynamic_slice_in_dim(all_grads, at * row_count, row_count, 1)
        updated = hessian + jnp.dot(mine.T, all_grads, precision=HIGHEST) / all_grads.shape[0]
    else:
        updated = update(at.reshape(1).astype(jnp.int32), all_grads, hessian)
    updated, other_scores = lax.optimization_barrier((updated, other_scores))
    return (updated, scores + other_scores)


def solution(mesh):
    return jax.shard_map(
        on_device,
        mesh=mesh,
        in_specs=(
            P(("groups", "dp"), "tensor"),
            P(("groups", "dp"), "tensor"),
            P(("groups", "dp"), "tensor"),
            P("tensor", None),
            P("tensor", None),
            P("tensor", None),
            P(("groups", "tensor", "dp"), None),
            P("groups", ("tensor", "dp")),
        ),
        out_specs=(P(("groups", "tensor", "dp"), None), P(("groups", "dp"), None)),
        check_vma=False,
    )
```

```python
import functools

import jax
import jax.numpy as jnp
from jax import lax
from jax.experimental import pallas as pl
from jax.experimental.pallas import tpu as pltpu
from jax.sharding import PartitionSpec as P

PROJ = 64
LEN = 512
HIGHEST = lax.Precision.HIGHEST
NT = (((1,), (1,)), ((), ()))
TILE = 512
LIMIT = 16
ANYWHERE = pl.BlockSpec(memory_space=pl.ANY)
INSIDE = pl.BlockSpec(memory_space=pltpu.VMEM)
OUTSIDE = pl.BlockSpec(memory_space=pltpu.HBM)


def silu(v):
    return 0.5 * v * (1.0 + jnp.tanh(0.5 * v))


def dot(a, b):
    return jnp.dot(a, b, preferred_element_type=jnp.float32)


def dot_nt(a, b):
    return lax.dot_general(a, b, NT, preferred_element_type=jnp.float32)


def placed(a, spec):
    if spec is INSIDE or spec is OUTSIDE:
        return pltpu.with_memory_space_constraint(a, spec.memory_space)
    return a


def call(body, name, where, grid, operands, in_specs, out_specs, out_shapes, scratch, mib, aliases=None, flops=1000):
    return pl.pallas_call(
        body,
        grid_spec=pltpu.PrefetchScalarGridSpec(
            num_scalar_prefetch=1, grid=grid, in_specs=in_specs, out_specs=out_specs, scratch_shapes=scratch
        ),
        out_shape=out_shapes,
        compiler_params=pltpu.CompilerParams(vmem_limit_bytes=mib * 2**20),
        cost_estimate=pl.CostEstimate(flops=flops, bytes_accessed=1000, transcendentals=0),
        name=name,
        input_output_aliases=aliases or {},
    )(where, *[placed(a, spec) for a, spec in zip(operands, in_specs)])


def after(a, *others):
    return lax.optimization_barrier((a, *others))[0]


def fixed(shape):
    return pl.BlockSpec(shape, lambda j, where: (0, 0), pipeline_mode=pl.Buffered(1))


def tile_rows(t, size=TILE):
    return pl.ds(pl.multiple_of(t * size, size), size)


def columns(where, i, width):
    return pl.ds(pl.multiple_of(where[i] * width, width), width)


def input_body(where, inputs, pi_t, in_t):
    in_t[...] = dot_nt(pi_t[...], inputs[...])


def input_block(where, inputs, pi_t):
    shape = (pi_t.shape[0], inputs.shape[0])
    (in_t,) = call(
        input_body,
        "input_block",
        where,
        (1,),
        (inputs, pi_t),
        [fixed(inputs.shape), fixed(pi_t.shape)],
        [pl.BlockSpec(shape, lambda j, where: (0, 0))],
        [jax.ShapeDtypeStruct(shape, jnp.float32)],
        [],
        LIMIT,
    )
    return in_t


def own_body(where, own, w, w_last, acc, kept, token):
    here = tile_rows(pl.program_id(0))
    token[...] = jnp.zeros_like(token)
    kept[:, here] = w_last[...].T
    acc[:, here] = dot_nt(own[...], w[...])


def own_block(where, own, w):
    tokens, feats = own.shape
    hidden = w.shape[0]
    return call(
        own_body,
        "own_block",
        where,
        (hidden // TILE,),
        (own, w, w),
        [
            fixed(own.shape),
            pl.BlockSpec((TILE, feats), lambda j, where: (j, where[0])),
            pl.BlockSpec((TILE, feats), lambda j, where: (j, where[3])),
        ],
        [INSIDE, INSIDE, pl.BlockSpec((8, 128), lambda j, where: (0, 0))],
        [
            pltpu.VMEM((tokens, hidden), jnp.float32),
            pltpu.VMEM((feats, hidden), w.dtype),
            jax.ShapeDtypeStruct((8, 128), jnp.float32),
        ],
        [],
        LIMIT,
    )


def select(where, inner, outer):
    return jnp.where(where[4] == 1, inner[...], outer[...])


def add_body(where, *refs):
    *blocks, w, old, _, acc, token, block = refs
    step = pl.program_id(0)

    @pl.when(step == 0)
    def _():
        token[...] = jnp.zeros_like(token)
        if len(blocks) == 1:
            block[...] = blocks[0][...]
        else:
            half = len(blocks) // 2
            size = blocks[0].shape[0]
            for h in range(half):
                block[h * size : (h + 1) * size, :] = select(where, blocks[h], blocks[half + h])

    here = tile_rows(step)
    acc[:, here] = old[:, here] + dot_nt(block[...], w[...])


def add_block(where, which, blocks, w, old, token, flops):
    tokens, feats = old.shape[0], blocks[0].shape[1]
    return call(
        add_body,
        f"add_block_{which}",
        where,
        (w.shape[0] // TILE,),
        (*blocks, w, old, token),
        [fixed(a.shape) for a in blocks]
        + [pl.BlockSpec((TILE, feats), lambda j, where: (j, where[which])), INSIDE, ANYWHERE],
        [INSIDE, pl.BlockSpec((8, 128), lambda j, where: (0, 0))],
        [pltpu.VMEM(old.shape, old.dtype), jax.ShapeDtypeStruct((8, 128), jnp.float32)],
        [pltpu.VMEM((tokens, feats), blocks[0].dtype)],
        LIMIT,
        aliases={len(blocks) + 2: 0},
        flops=flops,
    )


def last_body(
    start, inner_at, where, inner, outer, kept, old, gate, po_t, _, kept_same, old_same, right, gates, po, gate_sems, po_sem
):
    size = outer.shape[0]
    hidden = kept.shape[1]
    tokens = pl.ds(start, size)
    spans = [pl.ds(t * TILE, TILE) for t in range(hidden // TILE)]
    po_read = pltpu.make_async_copy(po_t, po, po_sem)
    reads = [
        pltpu.make_async_copy(gate.at[tokens, span], gates.at[t], gate_sems.at[t]) for t, span in enumerate(spans)
    ]
    reads[0].start()
    po_read.start()
    for read in reads[1:]:
        read.start()
    block = select(where, inner.at[pl.ds(inner_at, size)], outer)
    total = jnp.zeros((size, PROJ), jnp.float32)
    for t, span in enumerate(spans):
        hidden_grad = old[tokens, span] + dot(block, kept[:, span])
        reads[t].wait()
        up_grad = (hidden_grad * silu(gates[t].astype(jnp.float32))).astype(jnp.bfloat16)
        if t == 0:
            po_read.wait()
        total = total + dot_nt(up_grad, po[:, span])
    right[...] = total


def last_block(where, inner, inner_at, outer, start, kept, old, gate, po_t, token):
    size = outer.shape[0]
    tiles = kept.shape[1] // TILE
    return call(
        functools.partial(last_body, start, inner_at),
        "last_block",
        where,
        (1,),
        (inner, outer, kept, old, gate, po_t, token),
        [INSIDE, INSIDE, INSIDE, INSIDE, OUTSIDE, ANYWHERE, ANYWHERE],
        [INSIDE, INSIDE, pl.BlockSpec((size, PROJ), lambda j, where: (0, 0))],
        [
            pltpu.VMEM(kept.shape, kept.dtype),
            pltpu.VMEM(old.shape, old.dtype),
            jax.ShapeDtypeStruct((size, PROJ), jnp.float32),
        ],
        [
            pltpu.VMEM((tiles, size, TILE), gate.dtype),
            pltpu.VMEM(po_t.shape, po_t.dtype),
            pltpu.SemaphoreType.DMA((tiles,)),
            pltpu.SemaphoreType.DMA,
        ],
        LIMIT,
        aliases={3: 0, 4: 1},
    )


def outer_body(where, total, sent, *refs):
    *rights, grads = refs
    left_t = jnp.where(where[4] == 1, total[...], sent[...].astype(jnp.float32))
    start = 0
    terms = [None] * grads.shape[0]
    for right in rights:
        size = right.shape[0]
        s = start // LEN
        term = jnp.dot(
            left_t[:, start : start + size], right[...], precision=HIGHEST, preferred_element_type=jnp.float32
        )
        terms[s] = term if terms[s] is None else terms[s] + term
        start += size
    for s, term in enumerate(terms):
        grads[s] = term


def outer_products(where, total, sent, rights):
    shape = (total.shape[1] // LEN, PROJ, PROJ)
    (grads,) = call(
        outer_body,
        "outer_products",
        where,
        (1,),
        (total, sent, *rights),
        [fixed(a.shape) for a in (total, sent, *rights)],
        [pl.BlockSpec(shape, lambda j, where: (0, 0, 0))],
        [jax.ShapeDtypeStruct(shape, jnp.float32)],
        [],
        LIMIT,
    )
    return grads


def small_kernel(body, name, where, *operands):
    (out,) = call(
        body,
        name,
        where,
        (1,),
        operands,
        [fixed(a.shape) for a in operands],
        [pl.BlockSpec(operands[0].shape, lambda j, where: (0, 0))],
        [jax.ShapeDtypeStruct(operands[0].shape, operands[0].dtype)],
        [],
        LIMIT,
    )
    return out


def sum_body(where, a, b, out):
    out[...] = a[...] + b[...]


def score_body(order, grads, *rest):
    *parts, out = rest
    rows, width = parts[0].shape
    count = grads.shape[0]
    lane = lax.broadcasted_iota(jnp.int32, (rows, 128), 1)
    total = jnp.zeros((rows, 128), jnp.float32)
    for s in range(count):
        products = None
        for p, part in enumerate(parts):
            term = part[...] * grads[s : s + 1, columns(order, p, width)]
            products = term if products is None else products + term
        total = jnp.where(lane == s, jnp.sum(products, axis=1, keepdims=True), total)
    out[...] = total.T[:count, :]


def score_parts(order, grads, parts):
    width = parts[0].shape[1]
    shape = (grads.shape[0], parts[0].shape[0])
    if width % 128:
        slices = [lax.dynamic_slice_in_dim(grads, order[s] * width, width, 1) for s in range(len(parts))]
        return jnp.dot(jnp.concatenate(slices, axis=1), jnp.concatenate(parts, axis=1).T, precision=HIGHEST)
    (scores,) = call(
        score_body,
        "scores",
        order,
        (1,),
        (grads, *[pltpu.with_memory_space_constraint(a, pltpu.HBM) for a in parts]),
        [fixed(grads.shape)] + [fixed(a.shape) for a in parts],
        [pl.BlockSpec(shape, lambda j, order: (0, 0))],
        [jax.ShapeDtypeStruct(shape, jnp.float32)],
        [],
        LIMIT,
    )
    return scores


def pieces(a):
    high = a.astype(jnp.bfloat16)
    rest = a - high.astype(jnp.float32)
    middle = rest.astype(jnp.bfloat16)
    low = (rest - middle.astype(jnp.float32)).astype(jnp.bfloat16)
    return high, middle, low


def update_body(scale, row, grads, mine, hessian, out, old, new, in_sems, out_sems):
    count, columns = grads.shape
    width = old.shape[2]
    parts = columns // width
    reads = [
        pltpu.make_async_copy(hessian.at[:, pl.ds(t * width, width)], old.at[t], in_sems.at[t]) for t in range(parts)
    ]
    writes = [
        pltpu.make_async_copy(new.at[t], out.at[:, pl.ds(t * width, width)], out_sems.at[t]) for t in range(parts)
    ]
    for read in reads:
        read.start()
    high, middle, low = pieces(mine[...])
    left = jnp.concatenate([high, high, middle, middle, high, low], axis=0).T
    for t in range(parts):
        high, middle, low = pieces(grads[:, t * width : (t + 1) * width])
        right = jnp.concatenate([high, middle, high, middle, low, high], axis=0)
        total = dot(left, right) * scale
        reads[t].wait()
        new[t] = old[t] + total
        writes[t].start()
    for write in writes:
        write.wait()


def update(row, grads, hessian):
    rows, columns = hessian.shape
    count = grads.shape[0]
    parts = 8
    width = columns // parts
    (updated,) = call(
        functools.partial(update_body, 1.0 / count),
        "hessian_update",
        row,
        (1,),
        (grads, grads, hessian),
        [
            fixed(grads.shape),
            pl.BlockSpec((count, rows), lambda j, row: (0, row[0]), pipeline_mode=pl.Buffered(1)),
            OUTSIDE,
        ],
        [ANYWHERE],
        [jax.ShapeDtypeStruct((rows, columns), jnp.float32)],
        [
            pltpu.VMEM((parts, rows, width), jnp.float32),
            pltpu.VMEM((parts, rows, width), jnp.float32),
            pltpu.SemaphoreType.DMA((parts,)),
            pltpu.SemaphoreType.DMA((parts,)),
        ],
        LIMIT,
    )
    return updated


def line_of_four(inputs, gate_pre, grad_out, w_down, proj_in, proj_out, early):
    send = functools.partial(lax.ppermute, axis_name="tensor")
    pairs = [(0, 1), (1, 0), (2, 3), (3, 2)]
    inner = [(1, 2), (2, 1)]
    outward = [(1, 0), (2, 3)]
    inward = [(0, 1), (3, 2)]
    tokens = grad_out.shape[0]
    z = lax.axis_index("tensor")
    low = z < 2
    middle = jnp.logical_and(z > 0, z < 3)
    where = jnp.stack(
        [z, z + 1 - 2 * (z % 2), jnp.where(low, 2, 1), jnp.where(low, 3, 0), middle.astype(z.dtype)]
    ).astype(jnp.int32)

    halves = [slice(0, tokens // 2), slice(tokens // 2, tokens)]
    pair = send(grad_out, perm=pairs)
    own = [grad_out[half] for half in halves]
    mid_inner = [send(a, perm=inner) for a in own]
    in_part = input_block(where, inputs, proj_in.T)
    from_end = send(after(in_part, mid_inner[0]), perm=inward)
    acc, kept, begun = own_block(where, after(grad_out, in_part, *early), w_down)
    mid_outer = [send(after(a, begun), perm=outward) for a in mid_inner]
    end_inner = [send(pair[half], perm=inner) for half in halves]
    side = small_kernel(sum_body, "side", where, in_part, after(from_end, begun, pair))
    total = small_kernel(sum_body, "total", where, side, send(side, perm=inner))
    sent = send(total.astype(jnp.bfloat16), perm=outward)

    acc, first = add_block(where, 1, [pair], w_down, after(acc, mid_outer[0]), begun, 2 * grad_out.size * w_down.shape[0])
    acc, second = add_block(where, 2, mid_inner + mid_outer, w_down, acc, first, 1000)

    sizes = [256] * (tokens // 256 - 1) + [128, 128]
    arrived, done = [total, total, total], [first, first, second]
    rights = []
    start = 0
    for n, size in enumerate(sizes):
        h, at = divmod(start, tokens // 2)
        ahead = arrived[n + 1] if n < 4 else arrived[n]
        end_outer = send(after(end_inner[h][at : at + size], ahead, done[n]), perm=outward)
        arrived.append(end_outer)
        kept, acc, right = last_block(
            where, end_inner[h], at, end_outer, start, kept, acc, gate_pre, proj_out.T, second
        )
        rights.append(right)
        done.append(right)
        start += size
    return outer_products(where, total, sent, rights).reshape(-1, PROJ * PROJ)


def any_line(inputs, gate_pre, grad_out, w_down, proj_in, proj_out, early):
    in_part = jnp.dot(inputs, proj_in, preferred_element_type=jnp.float32)
    in_proj = lax.psum(in_part, "tensor").reshape(-1, LEN, PROJ)
    gathered = lax.all_gather(grad_out, "tensor", axis=1, tiled=True)
    up_grad = (dot_nt(gathered, w_down) * silu(gate_pre.astype(jnp.float32))).astype(jnp.bfloat16)
    out_part = jnp.dot(up_grad, proj_out, preferred_element_type=jnp.float32).reshape(-1, LEN, PROJ)
    grads = jnp.einsum("sti,stj->sij", in_proj, out_part, precision=HIGHEST)
    return grads.reshape(-1, PROJ * PROJ)


def swap(a, axis, bit):
    return lax.ppermute(a, axis, [(i, i ^ bit) for i in range(lax.axis_size(axis))])


def bits(axis):
    return [1 << b for b in range(lax.axis_size(axis).bit_length() - 1)]


def xor_sum(a, axis):
    for bit in bits(axis):
        a = a + swap(a, axis, bit)
    return a


def xor_order_sum(terms):
    while len(terms) > 1:
        terms = [terms[i] + terms[i + 1] for i in range(0, len(terms), 2)]
    return terms[0]


def xor_gather(a, axis):
    for bit in bits(axis):
        a = jnp.concatenate([a, swap(a, axis, bit)], axis=0)
    return a


def on_device(inputs, gate_pre, grad_out, w_down, proj_in, proj_out, hessian, queries):
    count = lax.axis_size("dp")
    parts = [queries] + [swap(queries, "dp", s) for s in range(1, count)]
    line = line_of_four if lax.axis_size("tensor") == 4 else any_line
    grads = line(inputs, gate_pre, grad_out, w_down, proj_in, proj_out, parts)
    grads = xor_sum(grads, "tensor")

    me = lax.axis_index("dp")
    order = lax.axis_index("tensor") * count + jnp.stack([me ^ s for s in range(count)])
    scores = score_parts(order.astype(jnp.int32), grads, parts)
    others = [swap(scores, "tensor", bit) for bit in range(1, lax.axis_size("tensor"))]
    all_grads = after(xor_gather(grads, "dp"), scores)
    row_count = hessian.shape[0]
    at = lax.axis_index(("tensor", "dp"))
    if row_count % 128:
        mine = lax.dynamic_slice_in_dim(all_grads, at * row_count, row_count, 1)
        updated = hessian + jnp.dot(mine.T, all_grads, precision=HIGHEST) / all_grads.shape[0]
    else:
        updated = update(at.reshape(1).astype(jnp.int32), all_grads, hessian)
    updated, *others = lax.optimization_barrier((updated, *others))
    return (updated, xor_order_sum([scores, *others]))


def solution(mesh):
    return jax.shard_map(
        on_device,
        mesh=mesh,
        in_specs=(
            P(("groups", "dp"), "tensor"),
            P(("groups", "dp"), "tensor"),
            P(("groups", "dp"), "tensor"),
            P("tensor", None),
            P("tensor", None),
            P("tensor", None),
            P(("groups", "tensor", "dp"), None),
            P("groups", ("tensor", "dp")),
        ),
        out_specs=(P(("groups", "tensor", "dp"), None), P(("groups", "dp"), None)),
        check_vma=False,
    )
```

```python
import functools

import jax
import jax.numpy as jnp
from jax import lax
from jax.experimental import pallas as pl
from jax.experimental.pallas import tpu as pltpu
from jax.sharding import PartitionSpec as P

PROJ = 64
LEN = 512
HIGHEST = lax.Precision.HIGHEST
NT = (((1,), (1,)), ((), ()))
TILE = 512
LIMIT = 16
ANYWHERE = pl.BlockSpec(memory_space=pl.ANY)
INSIDE = pl.BlockSpec(memory_space=pltpu.VMEM)
OUTSIDE = pl.BlockSpec(memory_space=pltpu.HBM)


def silu(v):
    return 0.5 * v * (1.0 + jnp.tanh(0.5 * v))


def dot(a, b):
    return jnp.dot(a, b, preferred_element_type=jnp.float32)


def dot_nt(a, b):
    return lax.dot_general(a, b, NT, preferred_element_type=jnp.float32)


def placed(a, spec):
    if spec is INSIDE or spec is OUTSIDE:
        return pltpu.with_memory_space_constraint(a, spec.memory_space)
    return a


def call(body, name, where, grid, operands, in_specs, out_specs, out_shapes, scratch, mib, aliases=None, flops=1000):
    return pl.pallas_call(
        body,
        grid_spec=pltpu.PrefetchScalarGridSpec(
            num_scalar_prefetch=1, grid=grid, in_specs=in_specs, out_specs=out_specs, scratch_shapes=scratch
        ),
        out_shape=out_shapes,
        compiler_params=pltpu.CompilerParams(vmem_limit_bytes=mib * 2**20),
        cost_estimate=pl.CostEstimate(flops=flops, bytes_accessed=1000, transcendentals=0),
        name=name,
        input_output_aliases=aliases or {},
    )(where, *[placed(a, spec) for a, spec in zip(operands, in_specs)])


def after(a, *others):
    return lax.optimization_barrier((a, *others))[0]


def fixed(shape):
    return pl.BlockSpec(shape, lambda j, where: (0, 0), pipeline_mode=pl.Buffered(1))


def tile_rows(t, size=TILE):
    return pl.ds(pl.multiple_of(t * size, size), size)


def columns(where, i, width):
    return pl.ds(pl.multiple_of(where[i] * width, width), width)


def input_body(where, inputs, pi_t, in_t):
    in_t[...] = dot_nt(pi_t[...], inputs[...])


def input_block(where, inputs, pi_t):
    shape = (pi_t.shape[0], inputs.shape[0])
    (in_t,) = call(
        input_body,
        "input_block",
        where,
        (1,),
        (inputs, pi_t),
        [fixed(inputs.shape), fixed(pi_t.shape)],
        [pl.BlockSpec(shape, lambda j, where: (0, 0))],
        [jax.ShapeDtypeStruct(shape, jnp.float32)],
        [],
        LIMIT,
    )
    return in_t


def own_body(where, own, w, w_last, acc, kept, token):
    here = tile_rows(pl.program_id(0))
    token[...] = jnp.zeros_like(token)
    kept[:, here] = w_last[...].T
    acc[:, here] = dot_nt(own[...], w[...])


def own_block(where, own, w):
    tokens, feats = own.shape
    hidden = w.shape[0]
    return call(
        own_body,
        "own_block",
        where,
        (hidden // TILE,),
        (own, w, w),
        [
            fixed(own.shape),
            pl.BlockSpec((TILE, feats), lambda j, where: (j, where[0])),
            pl.BlockSpec((TILE, feats), lambda j, where: (j, where[3])),
        ],
        [INSIDE, INSIDE, pl.BlockSpec((8, 128), lambda j, where: (0, 0))],
        [
            pltpu.VMEM((tokens, hidden), jnp.float32),
            pltpu.VMEM((feats, hidden), w.dtype),
            jax.ShapeDtypeStruct((8, 128), jnp.float32),
        ],
        [],
        LIMIT,
    )


def select(where, inner, outer):
    return jnp.where(where[4] == 1, inner[...], outer[...])


def add_body(where, *refs):
    *blocks, w, old, _, acc, token, block = refs
    step = pl.program_id(0)

    @pl.when(step == 0)
    def _():
        token[...] = jnp.zeros_like(token)
        if len(blocks) == 1:
            block[...] = blocks[0][...]
        else:
            half = len(blocks) // 2
            size = blocks[0].shape[0]
            for h in range(half):
                block[h * size : (h + 1) * size, :] = select(where, blocks[h], blocks[half + h])

    here = tile_rows(step)
    acc[:, here] = old[:, here] + dot_nt(block[...], w[...])


def add_block(where, which, blocks, w, old, token, flops):
    tokens, feats = old.shape[0], blocks[0].shape[1]
    return call(
        add_body,
        f"add_block_{which}",
        where,
        (w.shape[0] // TILE,),
        (*blocks, w, old, token),
        [fixed(a.shape) for a in blocks]
        + [pl.BlockSpec((TILE, feats), lambda j, where: (j, where[which])), INSIDE, ANYWHERE],
        [INSIDE, pl.BlockSpec((8, 128), lambda j, where: (0, 0))],
        [pltpu.VMEM(old.shape, old.dtype), jax.ShapeDtypeStruct((8, 128), jnp.float32)],
        [pltpu.VMEM((tokens, feats), blocks[0].dtype)],
        LIMIT,
        aliases={len(blocks) + 2: 0},
        flops=flops,
    )


def last_body(start, inner_at, bring, where, inner, outer, kept, old, gate, po_t, _, *rest):
    far, rest = rest[:bring], rest[bring:]
    _, _, right, *near = rest[: 3 + bring]
    gates, po, gate_sems, po_sem, near_sems = rest[3 + bring :]
    size = outer.shape[0]
    hidden = kept.shape[1]
    tokens = pl.ds(start, size)
    spans = [pl.ds(t * TILE, TILE) for t in range(hidden // TILE)]
    po_read = pltpu.make_async_copy(po_t, po, po_sem)
    reads = [
        pltpu.make_async_copy(gate.at[tokens, span], gates.at[t], gate_sems.at[t]) for t, span in enumerate(spans)
    ]
    reads[0].start()
    po_read.start()
    for read in reads[1:]:
        read.start()
    brought = [pltpu.make_async_copy(a, b, near_sems.at[i]) for i, (a, b) in enumerate(zip(far, near))]
    for copy in brought:
        copy.start()
    block = select(where, inner.at[pl.ds(inner_at, size)], outer)
    total = jnp.zeros((size, PROJ), jnp.float32)
    for t, span in enumerate(spans):
        hidden_grad = old[tokens, span] + dot(block, kept[:, span])
        reads[t].wait()
        up_grad = (hidden_grad * silu(gates[t].astype(jnp.float32))).astype(jnp.bfloat16)
        if t == 0:
            po_read.wait()
        total = total + dot_nt(up_grad, po[:, span])
    right[...] = total
    for copy in brought:
        copy.wait()


def last_block(where, inner, inner_at, outer, start, kept, old, gate, po_t, token, bring):
    size = outer.shape[0]
    tiles = kept.shape[1] // TILE
    return call(
        functools.partial(last_body, start, inner_at, len(bring)),
        "last_block",
        where,
        (1,),
        (inner, outer, kept, old, gate, po_t, token, *bring),
        [INSIDE, INSIDE, INSIDE, INSIDE, OUTSIDE, ANYWHERE, ANYWHERE] + [OUTSIDE] * len(bring),
        [INSIDE, INSIDE, pl.BlockSpec((size, PROJ), lambda j, where: (0, 0))] + [INSIDE] * len(bring),
        [
            pltpu.VMEM(kept.shape, kept.dtype),
            pltpu.VMEM(old.shape, old.dtype),
            jax.ShapeDtypeStruct((size, PROJ), jnp.float32),
            *[pltpu.VMEM(a.shape, a.dtype) for a in bring],
        ],
        [
            pltpu.VMEM((tiles, size, TILE), gate.dtype),
            pltpu.VMEM(po_t.shape, po_t.dtype),
            pltpu.SemaphoreType.DMA((tiles,)),
            pltpu.SemaphoreType.DMA,
            pltpu.SemaphoreType.DMA((max(len(bring), 1),)),
        ],
        LIMIT,
        aliases={3: 0, 4: 1},
    )


def outer_body(where, total, sent, *refs):
    *rights, grads = refs
    left_t = jnp.where(where[4] == 1, total[...], sent[...].astype(jnp.float32))
    start = 0
    terms = [None] * grads.shape[0]
    for right in rights:
        size = right.shape[0]
        s = start // LEN
        term = jnp.dot(
            left_t[:, start : start + size], right[...], precision=HIGHEST, preferred_element_type=jnp.float32
        )
        terms[s] = term if terms[s] is None else terms[s] + term
        start += size
    for s, term in enumerate(terms):
        grads[s] = term


def outer_products(where, total, sent, rights):
    shape = (total.shape[1] // LEN, PROJ, PROJ)
    (grads,) = call(
        outer_body,
        "outer_products",
        where,
        (1,),
        (total, sent, *rights),
        [fixed(a.shape) for a in (total, sent, *rights)],
        [pl.BlockSpec(shape, lambda j, where: (0, 0, 0))],
        [jax.ShapeDtypeStruct(shape, jnp.float32)],
        [],
        LIMIT,
    )
    return grads


def small_kernel(body, name, where, *operands):
    (out,) = call(
        body,
        name,
        where,
        (1,),
        operands,
        [fixed(a.shape) for a in operands],
        [pl.BlockSpec(operands[0].shape, lambda j, where: (0, 0))],
        [jax.ShapeDtypeStruct(operands[0].shape, operands[0].dtype)],
        [],
        LIMIT,
    )
    return out


def sum_body(where, a, b, out):
    out[...] = a[...] + b[...]


def score_body(order, grads, *rest):
    *parts, out = rest
    rows, width = parts[0].shape
    count = grads.shape[0]
    lane = lax.broadcasted_iota(jnp.int32, (rows, 128), 1)
    total = jnp.zeros((rows, 128), jnp.float32)
    for s in range(count):
        products = None
        for p, part in enumerate(parts):
            term = part[...] * grads[s : s + 1, columns(order, p, width)]
            products = term if products is None else products + term
        total = jnp.where(lane == s, jnp.sum(products, axis=1, keepdims=True), total)
    out[...] = total.T[:count, :]


def score_parts(order, grads, parts):
    width = parts[0].shape[1]
    shape = (grads.shape[0], parts[0].shape[0])
    if width % 128:
        slices = [lax.dynamic_slice_in_dim(grads, order[s] * width, width, 1) for s in range(len(parts))]
        return jnp.dot(jnp.concatenate(slices, axis=1), jnp.concatenate(parts, axis=1).T, precision=HIGHEST)
    (scores,) = call(
        score_body,
        "scores",
        order,
        (1,),
        (grads, *parts),
        [fixed(grads.shape)] + [INSIDE] * len(parts),
        [pl.BlockSpec(shape, lambda j, order: (0, 0))],
        [jax.ShapeDtypeStruct(shape, jnp.float32)],
        [],
        LIMIT,
    )
    return scores


def pieces(a):
    high = a.astype(jnp.bfloat16)
    rest = a - high.astype(jnp.float32)
    middle = rest.astype(jnp.bfloat16)
    low = (rest - middle.astype(jnp.float32)).astype(jnp.bfloat16)
    return high, middle, low


def update_body(scale, row, grads, mine, hessian, out, new, out_sems):
    columns = grads.shape[1]
    parts, _, width = new.shape
    high, middle, low = pieces(mine[...])
    left = jnp.concatenate([high, high, middle, middle, high, low], axis=0).T
    writes = []
    for t in range(parts):
        span = pl.ds(t * width, width)
        high, middle, low = pieces(grads[:, span])
        right = jnp.concatenate([high, middle, high, middle, low, high], axis=0)
        new[t] = hessian[:, span] + dot(left, right) * scale
        writes.append(pltpu.make_async_copy(new.at[t], out.at[:, span], out_sems.at[t]))
        writes[t].start()
    for write in writes:
        write.wait()


def update(row, grads, hessian):
    rows, columns = hessian.shape
    count = grads.shape[0]
    parts = 8
    width = columns // parts
    (updated,) = call(
        functools.partial(update_body, 1.0 / count),
        "hessian_update",
        row,
        (1,),
        (grads, grads, hessian),
        [
            fixed(grads.shape),
            pl.BlockSpec((count, rows), lambda j, row: (0, row[0]), pipeline_mode=pl.Buffered(1)),
            INSIDE,
        ],
        [ANYWHERE],
        [jax.ShapeDtypeStruct((rows, columns), jnp.float32)],
        [pltpu.VMEM((parts, rows, width), jnp.float32), pltpu.SemaphoreType.DMA((parts,))],
        LIMIT,
    )
    return updated


def line_of_four(inputs, gate_pre, grad_out, w_down, proj_in, proj_out, early, late):
    send = functools.partial(lax.ppermute, axis_name="tensor")
    pairs = [(0, 1), (1, 0), (2, 3), (3, 2)]
    inner = [(1, 2), (2, 1)]
    outward = [(1, 0), (2, 3)]
    inward = [(0, 1), (3, 2)]
    tokens = grad_out.shape[0]
    z = lax.axis_index("tensor")
    low = z < 2
    middle = jnp.logical_and(z > 0, z < 3)
    where = jnp.stack(
        [z, z + 1 - 2 * (z % 2), jnp.where(low, 2, 1), jnp.where(low, 3, 0), middle.astype(z.dtype)]
    ).astype(jnp.int32)

    halves = [slice(0, tokens // 2), slice(tokens // 2, tokens)]
    pair = send(grad_out, perm=pairs)
    own = [grad_out[half] for half in halves]
    mid_inner = [send(a, perm=inner) for a in own]
    in_part = input_block(where, inputs, proj_in.T)
    from_end = send(after(in_part, mid_inner[0]), perm=inward)
    acc, kept, begun = own_block(where, after(grad_out, in_part, *early), w_down)
    mid_outer = [send(after(a, begun), perm=outward) for a in mid_inner]
    end_inner = [send(pair[half], perm=inner) for half in halves]
    side = small_kernel(sum_body, "side", where, in_part, after(from_end, begun, pair))
    total = small_kernel(sum_body, "total", where, side, send(side, perm=inner))
    sent = send(total.astype(jnp.bfloat16), perm=outward)

    acc, first = add_block(where, 1, [pair], w_down, after(acc, mid_outer[0]), begun, 2 * grad_out.size * w_down.shape[0])
    acc, second = add_block(where, 2, mid_inner + mid_outer, w_down, acc, first, 1000)

    sizes = [256] * (tokens // 256 - 1) + [128, 128]
    arrived, done = [total, total, total], [first, first, second]
    rights = []
    start = 0
    for n, size in enumerate(sizes):
        h, at = divmod(start, tokens // 2)
        ahead = arrived[n + 1] if n < 4 else arrived[n]
        end_outer = send(after(end_inner[h][at : at + size], ahead, done[n]), perm=outward)
        arrived.append(end_outer)
        bring = [*early, late] if n == len(sizes) - 2 else []
        kept, acc, right, *brought = last_block(
            where, end_inner[h], at, end_outer, start, kept, acc, gate_pre, proj_out.T, second, bring
        )
        if bring:
            *early, late = brought
        rights.append(right)
        done.append(right)
        start += size
    return outer_products(where, total, sent, rights).reshape(-1, PROJ * PROJ), early, late


def any_line(inputs, gate_pre, grad_out, w_down, proj_in, proj_out, early, late):
    in_part = jnp.dot(inputs, proj_in, preferred_element_type=jnp.float32)
    in_proj = lax.psum(in_part, "tensor").reshape(-1, LEN, PROJ)
    gathered = lax.all_gather(grad_out, "tensor", axis=1, tiled=True)
    up_grad = (dot_nt(gathered, w_down) * silu(gate_pre.astype(jnp.float32))).astype(jnp.bfloat16)
    out_part = jnp.dot(up_grad, proj_out, preferred_element_type=jnp.float32).reshape(-1, LEN, PROJ)
    grads = jnp.einsum("sti,stj->sij", in_proj, out_part, precision=HIGHEST)
    return grads.reshape(-1, PROJ * PROJ), early, late


def swap(a, axis, bit):
    return lax.ppermute(a, axis, [(i, i ^ bit) for i in range(lax.axis_size(axis))])


def bits(axis):
    return [1 << b for b in range(lax.axis_size(axis).bit_length() - 1)]


def xor_sum(a, axis):
    for bit in bits(axis):
        a = a + swap(a, axis, bit)
    return a


def on_device(inputs, gate_pre, grad_out, w_down, proj_in, proj_out, hessian, queries):
    count = lax.axis_size("dp")
    parts = [queries] + [swap(queries, "dp", s) for s in range(1, count)]
    line = line_of_four if lax.axis_size("tensor") == 4 else any_line
    grads, parts, hessian = line(inputs, gate_pre, grad_out, w_down, proj_in, proj_out, parts, hessian)
    grads = xor_sum(grads, "tensor")

    me = lax.axis_index("dp")
    order = lax.axis_index("tensor") * count + jnp.stack([me ^ s for s in range(count)])
    scores = score_parts(order.astype(jnp.int32), grads, parts)
    all_grads = after(grads, scores)
    *first, last = bits("tensor")
    for n, bit in enumerate(bits("dp")):
        all_grads = jnp.concatenate([all_grads, swap(all_grads, "dp", bit)], axis=0)
        if n == 0:
            for score_bit in first:
                scores = scores + swap(scores, "tensor", score_bit)
            all_grads = after(all_grads, scores)
    others = swap(scores, "tensor", last)
    row_count = hessian.shape[0]
    at = lax.axis_index(("tensor", "dp"))
    if row_count % 128:
        mine = lax.dynamic_slice_in_dim(all_grads, at * row_count, row_count, 1)
        updated = hessian + jnp.dot(mine.T, all_grads, precision=HIGHEST) / all_grads.shape[0]
    else:
        updated = update(at.reshape(1).astype(jnp.int32), all_grads, hessian)
    updated, others = lax.optimization_barrier((updated, others))
    return (updated, scores + others)


def solution(mesh):
    return jax.shard_map(
        on_device,
        mesh=mesh,
        in_specs=(
            P(("groups", "dp"), "tensor"),
            P(("groups", "dp"), "tensor"),
            P(("groups", "dp"), "tensor"),
            P("tensor", None),
            P("tensor", None),
            P("tensor", None),
            P(("groups", "tensor", "dp"), None),
            P("groups", ("tensor", "dp")),
        ),
        out_specs=(P(("groups", "tensor", "dp"), None), P(("groups", "dp"), None)),
        check_vma=False,
    )
```

```python
import functools

import jax
import jax.numpy as jnp
from jax import lax
from jax.experimental import pallas as pl
from jax.experimental.pallas import tpu as pltpu
from jax.sharding import PartitionSpec as P

PROJ = 64
LEN = 512
HIGHEST = lax.Precision.HIGHEST
NT = (((1,), (1,)), ((), ()))
TILE = 512
LIMIT = 16
FIRST_PART = 5
ANYWHERE = pl.BlockSpec(memory_space=pl.ANY)
INSIDE = pl.BlockSpec(memory_space=pltpu.VMEM)
OUTSIDE = pl.BlockSpec(memory_space=pltpu.HBM)


def silu(v):
    return 0.5 * v * (1.0 + jnp.tanh(0.5 * v))


def dot(a, b):
    return jnp.dot(a, b, preferred_element_type=jnp.float32)


def dot_nt(a, b):
    return lax.dot_general(a, b, NT, preferred_element_type=jnp.float32)


def placed(a, spec):
    if spec is INSIDE or spec is OUTSIDE:
        return pltpu.with_memory_space_constraint(a, spec.memory_space)
    return a


def call(body, name, where, grid, operands, in_specs, out_specs, out_shapes, scratch, mib, aliases=None, flops=1000):
    return pl.pallas_call(
        body,
        grid_spec=pltpu.PrefetchScalarGridSpec(
            num_scalar_prefetch=1, grid=grid, in_specs=in_specs, out_specs=out_specs, scratch_shapes=scratch
        ),
        out_shape=out_shapes,
        compiler_params=pltpu.CompilerParams(vmem_limit_bytes=mib * 2**20),
        cost_estimate=pl.CostEstimate(flops=flops, bytes_accessed=1000, transcendentals=0),
        name=name,
        input_output_aliases=aliases or {},
    )(where, *[placed(a, spec) for a, spec in zip(operands, in_specs)])


def after(a, *others):
    return lax.optimization_barrier((a, *others))[0]


def fixed(shape):
    return pl.BlockSpec(shape, lambda j, where: (0, 0), pipeline_mode=pl.Buffered(1))


def tile_rows(t, size=TILE):
    return pl.ds(pl.multiple_of(t * size, size), size)


def columns(where, i, width):
    return pl.ds(pl.multiple_of(where[i] * width, width), width)


def input_body(where, inputs, pi_t, in_t):
    in_t[...] = dot_nt(pi_t[...], inputs[...])


def input_block(where, inputs, pi_t):
    shape = (pi_t.shape[0], inputs.shape[0])
    (in_t,) = call(
        input_body,
        "input_block",
        where,
        (1,),
        (inputs, pi_t),
        [fixed(inputs.shape), fixed(pi_t.shape)],
        [pl.BlockSpec(shape, lambda j, where: (0, 0))],
        [jax.ShapeDtypeStruct(shape, jnp.float32)],
        [],
        LIMIT,
    )
    return in_t


def own_body(where, own, w, w_last, acc, kept, token):
    here = tile_rows(pl.program_id(0))
    token[...] = jnp.zeros_like(token)
    kept[:, here] = w_last[...].T
    acc[:, here] = dot_nt(own[...], w[...])


def own_block(where, own, w):
    tokens, feats = own.shape
    hidden = w.shape[0]
    return call(
        own_body,
        "own_block",
        where,
        (hidden // TILE,),
        (own, w, w),
        [
            fixed(own.shape),
            pl.BlockSpec((TILE, feats), lambda j, where: (j, where[0])),
            pl.BlockSpec((TILE, feats), lambda j, where: (j, where[3])),
        ],
        [INSIDE, INSIDE, pl.BlockSpec((8, 128), lambda j, where: (0, 0))],
        [
            pltpu.VMEM((tokens, hidden), jnp.float32),
            pltpu.VMEM((feats, hidden), w.dtype),
            jax.ShapeDtypeStruct((8, 128), jnp.float32),
        ],
        [],
        LIMIT,
    )


def select(where, inner, outer):
    return jnp.where(where[4] == 1, inner[...], outer[...])


def add_body(where, *refs):
    *blocks, w, old, _, acc, token, block = refs
    step = pl.program_id(0)

    @pl.when(step == 0)
    def _():
        token[...] = jnp.zeros_like(token)
        if len(blocks) == 1:
            block[...] = blocks[0][...]
        else:
            half = len(blocks) // 2
            size = blocks[0].shape[0]
            for h in range(half):
                block[h * size : (h + 1) * size, :] = select(where, blocks[h], blocks[half + h])

    here = tile_rows(step)
    acc[:, here] = old[:, here] + dot_nt(block[...], w[...])


def add_block(where, which, blocks, w, old, token, flops):
    tokens, feats = old.shape[0], blocks[0].shape[1]
    return call(
        add_body,
        f"add_block_{which}",
        where,
        (w.shape[0] // TILE,),
        (*blocks, w, old, token),
        [fixed(a.shape) for a in blocks]
        + [pl.BlockSpec((TILE, feats), lambda j, where: (j, where[which])), INSIDE, ANYWHERE],
        [INSIDE, pl.BlockSpec((8, 128), lambda j, where: (0, 0))],
        [pltpu.VMEM(old.shape, old.dtype), jax.ShapeDtypeStruct((8, 128), jnp.float32)],
        [pltpu.VMEM((tokens, feats), blocks[0].dtype)],
        LIMIT,
        aliases={len(blocks) + 2: 0},
        flops=flops,
    )


def last_body(start, inner_at, bring, where, inner, outer, kept, old, gate, po_t, _, *rest):
    far, rest = rest[:bring], rest[bring:]
    _, _, right, *near = rest[: 3 + bring]
    gates, po, gate_sems, po_sem, near_sems = rest[3 + bring :]
    size = outer.shape[0]
    hidden = kept.shape[1]
    tokens = pl.ds(start, size)
    spans = [pl.ds(t * TILE, TILE) for t in range(hidden // TILE)]
    po_read = pltpu.make_async_copy(po_t, po, po_sem)
    reads = [
        pltpu.make_async_copy(gate.at[tokens, span], gates.at[t], gate_sems.at[t]) for t, span in enumerate(spans)
    ]
    reads[0].start()
    po_read.start()
    for read in reads[1:]:
        read.start()
    brought = [pltpu.make_async_copy(a, b, near_sems.at[i]) for i, (a, b) in enumerate(zip(far, near))]
    for copy in brought:
        copy.start()
    block = select(where, inner.at[pl.ds(inner_at, size)], outer)
    total = jnp.zeros((size, PROJ), jnp.float32)
    for t, span in enumerate(spans):
        hidden_grad = old[tokens, span] + dot(block, kept[:, span])
        reads[t].wait()
        up_grad = (hidden_grad * silu(gates[t].astype(jnp.float32))).astype(jnp.bfloat16)
        if t == 0:
            po_read.wait()
        total = total + dot_nt(up_grad, po[:, span])
    right[...] = total
    for copy in brought:
        copy.wait()


def last_block(where, inner, inner_at, outer, start, kept, old, gate, po_t, token, bring):
    size = outer.shape[0]
    tiles = kept.shape[1] // TILE
    return call(
        functools.partial(last_body, start, inner_at, len(bring)),
        "last_block",
        where,
        (1,),
        (inner, outer, kept, old, gate, po_t, token, *bring),
        [INSIDE, INSIDE, INSIDE, INSIDE, OUTSIDE, ANYWHERE, ANYWHERE] + [OUTSIDE] * len(bring),
        [INSIDE, INSIDE, pl.BlockSpec((size, PROJ), lambda j, where: (0, 0))] + [INSIDE] * len(bring),
        [
            pltpu.VMEM(kept.shape, kept.dtype),
            pltpu.VMEM(old.shape, old.dtype),
            jax.ShapeDtypeStruct((size, PROJ), jnp.float32),
            *[pltpu.VMEM(a.shape, a.dtype) for a in bring],
        ],
        [
            pltpu.VMEM((tiles, size, TILE), gate.dtype),
            pltpu.VMEM(po_t.shape, po_t.dtype),
            pltpu.SemaphoreType.DMA((tiles,)),
            pltpu.SemaphoreType.DMA,
            pltpu.SemaphoreType.DMA((max(len(bring), 1),)),
        ],
        LIMIT,
        aliases={3: 0, 4: 1},
    )


def outer_body(where, total, sent, *refs):
    *rights, grads, wide = refs
    left_t = jnp.where(where[4] == 1, total[...], sent[...].astype(jnp.float32))
    wide[...] = jnp.zeros_like(wide)
    start = 0
    terms = [None] * grads.shape[0]
    for right in rights:
        size = right.shape[0]
        s = start // LEN
        term = jnp.dot(
            left_t[:, start : start + size], right[...], precision=HIGHEST, preferred_element_type=jnp.float32
        )
        terms[s] = term if terms[s] is None else terms[s] + term
        start += size
    for s, term in enumerate(terms):
        wide[:, :PROJ] = term
        even = wide[pl.ds(0, PROJ // 2, stride=2), :]
        odd = wide[pl.ds(1, PROJ // 2, stride=2), :]
        rows = even + pltpu.roll(odd, PROJ, 1)
        for i in range(PROJ // 2):
            grads[s : s + 1, i * 2 * PROJ : (i + 1) * 2 * PROJ] = rows[i : i + 1, :]


def outer_products(where, total, sent, rights):
    shape = (total.shape[1] // LEN, PROJ * PROJ)
    (grads,) = call(
        outer_body,
        "outer_products",
        where,
        (1,),
        (total, sent, *rights),
        [fixed(a.shape) for a in (total, sent, *rights)],
        [pl.BlockSpec(shape, lambda j, where: (0, 0))],
        [jax.ShapeDtypeStruct(shape, jnp.float32)],
        [pltpu.VMEM((PROJ, 2 * PROJ), jnp.float32)],
        LIMIT,
    )
    return grads


def small_kernel(body, name, where, *operands):
    (out,) = call(
        body,
        name,
        where,
        (1,),
        operands,
        [fixed(a.shape) for a in operands],
        [pl.BlockSpec(operands[0].shape, lambda j, where: (0, 0))],
        [jax.ShapeDtypeStruct(operands[0].shape, operands[0].dtype)],
        [],
        LIMIT,
    )
    return out


def sum_body(where, a, b, out):
    out[...] = a[...] + b[...]


def score_body(where, grads, *rest):
    *parts, out = rest
    rows, width = parts[0].shape
    count = grads.shape[0]
    lane = lax.broadcasted_iota(jnp.int32, (rows, 128), 1)
    total = jnp.zeros((rows, 128), jnp.float32)
    for s in range(count):
        products = None
        for p, part in enumerate(parts):
            term = part[...] * grads[s : s + 1, columns(where, FIRST_PART + p, width)]
            products = term if products is None else products + term
        total = jnp.where(lane == s, jnp.sum(products, axis=1, keepdims=True), total)
    out[...] = total.T[:count, :]


def score_parts(where, grads, parts):
    width = parts[0].shape[1]
    shape = (grads.shape[0], parts[0].shape[0])
    if width % 128:
        slices = [
            lax.dynamic_slice_in_dim(grads, where[FIRST_PART + p] * width, width, 1) for p in range(len(parts))
        ]
        return jnp.dot(jnp.concatenate(slices, axis=1), jnp.concatenate(parts, axis=1).T, precision=HIGHEST)
    (scores,) = call(
        score_body,
        "scores",
        where,
        (1,),
        (grads, *parts),
        [fixed(grads.shape)] + [INSIDE] * len(parts),
        [pl.BlockSpec(shape, lambda j, where: (0, 0))],
        [jax.ShapeDtypeStruct(shape, jnp.float32)],
        [],
        LIMIT,
    )
    return scores


def pieces(a):
    high = a.astype(jnp.bfloat16)
    rest = a - high.astype(jnp.float32)
    middle = rest.astype(jnp.bfloat16)
    low = (rest - middle.astype(jnp.float32)).astype(jnp.bfloat16)
    return high, middle, low


def update_body(scale, where, grads, mine, hessian, out, new, out_sems):
    columns = grads.shape[1]
    parts, _, width = new.shape
    high, middle, low = pieces(mine[...])
    left = jnp.concatenate([high, high, middle, middle, high, low], axis=0).T
    writes = []
    for t in range(parts):
        span = pl.ds(t * width, width)
        high, middle, low = pieces(grads[:, span])
        right = jnp.concatenate([high, middle, high, middle, low, high], axis=0)
        new[t] = hessian[:, span] + dot(left, right) * scale
        writes.append(pltpu.make_async_copy(new.at[t], out.at[:, span], out_sems.at[t]))
        writes[t].start()
    for write in writes:
        write.wait()


def update(where, grads, hessian):
    rows, columns = hessian.shape
    count = grads.shape[0]
    parts = 8
    width = columns // parts
    (updated,) = call(
        functools.partial(update_body, 1.0 / count),
        "hessian_update",
        where,
        (1,),
        (grads, grads, hessian),
        [
            fixed(grads.shape),
            pl.BlockSpec((count, rows), lambda j, where: (0, where[FIRST_PART]), pipeline_mode=pl.Buffered(1)),
            INSIDE,
        ],
        [ANYWHERE],
        [jax.ShapeDtypeStruct((rows, columns), jnp.float32)],
        [pltpu.VMEM((parts, rows, width), jnp.float32), pltpu.SemaphoreType.DMA((parts,))],
        LIMIT,
    )
    return updated


def line_of_four(where, inputs, gate_pre, grad_out, w_down, proj_in, proj_out, early, late):
    send = functools.partial(lax.ppermute, axis_name="tensor")
    pairs = [(0, 1), (1, 0), (2, 3), (3, 2)]
    inner = [(1, 2), (2, 1)]
    outward = [(1, 0), (2, 3)]
    inward = [(0, 1), (3, 2)]
    tokens = grad_out.shape[0]
    halves = [slice(0, tokens // 2), slice(tokens // 2, tokens)]
    pair = send(grad_out, perm=pairs)
    own = [grad_out[half] for half in halves]
    mid_inner = [send(a, perm=inner) for a in own]
    in_part = input_block(where, inputs, proj_in.T)
    from_end = send(after(in_part, mid_inner[0]), perm=inward)
    acc, kept, begun = own_block(where, after(grad_out, in_part, *early), w_down)
    mid_outer = [send(after(a, begun), perm=outward) for a in mid_inner]
    end_inner = [send(pair[half], perm=inner) for half in halves]
    side = small_kernel(sum_body, "side", where, in_part, after(from_end, begun, pair))
    total = small_kernel(sum_body, "total", where, side, send(side, perm=inner))
    sent = send(total.astype(jnp.bfloat16), perm=outward)

    acc, first = add_block(where, 1, [pair], w_down, after(acc, mid_outer[0]), begun, 2 * grad_out.size * w_down.shape[0])
    acc, second = add_block(where, 2, mid_inner + mid_outer, w_down, acc, first, 1000)

    sizes = [256] * (tokens // 256 - 1) + [128, 128]
    arrived, done = [total, total, total], [first, first, second]
    rights = []
    start = 0
    for n, size in enumerate(sizes):
        h, at = divmod(start, tokens // 2)
        ahead = arrived[n + 1] if n < 4 else arrived[n]
        end_outer = send(after(end_inner[h][at : at + size], ahead, done[n]), perm=outward)
        arrived.append(end_outer)
        bring = [*early, late] if n == len(sizes) - 2 else []
        kept, acc, right, *brought = last_block(
            where, end_inner[h], at, end_outer, start, kept, acc, gate_pre, proj_out.T, second, bring
        )
        if bring:
            *early, late = brought
        rights.append(right)
        done.append(right)
        start += size
    return outer_products(where, total, sent, rights), early, late


def any_line(where, inputs, gate_pre, grad_out, w_down, proj_in, proj_out, early, late):
    in_part = jnp.dot(inputs, proj_in, preferred_element_type=jnp.float32)
    in_proj = lax.psum(in_part, "tensor").reshape(-1, LEN, PROJ)
    gathered = lax.all_gather(grad_out, "tensor", axis=1, tiled=True)
    up_grad = (dot_nt(gathered, w_down) * silu(gate_pre.astype(jnp.float32))).astype(jnp.bfloat16)
    out_part = jnp.dot(up_grad, proj_out, preferred_element_type=jnp.float32).reshape(-1, LEN, PROJ)
    grads = jnp.einsum("sti,stj->sij", in_proj, out_part, precision=HIGHEST)
    return grads.reshape(-1, PROJ * PROJ), early, late


def swap(a, axis, bit):
    return lax.ppermute(a, axis, [(i, i ^ bit) for i in range(lax.axis_size(axis))])


def bits(axis):
    return [1 << b for b in range(lax.axis_size(axis).bit_length() - 1)]


def xor_sum(a, axis):
    for bit in bits(axis):
        a = a + swap(a, axis, bit)
    return a


def positions():
    z, me, count = lax.axis_index("tensor"), lax.axis_index("dp"), lax.axis_size("dp")
    low = z < 2
    middle = jnp.logical_and(z > 0, z < 3)
    blocks = [z, z + 1 - 2 * (z % 2), jnp.where(low, 2, 1), jnp.where(low, 3, 0), middle]
    parts = [z * count + (me ^ s) for s in range(count)]
    return jnp.stack([a.astype(jnp.int32) for a in blocks + parts])


def on_device(inputs, gate_pre, grad_out, w_down, proj_in, proj_out, hessian, queries):
    where = positions()
    count = lax.axis_size("dp")
    parts = [queries] + [swap(queries, "dp", s) for s in range(1, count)]
    line = line_of_four if lax.axis_size("tensor") == 4 else any_line
    grads, parts, hessian = line(where, inputs, gate_pre, grad_out, w_down, proj_in, proj_out, parts, hessian)
    grads = xor_sum(grads, "tensor")

    scores = score_parts(where, grads, parts)
    all_grads = after(grads, scores)
    *first, last = bits("tensor")
    for n, bit in enumerate(bits("dp")):
        all_grads = jnp.concatenate([all_grads, swap(all_grads, "dp", bit)], axis=0)
        if n == 0:
            for score_bit in first:
                scores = scores + swap(scores, "tensor", score_bit)
            all_grads = after(all_grads, scores)
    others = swap(scores, "tensor", last)
    row_count = hessian.shape[0]
    if row_count % 128:
        mine = lax.dynamic_slice_in_dim(all_grads, where[FIRST_PART] * row_count, row_count, 1)
        updated = hessian + jnp.dot(mine.T, all_grads, precision=HIGHEST) / all_grads.shape[0]
    else:
        updated = update(where, all_grads, hessian)
    updated, others = lax.optimization_barrier((updated, others))
    return (updated, scores + others)


def solution(mesh):
    return jax.shard_map(
        on_device,
        mesh=mesh,
        in_specs=(
            P(("groups", "dp"), "tensor"),
            P(("groups", "dp"), "tensor"),
            P(("groups", "dp"), "tensor"),
            P("tensor", None),
            P("tensor", None),
            P("tensor", None),
            P(("groups", "tensor", "dp"), None),
            P("groups", ("tensor", "dp")),
        ),
        out_specs=(P(("groups", "tensor", "dp"), None), P(("groups", "dp"), None)),
        check_vma=False,
    )
```

```python
import functools

import jax
import jax.numpy as jnp
from jax import lax
from jax.experimental import pallas as pl
from jax.experimental.pallas import tpu as pltpu
from jax.sharding import PartitionSpec as P

PROJ = 64
LEN = 512
HIGHEST = lax.Precision.HIGHEST
NT = (((1,), (1,)), ((), ()))
TILE = 512
LIMIT = 16
FIRST_PART = 5
ANYWHERE = pl.BlockSpec(memory_space=pl.ANY)
INSIDE = pl.BlockSpec(memory_space=pltpu.VMEM)
OUTSIDE = pl.BlockSpec(memory_space=pltpu.HBM)


def silu(v):
    return 0.5 * v * (1.0 + jnp.tanh(0.5 * v))


def dot(a, b):
    return jnp.dot(a, b, preferred_element_type=jnp.float32)


def dot_nt(a, b):
    return lax.dot_general(a, b, NT, preferred_element_type=jnp.float32)


def placed(a, spec):
    if spec is INSIDE or spec is OUTSIDE:
        return pltpu.with_memory_space_constraint(a, spec.memory_space)
    return a


def call(body, name, where, grid, operands, in_specs, out_specs, out_shapes, scratch, mib, aliases=None, flops=1000):
    return pl.pallas_call(
        body,
        grid_spec=pltpu.PrefetchScalarGridSpec(
            num_scalar_prefetch=1, grid=grid, in_specs=in_specs, out_specs=out_specs, scratch_shapes=scratch
        ),
        out_shape=out_shapes,
        compiler_params=pltpu.CompilerParams(vmem_limit_bytes=mib * 2**20),
        cost_estimate=pl.CostEstimate(flops=flops, bytes_accessed=1000, transcendentals=0),
        name=name,
        input_output_aliases=aliases or {},
    )(where, *[placed(a, spec) for a, spec in zip(operands, in_specs)])


def after(a, *others):
    return lax.optimization_barrier((a, *others))[0]


def fixed(shape):
    return pl.BlockSpec(shape, lambda j, where: (0, 0), pipeline_mode=pl.Buffered(1))


def tile_rows(t, size=TILE):
    return pl.ds(pl.multiple_of(t * size, size), size)


def columns(where, i, width):
    return pl.ds(pl.multiple_of(where[i] * width, width), width)


def input_body(where, inputs, pi_t, in_t):
    in_t[...] = dot_nt(pi_t[...], inputs[...])


def input_block(where, inputs, pi_t):
    shape = (pi_t.shape[0], inputs.shape[0])
    (in_t,) = call(
        input_body,
        "input_block",
        where,
        (1,),
        (inputs, pi_t),
        [fixed(inputs.shape), fixed(pi_t.shape)],
        [pl.BlockSpec(shape, lambda j, where: (0, 0))],
        [jax.ShapeDtypeStruct(shape, jnp.float32)],
        [],
        LIMIT,
    )
    return in_t


def own_body(where, own, w, w_last, acc, kept, token):
    here = tile_rows(pl.program_id(0))
    token[...] = jnp.zeros_like(token)
    kept[:, here] = w_last[...].T
    acc[:, here] = dot_nt(own[...], w[...])


def own_block(where, own, w):
    tokens, feats = own.shape
    hidden = w.shape[0]
    return call(
        own_body,
        "own_block",
        where,
        (hidden // TILE,),
        (own, w, w),
        [
            fixed(own.shape),
            pl.BlockSpec((TILE, feats), lambda j, where: (j, where[0])),
            pl.BlockSpec((TILE, feats), lambda j, where: (j, where[3])),
        ],
        [INSIDE, INSIDE, pl.BlockSpec((8, 128), lambda j, where: (0, 0))],
        [
            pltpu.VMEM((tokens, hidden), jnp.float32),
            pltpu.VMEM((feats, hidden), w.dtype),
            jax.ShapeDtypeStruct((8, 128), jnp.float32),
        ],
        [],
        LIMIT,
    )


def select(where, inner, outer):
    return jnp.where(where[4] == 1, inner[...], outer[...])


def add_body(where, *refs):
    *blocks, w, old, _, acc, token, block = refs
    step = pl.program_id(0)

    @pl.when(step == 0)
    def _():
        token[...] = jnp.zeros_like(token)
        if len(blocks) == 1:
            block[...] = blocks[0][...]
        else:
            half = len(blocks) // 2
            size = blocks[0].shape[0]
            for h in range(half):
                block[h * size : (h + 1) * size, :] = select(where, blocks[h], blocks[half + h])

    here = tile_rows(step)
    acc[:, here] = old[:, here] + dot_nt(block[...], w[...])


def add_block(where, which, blocks, w, old, token, flops):
    tokens, feats = old.shape[0], blocks[0].shape[1]
    return call(
        add_body,
        f"add_block_{which}",
        where,
        (w.shape[0] // TILE,),
        (*blocks, w, old, token),
        [fixed(a.shape) for a in blocks]
        + [pl.BlockSpec((TILE, feats), lambda j, where: (j, where[which])), INSIDE, ANYWHERE],
        [INSIDE, pl.BlockSpec((8, 128), lambda j, where: (0, 0))],
        [pltpu.VMEM(old.shape, old.dtype), jax.ShapeDtypeStruct((8, 128), jnp.float32)],
        [pltpu.VMEM((tokens, feats), blocks[0].dtype)],
        LIMIT,
        aliases={len(blocks) + 2: 0},
        flops=flops,
    )


def last_body(start, inner_at, bring, where, inner, outer, kept, old, gate, po_t, _, *rest):
    far, rest = rest[:bring], rest[bring:]
    _, _, right, *near = rest[: 3 + bring]
    gates, po, gate_sems, po_sem, near_sems = rest[3 + bring :]
    size = outer.shape[0]
    hidden = kept.shape[1]
    tokens = pl.ds(start, size)
    spans = [pl.ds(t * TILE, TILE) for t in range(hidden // TILE)]
    po_read = pltpu.make_async_copy(po_t, po, po_sem)
    reads = [
        pltpu.make_async_copy(gate.at[tokens, span], gates.at[t], gate_sems.at[t]) for t, span in enumerate(spans)
    ]
    reads[0].start()
    po_read.start()
    for read in reads[1:]:
        read.start()
    brought = [pltpu.make_async_copy(a, b, near_sems.at[i]) for i, (a, b) in enumerate(zip(far, near))]
    for copy in brought:
        copy.start()
    block = select(where, inner.at[pl.ds(inner_at, size)], outer)
    total = jnp.zeros((size, PROJ), jnp.float32)
    for t, span in enumerate(spans):
        hidden_grad = old[tokens, span] + dot(block, kept[:, span])
        reads[t].wait()
        up_grad = (hidden_grad * silu(gates[t].astype(jnp.float32))).astype(jnp.bfloat16)
        if t == 0:
            po_read.wait()
        total = total + dot_nt(up_grad, po[:, span])
    right[...] = total
    for copy in brought:
        copy.wait()


def last_block(where, inner, inner_at, outer, start, kept, old, gate, po_t, token, bring):
    size = outer.shape[0]
    tiles = kept.shape[1] // TILE
    return call(
        functools.partial(last_body, start, inner_at, len(bring)),
        "last_block",
        where,
        (1,),
        (inner, outer, kept, old, gate, po_t, token, *bring),
        [INSIDE, INSIDE, INSIDE, INSIDE, OUTSIDE, ANYWHERE, ANYWHERE] + [OUTSIDE] * len(bring),
        [INSIDE, INSIDE, pl.BlockSpec((size, PROJ), lambda j, where: (0, 0))] + [INSIDE] * len(bring),
        [
            pltpu.VMEM(kept.shape, kept.dtype),
            pltpu.VMEM(old.shape, old.dtype),
            jax.ShapeDtypeStruct((size, PROJ), jnp.float32),
            *[pltpu.VMEM(a.shape, a.dtype) for a in bring],
        ],
        [
            pltpu.VMEM((tiles, size, TILE), gate.dtype),
            pltpu.VMEM(po_t.shape, po_t.dtype),
            pltpu.SemaphoreType.DMA((tiles,)),
            pltpu.SemaphoreType.DMA,
            pltpu.SemaphoreType.DMA((max(len(bring), 1),)),
        ],
        LIMIT,
        aliases={3: 0, 4: 1},
    )


def outer_body(where, total, sent, *refs):
    *rights, grads, wide = refs
    left_t = jnp.where(where[4] == 1, total[...], sent[...].astype(jnp.float32))
    wide[...] = jnp.zeros_like(wide)
    start = 0
    terms = [None] * grads.shape[0]
    for right in rights:
        size = right.shape[0]
        s = start // LEN
        term = jnp.dot(
            left_t[:, start : start + size], right[...], precision=HIGHEST, preferred_element_type=jnp.float32
        )
        terms[s] = term if terms[s] is None else terms[s] + term
        start += size
    for s, term in enumerate(terms):
        wide[:, :PROJ] = term
        even = wide[pl.ds(0, PROJ // 2, stride=2), :]
        odd = wide[pl.ds(1, PROJ // 2, stride=2), :]
        rows = even + pltpu.roll(odd, PROJ, 1)
        for i in range(PROJ // 2):
            grads[s : s + 1, i * 2 * PROJ : (i + 1) * 2 * PROJ] = rows[i : i + 1, :]


def outer_products(where, total, sent, rights):
    shape = (total.shape[1] // LEN, PROJ * PROJ)
    (grads,) = call(
        outer_body,
        "outer_products",
        where,
        (1,),
        (total, sent, *rights),
        [fixed(a.shape) for a in (total, sent, *rights)],
        [pl.BlockSpec(shape, lambda j, where: (0, 0))],
        [jax.ShapeDtypeStruct(shape, jnp.float32)],
        [pltpu.VMEM((PROJ, 2 * PROJ), jnp.float32)],
        LIMIT,
    )
    return grads


def small_kernel(body, name, where, *operands):
    (out,) = call(
        body,
        name,
        where,
        (1,),
        operands,
        [fixed(a.shape) for a in operands],
        [pl.BlockSpec(operands[0].shape, lambda j, where: (0, 0))],
        [jax.ShapeDtypeStruct(operands[0].shape, operands[0].dtype)],
        [],
        LIMIT,
    )
    return out


def sum_body(where, a, b, out):
    out[...] = a[...] + b[...]


def score_body(where, grads, *rest):
    *parts, out = rest
    rows, width = parts[0].shape
    count = grads.shape[0]
    lane = lax.broadcasted_iota(jnp.int32, (rows, 128), 1)
    total = jnp.zeros((rows, 128), jnp.float32)
    for s in range(count):
        products = None
        for p, part in enumerate(parts):
            term = part[...] * grads[s : s + 1, columns(where, FIRST_PART + p, width)]
            products = term if products is None else products + term
        total = jnp.where(lane == s, jnp.sum(products, axis=1, keepdims=True), total)
    out[...] = total.T[:count, :]


def score_parts(where, grads, parts):
    width = parts[0].shape[1]
    shape = (grads.shape[0], parts[0].shape[0])
    if width % 128:
        slices = [
            lax.dynamic_slice_in_dim(grads, where[FIRST_PART + p] * width, width, 1) for p in range(len(parts))
        ]
        return jnp.dot(jnp.concatenate(slices, axis=1), jnp.concatenate(parts, axis=1).T, precision=HIGHEST)
    (scores,) = call(
        score_body,
        "scores",
        where,
        (1,),
        (grads, *parts),
        [fixed(grads.shape)] + [INSIDE] * len(parts),
        [pl.BlockSpec(shape, lambda j, where: (0, 0))],
        [jax.ShapeDtypeStruct(shape, jnp.float32)],
        [],
        LIMIT,
    )
    return scores


def pieces(a):
    high = a.astype(jnp.bfloat16)
    rest = a - high.astype(jnp.float32)
    middle = rest.astype(jnp.bfloat16)
    low = (rest - middle.astype(jnp.float32)).astype(jnp.bfloat16)
    return high, middle, low


def update_body(scale, where, grads, mine, hessian, out, new, out_sems):
    columns = grads.shape[1]
    parts, _, width = new.shape
    high, middle, low = pieces(mine[...])
    left = jnp.concatenate([high, high, middle, middle, high, low], axis=0).T
    writes = []
    for t in range(parts):
        span = pl.ds(t * width, width)
        high, middle, low = pieces(grads[:, span])
        right = jnp.concatenate([high, middle, high, middle, low, high], axis=0)
        new[t] = hessian[:, span] + dot(left, right) * scale
        writes.append(pltpu.make_async_copy(new.at[t], out.at[:, span], out_sems.at[t]))
        writes[t].start()
    for write in writes:
        write.wait()


def update(where, grads, hessian):
    rows, columns = hessian.shape
    count = grads.shape[0]
    parts = 8
    width = columns // parts
    (updated,) = call(
        functools.partial(update_body, 1.0 / count),
        "hessian_update",
        where,
        (1,),
        (grads, grads, hessian),
        [
            fixed(grads.shape),
            pl.BlockSpec((count, rows), lambda j, where: (0, where[FIRST_PART]), pipeline_mode=pl.Buffered(1)),
            INSIDE,
        ],
        [ANYWHERE],
        [jax.ShapeDtypeStruct((rows, columns), jnp.float32)],
        [pltpu.VMEM((parts, rows, width), jnp.float32), pltpu.SemaphoreType.DMA((parts,))],
        LIMIT,
    )
    return updated


def line_of_four(where, inputs, gate_pre, grad_out, w_down, proj_in, proj_out, early, late):
    send = functools.partial(lax.ppermute, axis_name="tensor")
    pairs = [(0, 1), (1, 0), (2, 3), (3, 2)]
    inner = [(1, 2), (2, 1)]
    outward = [(1, 0), (2, 3)]
    inward = [(0, 1), (3, 2)]
    tokens = grad_out.shape[0]
    halves = [slice(0, tokens // 2), slice(tokens // 2, tokens)]
    pair = send(grad_out, perm=pairs)
    own = [grad_out[half] for half in halves]
    mid_inner = [send(a, perm=inner) for a in own]
    in_part = input_block(where, inputs, proj_in.T)
    from_end = send(after(in_part, mid_inner[0]), perm=inward)
    acc, kept, begun = own_block(where, after(grad_out, in_part, *early), w_down)
    mid_outer = [send(after(a, begun), perm=outward) for a in mid_inner]
    end_inner = [send(pair[half], perm=inner) for half in halves]
    side = small_kernel(sum_body, "side", where, in_part, after(from_end, begun, pair))
    total = small_kernel(sum_body, "total", where, side, send(side, perm=inner))
    sent = send(total.astype(jnp.bfloat16), perm=outward)

    acc, first = add_block(where, 1, [pair], w_down, after(acc, mid_outer[0]), begun, 2 * grad_out.size * w_down.shape[0])
    acc, second = add_block(where, 2, mid_inner + mid_outer, w_down, acc, first, 1000)

    sizes = [256] * (tokens // 256 - 1) + [128, 128]
    arrived, done = [total, total, total], [first, first, second]
    rights = []
    start = 0
    for n, size in enumerate(sizes):
        h, at = divmod(start, tokens // 2)
        ahead = arrived[n + 1] if n < 4 else arrived[n]
        end_outer = send(after(end_inner[h][at : at + size], ahead, done[n]), perm=outward)
        arrived.append(end_outer)
        bring = [*early, late] if n == len(sizes) - 2 else []
        kept, acc, right, *brought = last_block(
            where, end_inner[h], at, end_outer, start, kept, acc, gate_pre, proj_out.T, second, bring
        )
        if bring:
            *early, late = brought
        rights.append(right)
        done.append(right)
        start += size
    return outer_products(where, total, sent, rights), early, late


def any_line(where, inputs, gate_pre, grad_out, w_down, proj_in, proj_out, early, late):
    in_part = jnp.dot(inputs, proj_in, preferred_element_type=jnp.float32)
    in_proj = lax.psum(in_part, "tensor").reshape(-1, LEN, PROJ)
    gathered = lax.all_gather(grad_out, "tensor", axis=1, tiled=True)
    up_grad = (dot_nt(gathered, w_down) * silu(gate_pre.astype(jnp.float32))).astype(jnp.bfloat16)
    out_part = jnp.dot(up_grad, proj_out, preferred_element_type=jnp.float32).reshape(-1, LEN, PROJ)
    grads = jnp.einsum("sti,stj->sij", in_proj, out_part, precision=HIGHEST)
    return grads.reshape(-1, PROJ * PROJ), early, late


def swap(a, axis, bit):
    return lax.ppermute(a, axis, [(i, i ^ bit) for i in range(lax.axis_size(axis))])


def bits(axis):
    return [1 << b for b in range(lax.axis_size(axis).bit_length() - 1)]


def xor_sum(a, axis):
    for bit in bits(axis):
        a = a + swap(a, axis, bit)
    return a


def positions():
    z, me, count = lax.axis_index("tensor"), lax.axis_index("dp"), lax.axis_size("dp")
    low = z < 2
    middle = jnp.logical_and(z > 0, z < 3)
    blocks = [z, z + 1 - 2 * (z % 2), jnp.where(low, 2, 1), jnp.where(low, 3, 0), middle]
    parts = [z * count + (me ^ s) for s in range(count)]
    return jnp.stack([a.astype(jnp.int32) for a in blocks + parts])


def on_device(inputs, gate_pre, grad_out, w_down, proj_in, proj_out, hessian, queries):
    where = positions()
    count = lax.axis_size("dp")
    parts = [queries] + [swap(queries, "dp", s) for s in range(1, count)]
    line = line_of_four if lax.axis_size("tensor") == 4 else any_line
    grads, parts, hessian = line(where, inputs, gate_pre, grad_out, w_down, proj_in, proj_out, parts, hessian)
    grads = lax.all_gather(grads, "tensor").sum(0)

    scores = score_parts(where, grads, parts)
    all_grads = after(grads, scores)
    *first, last = bits("tensor")
    for n, bit in enumerate(bits("dp")):
        all_grads = jnp.concatenate([all_grads, swap(all_grads, "dp", bit)], axis=0)
        if n == 0:
            for score_bit in first:
                scores = scores + swap(scores, "tensor", score_bit)
            all_grads = after(all_grads, scores)
    others = swap(scores, "tensor", last)
    row_count = hessian.shape[0]
    if row_count % 128:
        mine = lax.dynamic_slice_in_dim(all_grads, where[FIRST_PART] * row_count, row_count, 1)
        updated = hessian + jnp.dot(mine.T, all_grads, precision=HIGHEST) / all_grads.shape[0]
    else:
        updated = update(where, all_grads, hessian)
    updated, others = lax.optimization_barrier((updated, others))
    return (updated, scores + others)


def solution(mesh):
    return jax.shard_map(
        on_device,
        mesh=mesh,
        in_specs=(
            P(("groups", "dp"), "tensor"),
            P(("groups", "dp"), "tensor"),
            P(("groups", "dp"), "tensor"),
            P("tensor", None),
            P("tensor", None),
            P("tensor", None),
            P(("groups", "tensor", "dp"), None),
            P("groups", ("tensor", "dp")),
        ),
        out_specs=(P(("groups", "tensor", "dp"), None), P(("groups", "dp"), None)),
        check_vma=False,
    )
```

```python
import functools

import jax
import jax.numpy as jnp
from jax import lax
from jax.experimental import pallas as pl
from jax.experimental.pallas import tpu as pltpu
from jax.sharding import PartitionSpec as P

PROJ = 64
LEN = 512
HIGHEST = lax.Precision.HIGHEST
NT = (((1,), (1,)), ((), ()))
TILE = 512
LIMIT = 16
FIRST_PART = 5
ANYWHERE = pl.BlockSpec(memory_space=pl.ANY)
INSIDE = pl.BlockSpec(memory_space=pltpu.VMEM)
OUTSIDE = pl.BlockSpec(memory_space=pltpu.HBM)


def silu(v):
    return 0.5 * v * (1.0 + jnp.tanh(0.5 * v))


def dot(a, b):
    return jnp.dot(a, b, preferred_element_type=jnp.float32)


def dot_nt(a, b):
    return lax.dot_general(a, b, NT, preferred_element_type=jnp.float32)


def placed(a, spec):
    if spec is INSIDE or spec is OUTSIDE:
        return pltpu.with_memory_space_constraint(a, spec.memory_space)
    return a


def call(body, name, where, grid, operands, in_specs, out_specs, out_shapes, scratch, mib, aliases=None, flops=1000):
    return pl.pallas_call(
        body,
        grid_spec=pltpu.PrefetchScalarGridSpec(
            num_scalar_prefetch=1, grid=grid, in_specs=in_specs, out_specs=out_specs, scratch_shapes=scratch
        ),
        out_shape=out_shapes,
        compiler_params=pltpu.CompilerParams(vmem_limit_bytes=mib * 2**20),
        cost_estimate=pl.CostEstimate(flops=flops, bytes_accessed=1000, transcendentals=0),
        name=name,
        input_output_aliases=aliases or {},
    )(where, *[placed(a, spec) for a, spec in zip(operands, in_specs)])


def after(a, *others):
    return lax.optimization_barrier((a, *others))[0]


def fixed(shape):
    return pl.BlockSpec(shape, lambda j, where: (0, 0), pipeline_mode=pl.Buffered(1))


def tile_rows(t, size=TILE):
    return pl.ds(pl.multiple_of(t * size, size), size)


def columns(where, i, width):
    return pl.ds(pl.multiple_of(where[i] * width, width), width)


def input_body(where, inputs, pi_t, in_t):
    in_t[...] = dot_nt(pi_t[...], inputs[...])


def input_block(where, inputs, pi_t):
    shape = (pi_t.shape[0], inputs.shape[0])
    (in_t,) = call(
        input_body,
        "input_block",
        where,
        (1,),
        (inputs, pi_t),
        [fixed(inputs.shape), fixed(pi_t.shape)],
        [pl.BlockSpec(shape, lambda j, where: (0, 0))],
        [jax.ShapeDtypeStruct(shape, jnp.float32)],
        [],
        LIMIT,
    )
    return in_t


def own_body(where, own, w, w_last, acc, kept, token):
    here = tile_rows(pl.program_id(0))
    token[...] = jnp.zeros_like(token)
    kept[:, here] = w_last[...].T
    acc[:, here] = dot_nt(own[...], w[...])


def own_block(where, own, w):
    tokens, feats = own.shape
    hidden = w.shape[0]
    return call(
        own_body,
        "own_block",
        where,
        (hidden // TILE,),
        (own, w, w),
        [
            fixed(own.shape),
            pl.BlockSpec((TILE, feats), lambda j, where: (j, where[0])),
            pl.BlockSpec((TILE, feats), lambda j, where: (j, where[3])),
        ],
        [INSIDE, INSIDE, pl.BlockSpec((8, 128), lambda j, where: (0, 0))],
        [
            pltpu.VMEM((tokens, hidden), jnp.float32),
            pltpu.VMEM((feats, hidden), w.dtype),
            jax.ShapeDtypeStruct((8, 128), jnp.float32),
        ],
        [],
        LIMIT,
    )


def select(where, inner, outer):
    return jnp.where(where[4] == 1, inner[...], outer[...])


def add_body(where, *refs):
    *blocks, w, old, _, acc, token, block = refs
    step = pl.program_id(0)

    @pl.when(step == 0)
    def _():
        token[...] = jnp.zeros_like(token)
        if len(blocks) == 1:
            block[...] = blocks[0][...]
        else:
            half = len(blocks) // 2
            size = blocks[0].shape[0]
            for h in range(half):
                block[h * size : (h + 1) * size, :] = select(where, blocks[h], blocks[half + h])

    here = tile_rows(step)
    acc[:, here] = old[:, here] + dot_nt(block[...], w[...])


def add_block(where, which, blocks, w, old, token, flops):
    tokens, feats = old.shape[0], blocks[0].shape[1]
    return call(
        add_body,
        f"add_block_{which}",
        where,
        (w.shape[0] // TILE,),
        (*blocks, w, old, token),
        [fixed(a.shape) for a in blocks]
        + [pl.BlockSpec((TILE, feats), lambda j, where: (j, where[which])), INSIDE, ANYWHERE],
        [INSIDE, pl.BlockSpec((8, 128), lambda j, where: (0, 0))],
        [pltpu.VMEM(old.shape, old.dtype), jax.ShapeDtypeStruct((8, 128), jnp.float32)],
        [pltpu.VMEM((tokens, feats), blocks[0].dtype)],
        LIMIT,
        aliases={len(blocks) + 2: 0},
        flops=flops,
    )


def part_body(start, inner_at, low, bring, where, inner, outer, kept, old, *rest):
    far, rest = rest[:bring], rest[bring:]
    _, acc, token, *near = rest[: 3 + bring]
    near_sems = rest[3 + bring]
    size, width = outer.shape
    feats = pl.ds(low, width)
    tokens = pl.ds(start, size)
    brought = [pltpu.make_async_copy(a, b, near_sems.at[i]) for i, (a, b) in enumerate(zip(far, near))]
    for copy in brought:
        copy.start()
    token[...] = jnp.zeros_like(token)
    block = select(where, inner.at[pl.ds(inner_at, size), feats], outer)
    for t in range(kept.shape[1] // TILE):
        span = pl.ds(t * TILE, TILE)
        acc[tokens, span] = old[tokens, span] + dot(block, kept[feats, span])
    for copy in brought:
        copy.wait()


def part_block(where, inner, inner_at, low, outer, start, kept, old, bring):
    return call(
        functools.partial(part_body, start, inner_at, low, len(bring)),
        "part_block",
        where,
        (1,),
        (inner, outer, kept, old, *bring),
        [INSIDE] * 4 + [OUTSIDE] * len(bring),
        [INSIDE, INSIDE, pl.BlockSpec((8, 128), lambda j, where: (0, 0))] + [INSIDE] * len(bring),
        [
            pltpu.VMEM(kept.shape, kept.dtype),
            pltpu.VMEM(old.shape, old.dtype),
            jax.ShapeDtypeStruct((8, 128), jnp.float32),
            *[pltpu.VMEM(a.shape, a.dtype) for a in bring],
        ],
        [pltpu.SemaphoreType.DMA((len(bring),))],
        LIMIT,
        aliases={3: 0, 4: 1},
    )


def last_body(start, inner_at, low, where, inner, outer, kept, old, gate, po_t, _, *rest):
    _, _, right, gates, po, gate_sems, po_sem = rest
    size, width = outer.shape
    feats = pl.ds(low, width)
    hidden = kept.shape[1]
    tokens = pl.ds(start, size)
    spans = [pl.ds(t * TILE, TILE) for t in range(hidden // TILE)]
    po_read = pltpu.make_async_copy(po_t, po, po_sem)
    reads = [
        pltpu.make_async_copy(gate.at[tokens, span], gates.at[t], gate_sems.at[t]) for t, span in enumerate(spans)
    ]
    reads[0].start()
    po_read.start()
    for read in reads[1:]:
        read.start()
    block = select(where, inner.at[pl.ds(inner_at, size), feats], outer)
    total = jnp.zeros((size, PROJ), jnp.float32)
    for t, span in enumerate(spans):
        hidden_grad = old[tokens, span] + dot(block, kept[feats, span])
        reads[t].wait()
        up_grad = (hidden_grad * silu(gates[t].astype(jnp.float32))).astype(jnp.bfloat16)
        if t == 0:
            po_read.wait()
        total = total + dot_nt(up_grad, po[:, span])
    right[...] = total


def last_block(where, inner, inner_at, low, outer, start, kept, old, gate, po_t, token):
    size = outer.shape[0]
    tiles = kept.shape[1] // TILE
    return call(
        functools.partial(last_body, start, inner_at, low),
        "last_block",
        where,
        (1,),
        (inner, outer, kept, old, gate, po_t, token),
        [INSIDE, INSIDE, INSIDE, INSIDE, OUTSIDE, ANYWHERE, ANYWHERE],
        [INSIDE, INSIDE, pl.BlockSpec((size, PROJ), lambda j, where: (0, 0))],
        [
            pltpu.VMEM(kept.shape, kept.dtype),
            pltpu.VMEM(old.shape, old.dtype),
            jax.ShapeDtypeStruct((size, PROJ), jnp.float32),
        ],
        [
            pltpu.VMEM((tiles, size, TILE), gate.dtype),
            pltpu.VMEM(po_t.shape, po_t.dtype),
            pltpu.SemaphoreType.DMA((tiles,)),
            pltpu.SemaphoreType.DMA,
        ],
        LIMIT,
        aliases={3: 0, 4: 1},
    )


def outer_body(where, total, sent, *refs):
    *rights, grads, wide = refs
    left_t = jnp.where(where[4] == 1, total[...], sent[...].astype(jnp.float32))
    wide[...] = jnp.zeros_like(wide)
    start = 0
    terms = [None] * grads.shape[0]
    for right in rights:
        size = right.shape[0]
        s = start // LEN
        term = jnp.dot(
            left_t[:, start : start + size], right[...], precision=HIGHEST, preferred_element_type=jnp.float32
        )
        terms[s] = term if terms[s] is None else terms[s] + term
        start += size
    for s, term in enumerate(terms):
        wide[:, :PROJ] = term
        even = wide[pl.ds(0, PROJ // 2, stride=2), :]
        odd = wide[pl.ds(1, PROJ // 2, stride=2), :]
        rows = even + pltpu.roll(odd, PROJ, 1)
        for i in range(PROJ // 2):
            grads[s : s + 1, i * 2 * PROJ : (i + 1) * 2 * PROJ] = rows[i : i + 1, :]


def outer_products(where, total, sent, rights):
    shape = (total.shape[1] // LEN, PROJ * PROJ)
    (grads,) = call(
        outer_body,
        "outer_products",
        where,
        (1,),
        (total, sent, *rights),
        [fixed(a.shape) for a in (total, sent, *rights)],
        [pl.BlockSpec(shape, lambda j, where: (0, 0))],
        [jax.ShapeDtypeStruct(shape, jnp.float32)],
        [pltpu.VMEM((PROJ, 2 * PROJ), jnp.float32)],
        LIMIT,
    )
    return grads


def small_kernel(body, name, where, *operands):
    (out,) = call(
        body,
        name,
        where,
        (1,),
        operands,
        [fixed(a.shape) for a in operands],
        [pl.BlockSpec(operands[0].shape, lambda j, where: (0, 0))],
        [jax.ShapeDtypeStruct(operands[0].shape, operands[0].dtype)],
        [],
        LIMIT,
    )
    return out


def score_sum(where, a, b):
    out = pltpu.VMEM(a.shape, a.dtype)
    (total,) = call(
        sum_body, "score_sum", where, (1,), (a, b), [INSIDE, INSIDE], [INSIDE], [out], [], LIMIT, flops=3 * 10**9
    )
    return total


def sum_body(where, a, b, out):
    out[...] = a[...] + b[...]


def score_body(where, grads, *rest):
    *parts, out = rest
    rows, width = parts[0].shape
    count = grads.shape[0]
    lane = lax.broadcasted_iota(jnp.int32, (rows, 128), 1)
    total = jnp.zeros((rows, 128), jnp.float32)
    for s in range(count):
        products = None
        for p, part in enumerate(parts):
            term = part[...] * grads[s : s + 1, columns(where, FIRST_PART + p, width)]
            products = term if products is None else products + term
        total = jnp.where(lane == s, jnp.sum(products, axis=1, keepdims=True), total)
    out[...] = total.T[:count, :]


def score_parts(where, grads, parts):
    width = parts[0].shape[1]
    shape = (grads.shape[0], parts[0].shape[0])
    if width % 128:
        slices = [
            lax.dynamic_slice_in_dim(grads, where[FIRST_PART + p] * width, width, 1) for p in range(len(parts))
        ]
        return jnp.dot(jnp.concatenate(slices, axis=1), jnp.concatenate(parts, axis=1).T, precision=HIGHEST)
    (scores,) = call(
        score_body,
        "scores",
        where,
        (1,),
        (grads, *parts),
        [fixed(grads.shape)] + [INSIDE] * len(parts),
        [pl.BlockSpec(shape, lambda j, where: (0, 0))],
        [jax.ShapeDtypeStruct(shape, jnp.float32)],
        [],
        LIMIT,
    )
    return scores


def pieces(a):
    high = a.astype(jnp.bfloat16)
    rest = a - high.astype(jnp.float32)
    middle = rest.astype(jnp.bfloat16)
    low = (rest - middle.astype(jnp.float32)).astype(jnp.bfloat16)
    return high, middle, low


def update_body(scale, where, grads, mine, hessian, out, new, out_sems):
    columns = grads.shape[1]
    parts, _, width = new.shape
    high, middle, low = pieces(mine[...])
    left = jnp.concatenate([high, high, middle, middle, high, low], axis=0).T
    writes = []
    for t in range(parts):
        span = pl.ds(t * width, width)
        high, middle, low = pieces(grads[:, span])
        right = jnp.concatenate([high, middle, high, middle, low, high], axis=0)
        new[t] = hessian[:, span] + dot(left, right) * scale
        writes.append(pltpu.make_async_copy(new.at[t], out.at[:, span], out_sems.at[t]))
        writes[t].start()
    for write in writes:
        write.wait()


def update(where, grads, hessian):
    rows, columns = hessian.shape
    count = grads.shape[0]
    parts = 8
    width = columns // parts
    (updated,) = call(
        functools.partial(update_body, 1.0 / count),
        "hessian_update",
        where,
        (1,),
        (grads, grads, hessian),
        [
            fixed(grads.shape),
            pl.BlockSpec((count, rows), lambda j, where: (0, where[FIRST_PART]), pipeline_mode=pl.Buffered(1)),
            INSIDE,
        ],
        [ANYWHERE],
        [jax.ShapeDtypeStruct((rows, columns), jnp.float32)],
        [pltpu.VMEM((parts, rows, width), jnp.float32), pltpu.SemaphoreType.DMA((parts,))],
        LIMIT,
        flops=1000,
    )
    return updated


def line_of_four(where, inputs, gate_pre, grad_out, w_down, proj_in, proj_out, early, late):
    send = functools.partial(lax.ppermute, axis_name="tensor")
    pairs = [(0, 1), (1, 0), (2, 3), (3, 2)]
    inner = [(1, 2), (2, 1)]
    outward = [(1, 0), (2, 3)]
    inward = [(0, 1), (3, 2)]
    tokens = grad_out.shape[0]
    halves = [slice(0, tokens // 2), slice(tokens // 2, tokens)]
    pair = send(grad_out, perm=pairs)
    own = [grad_out[half] for half in halves]
    mid_inner = [send(a, perm=inner) for a in own]
    in_part = input_block(where, inputs, proj_in.T)
    from_end = send(after(in_part, mid_inner[0]), perm=inward)
    acc, kept, begun = own_block(where, after(grad_out, in_part, *early), w_down)
    mid_outer = [send(after(a, begun), perm=outward) for a in mid_inner]
    end_inner = [send(pair[half], perm=inner) for half in halves]
    side = small_kernel(sum_body, "side", where, in_part, after(from_end, begun, pair))
    total = small_kernel(sum_body, "total", where, side, send(side, perm=inner))
    sent = send(total.astype(jnp.bfloat16), perm=outward)

    acc, first = add_block(where, 1, [pair], w_down, after(acc, mid_outer[0]), begun, 2 * grad_out.size * w_down.shape[0])
    acc, second = add_block(where, 2, mid_inner + mid_outer, w_down, acc, first, 1000)

    size, feats = 256, grad_out.shape[1]
    pieces_at = [(start, 0, feats) for start in range(0, tokens - size, size)]
    pieces_at += [(tokens - size, 0, feats // 2), (tokens - size, feats // 2, feats)]
    arrived, done = [total, total, total], [first, first, second]
    rights = []
    for n, (start, low, high) in enumerate(pieces_at):
        h, at = divmod(start, tokens // 2)
        ahead = arrived[n + 1] if n < 4 else arrived[n]
        end_outer = send(after(end_inner[h][at : at + size, low:high], ahead, done[n]), perm=outward)
        arrived.append(end_outer)
        if high < feats:
            kept, acc, token, *brought = part_block(
                where, end_inner[h], at, low, end_outer, start, kept, acc, [*early, late]
            )
            *early, late = brought
            done.append(token)
            continue
        kept, acc, right = last_block(
            where, end_inner[h], at, low, end_outer, start, kept, acc, gate_pre, proj_out.T, second
        )
        rights.append(right)
        done.append(right)
    return outer_products(where, total, sent, rights), early, late


def any_line(where, inputs, gate_pre, grad_out, w_down, proj_in, proj_out, early, late):
    in_part = jnp.dot(inputs, proj_in, preferred_element_type=jnp.float32)
    in_proj = lax.psum(in_part, "tensor").reshape(-1, LEN, PROJ)
    gathered = lax.all_gather(grad_out, "tensor", axis=1, tiled=True)
    up_grad = (dot_nt(gathered, w_down) * silu(gate_pre.astype(jnp.float32))).astype(jnp.bfloat16)
    out_part = jnp.dot(up_grad, proj_out, preferred_element_type=jnp.float32).reshape(-1, LEN, PROJ)
    grads = jnp.einsum("sti,stj->sij", in_proj, out_part, precision=HIGHEST)
    return grads.reshape(-1, PROJ * PROJ), early, late


def swap(a, axis, bit):
    return lax.ppermute(a, axis, [(i, i ^ bit) for i in range(lax.axis_size(axis))])


def bits(axis):
    return [1 << b for b in range(lax.axis_size(axis).bit_length() - 1)]


def xor_sum(a, axis):
    for bit in bits(axis):
        a = a + swap(a, axis, bit)
    return a


def positions():
    z, me, count = lax.axis_index("tensor"), lax.axis_index("dp"), lax.axis_size("dp")
    low = z < 2
    middle = jnp.logical_and(z > 0, z < 3)
    blocks = [z, z + 1 - 2 * (z % 2), jnp.where(low, 2, 1), jnp.where(low, 3, 0), middle]
    parts = [z * count + (me ^ s) for s in range(count)]
    return jnp.stack([a.astype(jnp.int32) for a in blocks + parts])


def on_device(inputs, gate_pre, grad_out, w_down, proj_in, proj_out, hessian, queries):
    where = positions()
    count = lax.axis_size("dp")
    parts = [queries] + [swap(queries, "dp", s) for s in range(1, count)]
    line = line_of_four if lax.axis_size("tensor") == 4 else any_line
    grads, parts, hessian = line(where, inputs, gate_pre, grad_out, w_down, proj_in, proj_out, parts, hessian)
    grads = xor_sum(grads, "tensor")

    scores = score_parts(where, grads, parts)
    all_grads = after(grads, scores)
    *first, last = bits("tensor")
    for bit in bits("dp"):
        all_grads = jnp.concatenate([all_grads, swap(all_grads, "dp", bit)], axis=0)
    for bit in first:
        scores = score_sum(where, scores, swap(scores, "tensor", bit))
    others = swap(scores, "tensor", last)
    all_grads = after(all_grads, scores)
    row_count = hessian.shape[0]
    if row_count % 128:
        mine = lax.dynamic_slice_in_dim(all_grads, where[FIRST_PART] * row_count, row_count, 1)
        updated = hessian + jnp.dot(mine.T, all_grads, precision=HIGHEST) / all_grads.shape[0]
    else:
        updated = update(where, all_grads, hessian)
    updated, others = lax.optimization_barrier((updated, others))
    return (updated, scores + others)


def solution(mesh):
    return jax.shard_map(
        on_device,
        mesh=mesh,
        in_specs=(
            P(("groups", "dp"), "tensor"),
            P(("groups", "dp"), "tensor"),
            P(("groups", "dp"), "tensor"),
            P("tensor", None),
            P("tensor", None),
            P("tensor", None),
            P(("groups", "tensor", "dp"), None),
            P("groups", ("tensor", "dp")),
        ),
        out_specs=(P(("groups", "tensor", "dp"), None), P(("groups", "dp"), None)),
        check_vma=False,
    )
```

```python
import functools

import jax
import jax.numpy as jnp
from jax import lax
from jax.experimental import pallas as pl
from jax.experimental.pallas import tpu as pltpu
from jax.sharding import PartitionSpec as P

PROJ = 64
LEN = 512
HIGHEST = lax.Precision.HIGHEST
NT = (((1,), (1,)), ((), ()))
TILE = 512
LIMIT = 16
FIRST_PART = 5
ANYWHERE = pl.BlockSpec(memory_space=pl.ANY)
INSIDE = pl.BlockSpec(memory_space=pltpu.VMEM)
OUTSIDE = pl.BlockSpec(memory_space=pltpu.HBM)


def silu(v):
    return 0.5 * v * (1.0 + jnp.tanh(0.5 * v))


def dot(a, b):
    return jnp.dot(a, b, preferred_element_type=jnp.float32)


def dot_nt(a, b):
    return lax.dot_general(a, b, NT, preferred_element_type=jnp.float32)


def placed(a, spec):
    if spec is INSIDE or spec is OUTSIDE:
        return pltpu.with_memory_space_constraint(a, spec.memory_space)
    return a


def call(body, name, where, grid, operands, in_specs, out_specs, out_shapes, scratch, mib, aliases=None, flops=1000):
    return pl.pallas_call(
        body,
        grid_spec=pltpu.PrefetchScalarGridSpec(
            num_scalar_prefetch=1, grid=grid, in_specs=in_specs, out_specs=out_specs, scratch_shapes=scratch
        ),
        out_shape=out_shapes,
        compiler_params=pltpu.CompilerParams(vmem_limit_bytes=mib * 2**20),
        cost_estimate=pl.CostEstimate(flops=flops, bytes_accessed=1000, transcendentals=0),
        name=name,
        input_output_aliases=aliases or {},
    )(where, *[placed(a, spec) for a, spec in zip(operands, in_specs)])


def after(a, *others):
    return lax.optimization_barrier((a, *others))[0]


def fixed(shape):
    return pl.BlockSpec(shape, lambda j, where: (0, 0), pipeline_mode=pl.Buffered(1))


def tile_rows(t, size=TILE):
    return pl.ds(pl.multiple_of(t * size, size), size)


def columns(where, i, width):
    return pl.ds(pl.multiple_of(where[i] * width, width), width)


def input_body(where, inputs, pi_t, in_t):
    in_t[...] = dot_nt(pi_t[...], inputs[...])


def input_block(where, inputs, pi_t):
    shape = (pi_t.shape[0], inputs.shape[0])
    (in_t,) = call(
        input_body,
        "input_block",
        where,
        (1,),
        (inputs, pi_t),
        [fixed(inputs.shape), fixed(pi_t.shape)],
        [pl.BlockSpec(shape, lambda j, where: (0, 0))],
        [jax.ShapeDtypeStruct(shape, jnp.float32)],
        [],
        LIMIT,
    )
    return in_t


def own_body(where, own, w, w_last, acc, kept, token):
    here = tile_rows(pl.program_id(0))
    token[...] = jnp.zeros_like(token)
    kept[:, here] = w_last[...].T
    acc[:, here] = dot_nt(own[...], w[...])


def own_block(where, own, w):
    tokens, feats = own.shape
    hidden = w.shape[0]
    return call(
        own_body,
        "own_block",
        where,
        (hidden // TILE,),
        (own, w, w),
        [
            fixed(own.shape),
            pl.BlockSpec((TILE, feats), lambda j, where: (j, where[0])),
            pl.BlockSpec((TILE, feats), lambda j, where: (j, where[3])),
        ],
        [INSIDE, INSIDE, pl.BlockSpec((8, 128), lambda j, where: (0, 0))],
        [
            pltpu.VMEM((tokens, hidden), jnp.float32),
            pltpu.VMEM((feats, hidden), w.dtype),
            jax.ShapeDtypeStruct((8, 128), jnp.float32),
        ],
        [],
        LIMIT,
    )


def select(where, inner, outer):
    return jnp.where(where[4] == 1, inner[...], outer[...])


def add_body(where, *refs):
    *blocks, w, old, _, acc, token, block = refs
    step = pl.program_id(0)

    @pl.when(step == 0)
    def _():
        token[...] = jnp.zeros_like(token)
        if len(blocks) == 1:
            block[...] = blocks[0][...]
        else:
            half = len(blocks) // 2
            size = blocks[0].shape[0]
            for h in range(half):
                block[h * size : (h + 1) * size, :] = select(where, blocks[h], blocks[half + h])

    here = tile_rows(step)
    acc[:, here] = old[:, here] + dot_nt(block[...], w[...])


def add_block(where, which, blocks, w, old, token, flops):
    tokens, feats = old.shape[0], blocks[0].shape[1]
    return call(
        add_body,
        f"add_block_{which}",
        where,
        (w.shape[0] // TILE,),
        (*blocks, w, old, token),
        [fixed(a.shape) for a in blocks]
        + [pl.BlockSpec((TILE, feats), lambda j, where: (j, where[which])), INSIDE, ANYWHERE],
        [INSIDE, pl.BlockSpec((8, 128), lambda j, where: (0, 0))],
        [pltpu.VMEM(old.shape, old.dtype), jax.ShapeDtypeStruct((8, 128), jnp.float32)],
        [pltpu.VMEM((tokens, feats), blocks[0].dtype)],
        LIMIT,
        aliases={len(blocks) + 2: 0},
        flops=flops,
    )


def last_body(start, inner_at, bring, where, inner, outer, kept, old, gate, po_t, _, *rest):
    far, rest = rest[:bring], rest[bring:]
    _, _, right, *near = rest[: 3 + bring]
    gates, po, gate_sems, po_sem, near_sems = rest[3 + bring :]
    size = outer.shape[0]
    hidden = kept.shape[1]
    tokens = pl.ds(start, size)
    spans = [pl.ds(t * TILE, TILE) for t in range(hidden // TILE)]
    po_read = pltpu.make_async_copy(po_t, po, po_sem)
    reads = [
        pltpu.make_async_copy(gate.at[tokens, span], gates.at[t], gate_sems.at[t]) for t, span in enumerate(spans)
    ]
    reads[0].start()
    po_read.start()
    for read in reads[1:]:
        read.start()
    brought = [pltpu.make_async_copy(a, b, near_sems.at[i]) for i, (a, b) in enumerate(zip(far, near))]
    for copy in brought:
        copy.start()
    block = select(where, inner.at[pl.ds(inner_at, size)], outer)
    total = jnp.zeros((size, PROJ), jnp.float32)
    for t, span in enumerate(spans):
        hidden_grad = old[tokens, span] + dot(block, kept[:, span])
        reads[t].wait()
        up_grad = (hidden_grad * silu(gates[t].astype(jnp.float32))).astype(jnp.bfloat16)
        if t == 0:
            po_read.wait()
        total = total + dot_nt(up_grad, po[:, span])
    right[...] = total
    for copy in brought:
        copy.wait()


def last_block(where, inner, inner_at, outer, start, kept, old, gate, po_t, token, bring):
    size = outer.shape[0]
    tiles = kept.shape[1] // TILE
    return call(
        functools.partial(last_body, start, inner_at, len(bring)),
        "last_block",
        where,
        (1,),
        (inner, outer, kept, old, gate, po_t, token, *bring),
        [INSIDE, INSIDE, INSIDE, INSIDE, OUTSIDE, ANYWHERE, ANYWHERE] + [OUTSIDE] * len(bring),
        [INSIDE, INSIDE, pl.BlockSpec((size, PROJ), lambda j, where: (0, 0))] + [INSIDE] * len(bring),
        [
            pltpu.VMEM(kept.shape, kept.dtype),
            pltpu.VMEM(old.shape, old.dtype),
            jax.ShapeDtypeStruct((size, PROJ), jnp.float32),
            *[pltpu.VMEM(a.shape, a.dtype) for a in bring],
        ],
        [
            pltpu.VMEM((tiles, size, TILE), gate.dtype),
            pltpu.VMEM(po_t.shape, po_t.dtype),
            pltpu.SemaphoreType.DMA((tiles,)),
            pltpu.SemaphoreType.DMA,
            pltpu.SemaphoreType.DMA((max(len(bring), 1),)),
        ],
        LIMIT,
        aliases={3: 0, 4: 1},
    )


def outer_body(where, total, sent, *refs):
    *rights, grads, wide = refs
    left_t = jnp.where(where[4] == 1, total[...], sent[...].astype(jnp.float32))
    wide[...] = jnp.zeros_like(wide)
    start = 0
    terms = [None] * grads.shape[0]
    for right in rights:
        size = right.shape[0]
        s = start // LEN
        term = jnp.dot(
            left_t[:, start : start + size], right[...], precision=HIGHEST, preferred_element_type=jnp.float32
        )
        terms[s] = term if terms[s] is None else terms[s] + term
        start += size
    for s, term in enumerate(terms):
        wide[:, :PROJ] = term
        even = wide[pl.ds(0, PROJ // 2, stride=2), :]
        odd = wide[pl.ds(1, PROJ // 2, stride=2), :]
        rows = even + pltpu.roll(odd, PROJ, 1)
        for i in range(PROJ // 2):
            grads[s : s + 1, i * 2 * PROJ : (i + 1) * 2 * PROJ] = rows[i : i + 1, :]


def outer_products(where, total, sent, rights):
    shape = (total.shape[1] // LEN, PROJ * PROJ)
    (grads,) = call(
        outer_body,
        "outer_products",
        where,
        (1,),
        (total, sent, *rights),
        [fixed(a.shape) for a in (total, sent, *rights)],
        [pl.BlockSpec(shape, lambda j, where: (0, 0))],
        [jax.ShapeDtypeStruct(shape, jnp.float32)],
        [pltpu.VMEM((PROJ, 2 * PROJ), jnp.float32)],
        LIMIT,
    )
    return grads


def small_kernel(body, name, where, *operands):
    (out,) = call(
        body,
        name,
        where,
        (1,),
        operands,
        [fixed(a.shape) for a in operands],
        [pl.BlockSpec(operands[0].shape, lambda j, where: (0, 0))],
        [jax.ShapeDtypeStruct(operands[0].shape, operands[0].dtype)],
        [],
        LIMIT,
    )
    return out


def score_sum(where, a, b):
    out = pltpu.VMEM(a.shape, a.dtype)
    (total,) = call(
        sum_body, "score_sum", where, (1,), (a, b), [INSIDE, INSIDE], [INSIDE], [out], [], LIMIT, flops=3 * 10**9
    )
    return total


def sum_body(where, a, b, out):
    out[...] = a[...] + b[...]


def score_body(where, grads, *rest):
    *parts, out = rest
    rows, width = parts[0].shape
    count = grads.shape[0]
    lane = lax.broadcasted_iota(jnp.int32, (rows, 128), 1)
    total = jnp.zeros((rows, 128), jnp.float32)
    for s in range(count):
        products = None
        for p, part in enumerate(parts):
            term = part[...] * grads[s : s + 1, columns(where, FIRST_PART + p, width)]
            products = term if products is None else products + term
        total = jnp.where(lane == s, jnp.sum(products, axis=1, keepdims=True), total)
    out[...] = total.T[:count, :]


def score_parts(where, grads, parts):
    width = parts[0].shape[1]
    shape = (grads.shape[0], parts[0].shape[0])
    if width % 128:
        slices = [
            lax.dynamic_slice_in_dim(grads, where[FIRST_PART + p] * width, width, 1) for p in range(len(parts))
        ]
        return jnp.dot(jnp.concatenate(slices, axis=1), jnp.concatenate(parts, axis=1).T, precision=HIGHEST)
    (scores,) = call(
        score_body,
        "scores",
        where,
        (1,),
        (grads, *parts),
        [fixed(grads.shape)] + [INSIDE] * len(parts),
        [pl.BlockSpec(shape, lambda j, where: (0, 0))],
        [jax.ShapeDtypeStruct(shape, jnp.float32)],
        [],
        LIMIT,
    )
    return scores


def pieces(a):
    high = a.astype(jnp.bfloat16)
    rest = a - high.astype(jnp.float32)
    middle = rest.astype(jnp.bfloat16)
    low = (rest - middle.astype(jnp.float32)).astype(jnp.bfloat16)
    return high, middle, low


def update_body(scale, where, grads, mine, hessian, out, new, out_sems):
    columns = grads.shape[1]
    parts, _, width = new.shape
    high, middle, low = pieces(mine[...])
    left = jnp.concatenate([high, high, middle, middle, high, low], axis=0).T
    writes = []
    for t in range(parts):
        span = pl.ds(t * width, width)
        high, middle, low = pieces(grads[:, span])
        right = jnp.concatenate([high, middle, high, middle, low, high], axis=0)
        new[t] = hessian[:, span] + dot(left, right) * scale
        writes.append(pltpu.make_async_copy(new.at[t], out.at[:, span], out_sems.at[t]))
        writes[t].start()
    for write in writes:
        write.wait()


def update(where, grads, hessian):
    rows, columns = hessian.shape
    count = grads.shape[0]
    parts = 8
    width = columns // parts
    (updated,) = call(
        functools.partial(update_body, 1.0 / count),
        "hessian_update",
        where,
        (1,),
        (grads, grads, hessian),
        [
            fixed(grads.shape),
            pl.BlockSpec((count, rows), lambda j, where: (0, where[FIRST_PART]), pipeline_mode=pl.Buffered(1)),
            INSIDE,
        ],
        [ANYWHERE],
        [jax.ShapeDtypeStruct((rows, columns), jnp.float32)],
        [pltpu.VMEM((parts, rows, width), jnp.float32), pltpu.SemaphoreType.DMA((parts,))],
        LIMIT,
        flops=1000,
    )
    return updated


def line_of_four(where, inputs, gate_pre, grad_out, w_down, proj_in, proj_out, early, late):
    send = functools.partial(lax.ppermute, axis_name="tensor")
    pairs = [(0, 1), (1, 0), (2, 3), (3, 2)]
    inner = [(1, 2), (2, 1)]
    outward = [(1, 0), (2, 3)]
    inward = [(0, 1), (3, 2)]
    tokens = grad_out.shape[0]
    halves = [slice(0, tokens // 2), slice(tokens // 2, tokens)]
    pair = send(grad_out, perm=pairs)
    own = [grad_out[half] for half in halves]
    mid_inner = [send(a, perm=inner) for a in own]
    in_part = input_block(where, inputs, proj_in.T)
    from_end = send(after(in_part, mid_inner[0]), perm=inward)
    acc, kept, begun = own_block(where, after(grad_out, in_part, *early), w_down)
    mid_outer = [send(after(a, begun), perm=outward) for a in mid_inner]
    side = small_kernel(sum_body, "side", where, in_part, after(from_end, begun, pair))
    end_inner = [send(pair[halves[0]], perm=inner)]
    end_inner.append(send(after(pair[halves[1]], mid_outer[0], side), perm=inner))
    total = small_kernel(sum_body, "total", where, side, send(side, perm=inner))
    sent = send(total.astype(jnp.bfloat16), perm=outward)

    acc, first = add_block(where, 1, [pair], w_down, after(acc, mid_outer[0]), begun, 2 * grad_out.size * w_down.shape[0])
    acc, second = add_block(where, 2, mid_inner + mid_outer, w_down, acc, first, 1000)

    sizes = [256] * (tokens // 256 - 1) + [128, 128]
    arrived, done = [total, total, total], [first, first, second]
    rights = []
    start = 0
    for n, size in enumerate(sizes):
        h, at = divmod(start, tokens // 2)
        ahead = arrived[n + 1] if n < 4 else arrived[n]
        end_outer = send(after(end_inner[h][at : at + size], ahead, done[n]), perm=outward)
        arrived.append(end_outer)
        bring = [*early, late] if n == len(sizes) - 2 else []
        kept, acc, right, *brought = last_block(
            where, end_inner[h], at, end_outer, start, kept, acc, gate_pre, proj_out.T, second, bring
        )
        if bring:
            *early, late = brought
        rights.append(right)
        done.append(right)
        start += size
    return outer_products(where, total, sent, rights), early, late


def any_line(where, inputs, gate_pre, grad_out, w_down, proj_in, proj_out, early, late):
    in_part = jnp.dot(inputs, proj_in, preferred_element_type=jnp.float32)
    in_proj = lax.psum(in_part, "tensor").reshape(-1, LEN, PROJ)
    gathered = lax.all_gather(grad_out, "tensor", axis=1, tiled=True)
    up_grad = (dot_nt(gathered, w_down) * silu(gate_pre.astype(jnp.float32))).astype(jnp.bfloat16)
    out_part = jnp.dot(up_grad, proj_out, preferred_element_type=jnp.float32).reshape(-1, LEN, PROJ)
    grads = jnp.einsum("sti,stj->sij", in_proj, out_part, precision=HIGHEST)
    return grads.reshape(-1, PROJ * PROJ), early, late


def swap(a, axis, bit):
    return lax.ppermute(a, axis, [(i, i ^ bit) for i in range(lax.axis_size(axis))])


def bits(axis):
    return [1 << b for b in range(lax.axis_size(axis).bit_length() - 1)]


def xor_sum(a, axis):
    for bit in bits(axis):
        a = a + swap(a, axis, bit)
    return a


def positions():
    z, me, count = lax.axis_index("tensor"), lax.axis_index("dp"), lax.axis_size("dp")
    low = z < 2
    middle = jnp.logical_and(z > 0, z < 3)
    blocks = [z, z + 1 - 2 * (z % 2), jnp.where(low, 2, 1), jnp.where(low, 3, 0), middle]
    parts = [z * count + (me ^ s) for s in range(count)]
    return jnp.stack([a.astype(jnp.int32) for a in blocks + parts])


def on_device(inputs, gate_pre, grad_out, w_down, proj_in, proj_out, hessian, queries):
    where = positions()
    count = lax.axis_size("dp")
    parts = [queries] + [swap(queries, "dp", s) for s in range(1, count)]
    line = line_of_four if lax.axis_size("tensor") == 4 else any_line
    grads, parts, hessian = line(where, inputs, gate_pre, grad_out, w_down, proj_in, proj_out, parts, hessian)
    grads = xor_sum(grads, "tensor")

    scores = score_parts(where, grads, parts)
    all_grads = after(grads, scores)
    *first, last = bits("tensor")
    for bit in bits("dp"):
        all_grads = jnp.concatenate([all_grads, swap(all_grads, "dp", bit)], axis=0)
    for bit in first:
        scores = score_sum(where, scores, swap(scores, "tensor", bit))
    others = swap(scores, "tensor", last)
    all_grads = after(all_grads, scores)
    row_count = hessian.shape[0]
    if row_count % 128:
        mine = lax.dynamic_slice_in_dim(all_grads, where[FIRST_PART] * row_count, row_count, 1)
        updated = hessian + jnp.dot(mine.T, all_grads, precision=HIGHEST) / all_grads.shape[0]
    else:
        updated = update(where, all_grads, hessian)
    updated, others = lax.optimization_barrier((updated, others))
    return (updated, scores + others)


def solution(mesh):
    return jax.shard_map(
        on_device,
        mesh=mesh,
        in_specs=(
            P(("groups", "dp"), "tensor"),
            P(("groups", "dp"), "tensor"),
            P(("groups", "dp"), "tensor"),
            P("tensor", None),
            P("tensor", None),
            P("tensor", None),
            P(("groups", "tensor", "dp"), None),
            P("groups", ("tensor", "dp")),
        ),
        out_specs=(P(("groups", "tensor", "dp"), None), P(("groups", "dp"), None)),
        check_vma=False,
    )
```

```python
import functools

import jax
import jax.numpy as jnp
from jax import lax
from jax.experimental import pallas as pl
from jax.experimental.pallas import tpu as pltpu
from jax.sharding import PartitionSpec as P

PROJ = 64
LEN = 512
HIGHEST = lax.Precision.HIGHEST
NT = (((1,), (1,)), ((), ()))
TILE = 512
LIMIT = 16
FIRST_PART = 5
ANYWHERE = pl.BlockSpec(memory_space=pl.ANY)
INSIDE = pl.BlockSpec(memory_space=pltpu.VMEM)
OUTSIDE = pl.BlockSpec(memory_space=pltpu.HBM)


def silu(v):
    return 0.5 * v * (1.0 + jnp.tanh(0.5 * v))


def dot(a, b):
    return jnp.dot(a, b, preferred_element_type=jnp.float32)


def dot_nt(a, b):
    return lax.dot_general(a, b, NT, preferred_element_type=jnp.float32)


def placed(a, spec):
    if spec is INSIDE or spec is OUTSIDE:
        return pltpu.with_memory_space_constraint(a, spec.memory_space)
    return a


def call(body, name, where, grid, operands, in_specs, out_specs, out_shapes, scratch, mib, aliases=None, flops=1000):
    return pl.pallas_call(
        body,
        grid_spec=pltpu.PrefetchScalarGridSpec(
            num_scalar_prefetch=1, grid=grid, in_specs=in_specs, out_specs=out_specs, scratch_shapes=scratch
        ),
        out_shape=out_shapes,
        compiler_params=pltpu.CompilerParams(vmem_limit_bytes=mib * 2**20),
        cost_estimate=pl.CostEstimate(flops=flops, bytes_accessed=1000, transcendentals=0),
        name=name,
        input_output_aliases=aliases or {},
    )(where, *[placed(a, spec) for a, spec in zip(operands, in_specs)])


def after(a, *others):
    return lax.optimization_barrier((a, *others))[0]


def fixed(shape):
    return pl.BlockSpec(shape, lambda j, where: (0, 0), pipeline_mode=pl.Buffered(1))


def tile_rows(t, size=TILE):
    return pl.ds(pl.multiple_of(t * size, size), size)


def columns(where, i, width):
    return pl.ds(pl.multiple_of(where[i] * width, width), width)


def input_body(where, inputs, pi_t, in_t):
    in_t[...] = dot_nt(pi_t[...], inputs[...])


def input_block(where, inputs, pi_t):
    shape = (pi_t.shape[0], inputs.shape[0])
    (in_t,) = call(
        input_body,
        "input_block",
        where,
        (1,),
        (inputs, pi_t),
        [fixed(inputs.shape), fixed(pi_t.shape)],
        [pl.BlockSpec(shape, lambda j, where: (0, 0))],
        [jax.ShapeDtypeStruct(shape, jnp.float32)],
        [],
        LIMIT,
    )
    return in_t


def own_body(where, own, w, w_last, acc, kept, token):
    here = tile_rows(pl.program_id(0))
    token[...] = jnp.zeros_like(token)
    kept[:, here] = w_last[...].T
    acc[:, here] = dot_nt(own[...], w[...])


def own_block(where, own, w):
    tokens, feats = own.shape
    hidden = w.shape[0]
    return call(
        own_body,
        "own_block",
        where,
        (hidden // TILE,),
        (own, w, w),
        [
            fixed(own.shape),
            pl.BlockSpec((TILE, feats), lambda j, where: (j, where[0])),
            pl.BlockSpec((TILE, feats), lambda j, where: (j, where[3])),
        ],
        [INSIDE, INSIDE, pl.BlockSpec((8, 128), lambda j, where: (0, 0))],
        [
            pltpu.VMEM((tokens, hidden), jnp.float32),
            pltpu.VMEM((feats, hidden), w.dtype),
            jax.ShapeDtypeStruct((8, 128), jnp.float32),
        ],
        [],
        LIMIT,
    )


def select(where, inner, outer):
    return jnp.where(where[4] == 1, inner[...], outer[...])


def add_body(where, *refs):
    *blocks, w, old, _, acc, token, block = refs
    step = pl.program_id(0)

    @pl.when(step == 0)
    def _():
        token[...] = jnp.zeros_like(token)
        if len(blocks) == 1:
            block[...] = blocks[0][...]
        else:
            half = len(blocks) // 2
            size = blocks[0].shape[0]
            for h in range(half):
                block[h * size : (h + 1) * size, :] = select(where, blocks[h], blocks[half + h])

    here = tile_rows(step)
    acc[:, here] = old[:, here] + dot_nt(block[...], w[...])


def add_block(where, which, blocks, w, old, token, flops):
    tokens, feats = old.shape[0], blocks[0].shape[1]
    return call(
        add_body,
        f"add_block_{which}",
        where,
        (w.shape[0] // TILE,),
        (*blocks, w, old, token),
        [fixed(a.shape) for a in blocks]
        + [pl.BlockSpec((TILE, feats), lambda j, where: (j, where[which])), INSIDE, ANYWHERE],
        [INSIDE, pl.BlockSpec((8, 128), lambda j, where: (0, 0))],
        [pltpu.VMEM(old.shape, old.dtype), jax.ShapeDtypeStruct((8, 128), jnp.float32)],
        [pltpu.VMEM((tokens, feats), blocks[0].dtype)],
        LIMIT,
        aliases={len(blocks) + 2: 0},
        flops=flops,
    )


def last_body(start, inner_at, bring, where, inner, outer, kept, old, gate, po_t, _, *rest):
    count = len(bring)
    far, rest = rest[:count], rest[count:]
    _, _, right, *near = rest[: 3 + count]
    gates, po, gate_sems, po_sem, near_sems = rest[3 + count :]
    size = outer.shape[0]
    hidden = kept.shape[1]
    tokens = pl.ds(start, size)
    spans = [pl.ds(t * TILE, TILE) for t in range(hidden // TILE)]
    po_read = pltpu.make_async_copy(po_t, po, po_sem)
    reads = [
        pltpu.make_async_copy(gate.at[tokens, span], gates.at[t], gate_sems.at[t]) for t, span in enumerate(spans)
    ]
    reads[0].start()
    po_read.start()
    for read in reads[1:]:
        read.start()
    brought = [
        pltpu.make_async_copy(a.at[pl.ds(first, b.shape[0])], b, near_sems.at[i])
        for i, (a, b, first) in enumerate(zip(far, near, bring))
    ]
    for copy in brought:
        copy.start()
    block = select(where, inner.at[pl.ds(inner_at, size)], outer)
    total = jnp.zeros((size, PROJ), jnp.float32)
    for t, span in enumerate(spans):
        hidden_grad = old[tokens, span] + dot(block, kept[:, span])
        reads[t].wait()
        up_grad = (hidden_grad * silu(gates[t].astype(jnp.float32))).astype(jnp.bfloat16)
        if t == 0:
            po_read.wait()
        total = total + dot_nt(up_grad, po[:, span])
    right[...] = total
    for copy in brought:
        copy.wait()


def last_block(where, inner, inner_at, outer, start, kept, old, gate, po_t, token, bring):
    size = outer.shape[0]
    tiles = kept.shape[1] // TILE
    return call(
        functools.partial(last_body, start, inner_at, [first for _, first, _ in bring]),
        "last_block",
        where,
        (1,),
        (inner, outer, kept, old, gate, po_t, token, *[a for a, _, _ in bring]),
        [INSIDE, INSIDE, INSIDE, INSIDE, OUTSIDE, ANYWHERE, ANYWHERE] + [OUTSIDE] * len(bring),
        [INSIDE] * (3 + len(bring)),
        [
            pltpu.VMEM(kept.shape, kept.dtype),
            pltpu.VMEM(old.shape, old.dtype),
            pltpu.VMEM((size, PROJ), jnp.float32),
            *[pltpu.VMEM((rows, a.shape[1]), a.dtype) for a, _, rows in bring],
        ],
        [
            pltpu.VMEM((tiles, size, TILE), gate.dtype),
            pltpu.VMEM(po_t.shape, po_t.dtype),
            pltpu.SemaphoreType.DMA((tiles,)),
            pltpu.SemaphoreType.DMA,
            pltpu.SemaphoreType.DMA((max(len(bring), 1),)),
        ],
        LIMIT,
        aliases={3: 0, 4: 1},
    )


def final_body(start, inner_at, where, inner, outer, kept, old, gate, po, right):
    size = outer.shape[0]
    block = select(where, inner.at[pl.ds(inner_at, size)], outer)
    total = jnp.zeros((size, PROJ), jnp.float32)
    for t in range(kept.shape[1] // TILE):
        span = pl.ds(t * TILE, TILE)
        hidden_grad = old[pl.ds(start, size), span] + dot(block, kept[:, span])
        up_grad = (hidden_grad * silu(gate[:, span].astype(jnp.float32))).astype(jnp.bfloat16)
        total = total + dot_nt(up_grad, po[:, span])
    right[...] = total


def final_block(where, inner, inner_at, outer, start, kept, old, gate, po):
    (right,) = call(
        functools.partial(final_body, start, inner_at),
        "final_block",
        where,
        (1,),
        (inner, outer, kept, old, gate, po),
        [INSIDE] * 6,
        [INSIDE],
        [pltpu.VMEM((outer.shape[0], PROJ), jnp.float32)],
        [],
        LIMIT,
    )
    return right


def outer_body(where, total, sent, *refs):
    *rights, grads, wide = refs
    left_t = jnp.where(where[4] == 1, total[...], sent[...].astype(jnp.float32))
    wide[...] = jnp.zeros_like(wide)
    start = 0
    terms = [None] * grads.shape[0]
    for right in rights:
        size = right.shape[0]
        s = start // LEN
        term = jnp.dot(
            left_t[:, start : start + size], right[...], precision=HIGHEST, preferred_element_type=jnp.float32
        )
        terms[s] = term if terms[s] is None else terms[s] + term
        start += size
    for s, term in enumerate(terms):
        wide[:, :PROJ] = term
        even = wide[pl.ds(0, PROJ // 2, stride=2), :]
        odd = wide[pl.ds(1, PROJ // 2, stride=2), :]
        rows = even + pltpu.roll(odd, PROJ, 1)
        for i in range(PROJ // 2):
            grads[s : s + 1, i * 2 * PROJ : (i + 1) * 2 * PROJ] = rows[i : i + 1, :]


def outer_products(where, total, sent, rights):
    shape = (total.shape[1] // LEN, PROJ * PROJ)
    (grads,) = call(
        outer_body,
        "outer_products",
        where,
        (1,),
        (total, sent, *rights),
        [INSIDE] * (2 + len(rights)),
        [INSIDE],
        [pltpu.VMEM(shape, jnp.float32)],
        [pltpu.VMEM((PROJ, 2 * PROJ), jnp.float32)],
        LIMIT,
    )
    return grads


def small_kernel(body, name, where, *operands):
    (out,) = call(
        body,
        name,
        where,
        (1,),
        operands,
        [fixed(a.shape) for a in operands],
        [pl.BlockSpec(operands[0].shape, lambda j, where: (0, 0))],
        [jax.ShapeDtypeStruct(operands[0].shape, operands[0].dtype)],
        [],
        LIMIT,
    )
    return out


def score_sum(where, a, b):
    out = pltpu.VMEM(a.shape, a.dtype)
    (total,) = call(
        sum_body, "score_sum", where, (1,), (a, b), [INSIDE, INSIDE], [INSIDE], [out], [], LIMIT, flops=3 * 10**9
    )
    return total


def sum_body(where, a, b, out):
    out[...] = a[...] + b[...]


def score_body(where, grads, *rest):
    *parts, out = rest
    rows, width = parts[0].shape
    count = grads.shape[0]
    lane = lax.broadcasted_iota(jnp.int32, (rows, 128), 1)
    total = jnp.zeros((rows, 128), jnp.float32)
    for s in range(count):
        products = None
        for p, part in enumerate(parts):
            term = part[...] * grads[s : s + 1, columns(where, FIRST_PART + p, width)]
            products = term if products is None else products + term
        total = jnp.where(lane == s, jnp.sum(products, axis=1, keepdims=True), total)
    out[...] = total.T[:count, :]


def score_parts(where, grads, parts):
    width = parts[0].shape[1]
    shape = (grads.shape[0], parts[0].shape[0])
    if width % 128:
        slices = [
            lax.dynamic_slice_in_dim(grads, where[FIRST_PART + p] * width, width, 1) for p in range(len(parts))
        ]
        return jnp.dot(jnp.concatenate(slices, axis=1), jnp.concatenate(parts, axis=1).T, precision=HIGHEST)
    (scores,) = call(
        score_body,
        "scores",
        where,
        (1,),
        (grads, *parts),
        [INSIDE] * (1 + len(parts)),
        [pl.BlockSpec(shape, lambda j, where: (0, 0))],
        [jax.ShapeDtypeStruct(shape, jnp.float32)],
        [],
        LIMIT,
    )
    return scores


def pieces(a):
    high = a.astype(jnp.bfloat16)
    rest = a - high.astype(jnp.float32)
    middle = rest.astype(jnp.bfloat16)
    low = (rest - middle.astype(jnp.float32)).astype(jnp.bfloat16)
    return high, middle, low


def update_body(scale, where, grads, hessian, out, new, out_sems):
    parts, _, width = new.shape
    high, middle, low = pieces(grads[:, columns(where, FIRST_PART, new.shape[1])])
    left = jnp.concatenate([high, high, middle, middle, high, low], axis=0).T
    writes = []
    for t in range(parts):
        span = pl.ds(t * width, width)
        high, middle, low = pieces(grads[:, span])
        right = jnp.concatenate([high, middle, high, middle, low, high], axis=0)
        new[t] = hessian[:, span] + dot(left, right) * scale
        writes.append(pltpu.make_async_copy(new.at[t], out.at[:, span], out_sems.at[t]))
        writes[t].start()
    for write in writes:
        write.wait()


def update(where, grads, hessian):
    rows, length = hessian.shape
    count = grads.shape[0]
    parts = 8
    width = length // parts
    (updated,) = call(
        functools.partial(update_body, 1.0 / count),
        "hessian_update",
        where,
        (1,),
        (grads, hessian),
        [INSIDE, INSIDE],
        [ANYWHERE],
        [jax.ShapeDtypeStruct((rows, length), jnp.float32)],
        [pltpu.VMEM((parts, rows, width), jnp.float32), pltpu.SemaphoreType.DMA((parts,))],
        LIMIT,
        flops=1000,
    )
    return updated


def line_of_four(where, inputs, gate_pre, grad_out, w_down, proj_in, proj_out, early, late):
    send = functools.partial(lax.ppermute, axis_name="tensor")
    pairs = [(0, 1), (1, 0), (2, 3), (3, 2)]
    inner = [(1, 2), (2, 1)]
    outward = [(1, 0), (2, 3)]
    inward = [(0, 1), (3, 2)]
    tokens = grad_out.shape[0]
    halves = [slice(0, tokens // 2), slice(tokens // 2, tokens)]
    pair = send(grad_out, perm=pairs)
    own = [grad_out[half] for half in halves]
    mid_inner = [send(a, perm=inner) for a in own]
    in_part = input_block(where, inputs, proj_in.T)
    from_end = send(after(in_part, mid_inner[0]), perm=inward)
    acc, kept, begun = own_block(where, after(grad_out, in_part, *early), w_down)
    mid_outer = [send(after(a, begun), perm=outward) for a in mid_inner]
    side = small_kernel(sum_body, "side", where, in_part, after(from_end, begun, pair))
    end_inner = [send(pair[halves[0]], perm=inner)]
    end_inner.append(send(after(pair[halves[1]], mid_outer[0], side), perm=inner))
    total = small_kernel(sum_body, "total", where, side, send(side, perm=inner))
    sent = send(total.astype(jnp.bfloat16), perm=outward)

    acc, first = add_block(where, 1, [pair], w_down, after(acc, mid_outer[0]), begun, 2 * grad_out.size * w_down.shape[0])
    acc, second = add_block(where, 2, mid_inner + mid_outer, w_down, acc, first, 1000)

    sizes = [256] * (tokens // 256 - 1) + [128, 128]
    arrived, done = [total, total, total], [first, first, second]
    rights = []
    start = 0
    for n, size in enumerate(sizes):
        h, at = divmod(start, tokens // 2)
        ahead = arrived[n + 1] if n < 4 else arrived[n]
        end_outer = send(after(end_inner[h][at : at + size], ahead, done[n]), perm=outward)
        arrived.append(end_outer)
        if n == len(sizes) - 1:
            rights.append(final_block(where, end_inner[h], at, end_outer, start, kept, acc, gate_near, po_near))
            break
        bring = []
        if n == len(sizes) - 2:
            bring = [(a, 0, a.shape[0]) for a in (*early, late, proj_out.T)]
            bring.append((gate_pre, start + size, tokens - start - size))
        kept, acc, right, *brought = last_block(
            where, end_inner[h], at, end_outer, start, kept, acc, gate_pre, proj_out.T, second, bring
        )
        if bring:
            *early, late, po_near, gate_near = brought
        rights.append(right)
        done.append(right)
        start += size
    return outer_products(where, total, sent, rights), early, late


def any_line(where, inputs, gate_pre, grad_out, w_down, proj_in, proj_out, early, late):
    in_part = jnp.dot(inputs, proj_in, preferred_element_type=jnp.float32)
    in_proj = lax.psum(in_part, "tensor").reshape(-1, LEN, PROJ)
    gathered = lax.all_gather(grad_out, "tensor", axis=1, tiled=True)
    up_grad = (dot_nt(gathered, w_down) * silu(gate_pre.astype(jnp.float32))).astype(jnp.bfloat16)
    out_part = jnp.dot(up_grad, proj_out, preferred_element_type=jnp.float32).reshape(-1, LEN, PROJ)
    grads = jnp.einsum("sti,stj->sij", in_proj, out_part, precision=HIGHEST)
    return grads.reshape(-1, PROJ * PROJ), early, late


def swap(a, axis, bit):
    return lax.ppermute(a, axis, [(i, i ^ bit) for i in range(lax.axis_size(axis))])


def bits(axis):
    return [1 << b for b in range(lax.axis_size(axis).bit_length() - 1)]


def xor_sum(a, axis):
    for bit in bits(axis):
        a = a + swap(a, axis, bit)
    return a


def positions():
    z, me, count = lax.axis_index("tensor"), lax.axis_index("dp"), lax.axis_size("dp")
    low = z < 2
    middle = jnp.logical_and(z > 0, z < 3)
    blocks = [z, z + 1 - 2 * (z % 2), jnp.where(low, 2, 1), jnp.where(low, 3, 0), middle]
    parts = [z * count + (me ^ s) for s in range(count)]
    return jnp.stack([a.astype(jnp.int32) for a in blocks + parts])


def on_device(inputs, gate_pre, grad_out, w_down, proj_in, proj_out, hessian, queries):
    where = positions()
    count = lax.axis_size("dp")
    parts = [queries] + [swap(queries, "dp", s) for s in range(1, count)]
    line = line_of_four if lax.axis_size("tensor") == 4 else any_line
    grads, parts, hessian = line(where, inputs, gate_pre, grad_out, w_down, proj_in, proj_out, parts, hessian)
    grads = xor_sum(grads, "tensor")

    scores = score_parts(where, grads, parts)
    all_grads = after(grads, scores)
    *first, last = bits("tensor")
    for bit in bits("dp"):
        all_grads = jnp.concatenate([all_grads, swap(all_grads, "dp", bit)], axis=0)
    for bit in first:
        scores = score_sum(where, scores, swap(scores, "tensor", bit))
    others = swap(scores, "tensor", last)
    all_grads = after(all_grads, scores)
    row_count = hessian.shape[0]
    if row_count % 128:
        mine = lax.dynamic_slice_in_dim(all_grads, where[FIRST_PART] * row_count, row_count, 1)
        updated = hessian + jnp.dot(mine.T, all_grads, precision=HIGHEST) / all_grads.shape[0]
    else:
        updated = update(where, all_grads, hessian)
    updated, others = lax.optimization_barrier((updated, others))
    return (updated, scores + others)


def solution(mesh):
    return jax.shard_map(
        on_device,
        mesh=mesh,
        in_specs=(
            P(("groups", "dp"), "tensor"),
            P(("groups", "dp"), "tensor"),
            P(("groups", "dp"), "tensor"),
            P("tensor", None),
            P("tensor", None),
            P("tensor", None),
            P(("groups", "tensor", "dp"), None),
            P("groups", ("tensor", "dp")),
        ),
        out_specs=(P(("groups", "tensor", "dp"), None), P(("groups", "dp"), None)),
        check_vma=False,
    )
```

```python
import functools

import jax
import jax.numpy as jnp
from jax import lax
from jax.experimental import pallas as pl
from jax.experimental.pallas import tpu as pltpu
from jax.sharding import PartitionSpec as P

PROJ = 64
LEN = 512
HIGHEST = lax.Precision.HIGHEST
NT = (((1,), (1,)), ((), ()))
TILE = 512
LIMIT = 16
FIRST_PART = 5
ANYWHERE = pl.BlockSpec(memory_space=pl.ANY)
INSIDE = pl.BlockSpec(memory_space=pltpu.VMEM)
OUTSIDE = pl.BlockSpec(memory_space=pltpu.HBM)


def silu(v):
    return 0.5 * v * (1.0 + jnp.tanh(0.5 * v))


def dot(a, b):
    return jnp.dot(a, b, preferred_element_type=jnp.float32)


def dot_nt(a, b):
    return lax.dot_general(a, b, NT, preferred_element_type=jnp.float32)


def placed(a, spec):
    if spec is INSIDE or spec is OUTSIDE:
        return pltpu.with_memory_space_constraint(a, spec.memory_space)
    return a


def call(body, name, where, grid, operands, in_specs, out_specs, out_shapes, scratch, mib, aliases=None, flops=1000):
    return pl.pallas_call(
        body,
        grid_spec=pltpu.PrefetchScalarGridSpec(
            num_scalar_prefetch=1, grid=grid, in_specs=in_specs, out_specs=out_specs, scratch_shapes=scratch
        ),
        out_shape=out_shapes,
        compiler_params=pltpu.CompilerParams(vmem_limit_bytes=mib * 2**20),
        cost_estimate=pl.CostEstimate(flops=flops, bytes_accessed=1000, transcendentals=0),
        name=name,
        input_output_aliases=aliases or {},
    )(where, *[placed(a, spec) for a, spec in zip(operands, in_specs)])


def after(a, *others):
    return lax.optimization_barrier((a, *others))[0]


def fixed(shape):
    return pl.BlockSpec(shape, lambda j, where: (0, 0), pipeline_mode=pl.Buffered(1))


def tile_rows(t, size=TILE):
    return pl.ds(pl.multiple_of(t * size, size), size)


def columns(where, i, width):
    return pl.ds(pl.multiple_of(where[i] * width, width), width)


def input_body(where, inputs, pi_t, in_t):
    in_t[...] = dot_nt(pi_t[...], inputs[...])


def input_block(where, inputs, pi_t):
    shape = (pi_t.shape[0], inputs.shape[0])
    (in_t,) = call(
        input_body,
        "input_block",
        where,
        (1,),
        (inputs, pi_t),
        [fixed(inputs.shape), fixed(pi_t.shape)],
        [pl.BlockSpec(shape, lambda j, where: (0, 0))],
        [jax.ShapeDtypeStruct(shape, jnp.float32)],
        [],
        LIMIT,
    )
    return in_t


def own_body(where, own, w, w_last, acc, kept, token):
    here = tile_rows(pl.program_id(0))
    token[...] = jnp.zeros_like(token)
    kept[:, here] = w_last[...].T
    acc[:, here] = dot_nt(own[...], w[...])


def own_block(where, own, w):
    tokens, feats = own.shape
    hidden = w.shape[0]
    return call(
        own_body,
        "own_block",
        where,
        (hidden // TILE,),
        (own, w, w),
        [
            fixed(own.shape),
            pl.BlockSpec((TILE, feats), lambda j, where: (j, where[0])),
            pl.BlockSpec((TILE, feats), lambda j, where: (j, where[3])),
        ],
        [INSIDE, INSIDE, pl.BlockSpec((8, 128), lambda j, where: (0, 0))],
        [
            pltpu.VMEM((tokens, hidden), jnp.float32),
            pltpu.VMEM((feats, hidden), w.dtype),
            jax.ShapeDtypeStruct((8, 128), jnp.float32),
        ],
        [],
        LIMIT,
    )


def select(where, inner, outer):
    return jnp.where(where[4] == 1, inner[...], outer[...])


def add_body(where, *refs):
    *blocks, w, old, _, acc, token, block = refs
    step = pl.program_id(0)

    @pl.when(step == 0)
    def _():
        token[...] = jnp.zeros_like(token)
        if len(blocks) == 1:
            block[...] = blocks[0][...]
        else:
            half = len(blocks) // 2
            size = blocks[0].shape[0]
            for h in range(half):
                block[h * size : (h + 1) * size, :] = select(where, blocks[h], blocks[half + h])

    here = tile_rows(step)
    acc[:, here] = old[:, here] + dot_nt(block[...], w[...])


def add_block(where, which, blocks, w, old, token, flops):
    tokens, feats = old.shape[0], blocks[0].shape[1]
    return call(
        add_body,
        f"add_block_{which}",
        where,
        (w.shape[0] // TILE,),
        (*blocks, w, old, token),
        [fixed(a.shape) for a in blocks]
        + [pl.BlockSpec((TILE, feats), lambda j, where: (j, where[which])), INSIDE, ANYWHERE],
        [INSIDE, pl.BlockSpec((8, 128), lambda j, where: (0, 0))],
        [pltpu.VMEM(old.shape, old.dtype), jax.ShapeDtypeStruct((8, 128), jnp.float32)],
        [pltpu.VMEM((tokens, feats), blocks[0].dtype)],
        LIMIT,
        aliases={len(blocks) + 2: 0},
        flops=flops,
    )


def last_body(start, inner_at, bring, where, inner, outer, kept, old, gate, po_t, _, *rest):
    count = len(bring)
    far, rest = rest[:count], rest[count:]
    _, _, right, *near = rest[: 3 + count]
    gates, po, gate_sems, po_sem, near_sems = rest[3 + count :]
    size = outer.shape[0]
    hidden = kept.shape[1]
    tokens = pl.ds(start, size)
    spans = [pl.ds(t * TILE, TILE) for t in range(hidden // TILE)]
    po_read = pltpu.make_async_copy(po_t, po, po_sem)
    reads = [
        pltpu.make_async_copy(gate.at[tokens, span], gates.at[t], gate_sems.at[t]) for t, span in enumerate(spans)
    ]
    reads[0].start()
    po_read.start()
    for read in reads[1:]:
        read.start()
    brought = [
        pltpu.make_async_copy(a.at[pl.ds(first, b.shape[0])], b, near_sems.at[i])
        for i, (a, b, first) in enumerate(zip(far, near, bring))
    ]
    for copy in brought:
        copy.start()
    block = select(where, inner.at[pl.ds(inner_at, size)], outer)
    total = jnp.zeros((size, PROJ), jnp.float32)
    for t, span in enumerate(spans):
        hidden_grad = old[tokens, span] + dot(block, kept[:, span])
        reads[t].wait()
        up_grad = (hidden_grad * silu(gates[t].astype(jnp.float32))).astype(jnp.bfloat16)
        if t == 0:
            po_read.wait()
        total = total + dot_nt(up_grad, po[:, span])
    right[...] = total
    for copy in brought:
        copy.wait()


def last_block(where, inner, inner_at, outer, start, kept, old, gate, po_t, token, bring):
    size = outer.shape[0]
    tiles = kept.shape[1] // TILE
    return call(
        functools.partial(last_body, start, inner_at, [first for _, first, _ in bring]),
        "last_block",
        where,
        (1,),
        (inner, outer, kept, old, gate, po_t, token, *[a for a, _, _ in bring]),
        [INSIDE, INSIDE, INSIDE, INSIDE, OUTSIDE, ANYWHERE, ANYWHERE] + [OUTSIDE] * len(bring),
        [INSIDE] * (3 + len(bring)),
        [
            pltpu.VMEM(kept.shape, kept.dtype),
            pltpu.VMEM(old.shape, old.dtype),
            pltpu.VMEM((size, PROJ), jnp.float32),
            *[pltpu.VMEM((rows, a.shape[1]), a.dtype) for a, _, rows in bring],
        ],
        [
            pltpu.VMEM((tiles, size, TILE), gate.dtype),
            pltpu.VMEM(po_t.shape, po_t.dtype),
            pltpu.SemaphoreType.DMA((tiles,)),
            pltpu.SemaphoreType.DMA,
            pltpu.SemaphoreType.DMA((max(len(bring), 1),)),
        ],
        LIMIT,
        aliases={3: 0, 4: 1},
    )


def near_body(start, inner_at, bring, where, inner, outer, kept, old, gate, po, *rest):
    far, rest = rest[: len(bring)], rest[len(bring) :]
    _, _, right, *near = rest[: 3 + len(bring)]
    near_sems = rest[-1]
    size = outer.shape[0]
    brought = [
        pltpu.make_async_copy(a.at[pl.ds(first, b.shape[0])], b, near_sems.at[i])
        for i, (a, b, first) in enumerate(zip(far, near, bring))
    ]
    for copy in brought:
        copy.start()
    block = select(where, inner.at[pl.ds(inner_at, size)], outer)
    total = jnp.zeros((size, PROJ), jnp.float32)
    for t in range(kept.shape[1] // TILE):
        span = pl.ds(t * TILE, TILE)
        hidden_grad = old[pl.ds(start, size), span] + dot(block, kept[:, span])
        up_grad = (hidden_grad * silu(gate[:, span].astype(jnp.float32))).astype(jnp.bfloat16)
        total = total + dot_nt(up_grad, po[:, span])
    right[...] = total
    for copy in brought:
        copy.wait()


def near_block(where, inner, inner_at, outer, start, kept, old, gate, po, bring):
    return call(
        functools.partial(near_body, start, inner_at, [first for _, first, _ in bring]),
        "near_block",
        where,
        (1,),
        (inner, outer, kept, old, gate, po, *[a for a, _, _ in bring]),
        [INSIDE] * 6 + [OUTSIDE] * len(bring),
        [INSIDE] * (3 + len(bring)),
        [
            pltpu.VMEM(kept.shape, kept.dtype),
            pltpu.VMEM(old.shape, old.dtype),
            pltpu.VMEM((outer.shape[0], PROJ), jnp.float32),
            *[pltpu.VMEM((rows, a.shape[1]), a.dtype) for a, _, rows in bring],
        ],
        [pltpu.SemaphoreType.DMA((max(len(bring), 1),))],
        LIMIT,
        aliases={3: 0, 4: 1},
    )


def outer_body(where, total, sent, *refs):
    *rights, grads, wide = refs
    left_t = jnp.where(where[4] == 1, total[...], sent[...].astype(jnp.float32))
    wide[...] = jnp.zeros_like(wide)
    start = 0
    terms = [None] * grads.shape[0]
    for right in rights:
        size = right.shape[0]
        s = start // LEN
        term = jnp.dot(
            left_t[:, start : start + size], right[...], precision=HIGHEST, preferred_element_type=jnp.float32
        )
        terms[s] = term if terms[s] is None else terms[s] + term
        start += size
    for s, term in enumerate(terms):
        wide[:, :PROJ] = term
        even = wide[pl.ds(0, PROJ // 2, stride=2), :]
        odd = wide[pl.ds(1, PROJ // 2, stride=2), :]
        rows = even + pltpu.roll(odd, PROJ, 1)
        for i in range(PROJ // 2):
            grads[s : s + 1, i * 2 * PROJ : (i + 1) * 2 * PROJ] = rows[i : i + 1, :]


def outer_products(where, total, sent, rights):
    shape = (total.shape[1] // LEN, PROJ * PROJ)
    (grads,) = call(
        outer_body,
        "outer_products",
        where,
        (1,),
        (total, sent, *rights),
        [INSIDE] * (2 + len(rights)),
        [INSIDE],
        [pltpu.VMEM(shape, jnp.float32)],
        [pltpu.VMEM((PROJ, 2 * PROJ), jnp.float32)],
        LIMIT,
    )
    return grads


def small_kernel(body, name, where, *operands):
    (out,) = call(
        body,
        name,
        where,
        (1,),
        operands,
        [fixed(a.shape) for a in operands],
        [pl.BlockSpec(operands[0].shape, lambda j, where: (0, 0))],
        [jax.ShapeDtypeStruct(operands[0].shape, operands[0].dtype)],
        [],
        LIMIT,
    )
    return out


def score_sum(where, a, b):
    out = pltpu.VMEM(a.shape, a.dtype)
    (total,) = call(
        sum_body, "score_sum", where, (1,), (a, b), [INSIDE, INSIDE], [INSIDE], [out], [], LIMIT, flops=3 * 10**9
    )
    return total


def sum_body(where, a, b, out):
    out[...] = a[...] + b[...]


def score_body(where, grads, *rest):
    *parts, out = rest
    rows, width = parts[0].shape
    count = grads.shape[0]
    lane = lax.broadcasted_iota(jnp.int32, (rows, 128), 1)
    total = jnp.zeros((rows, 128), jnp.float32)
    for s in range(count):
        products = None
        for p, part in enumerate(parts):
            term = part[...] * grads[s : s + 1, columns(where, FIRST_PART + p, width)]
            products = term if products is None else products + term
        total = jnp.where(lane == s, jnp.sum(products, axis=1, keepdims=True), total)
    out[...] = total.T[:count, :]


def score_parts(where, grads, parts):
    width = parts[0].shape[1]
    shape = (grads.shape[0], parts[0].shape[0])
    if width % 128:
        slices = [
            lax.dynamic_slice_in_dim(grads, where[FIRST_PART + p] * width, width, 1) for p in range(len(parts))
        ]
        return jnp.dot(jnp.concatenate(slices, axis=1), jnp.concatenate(parts, axis=1).T, precision=HIGHEST)
    (scores,) = call(
        score_body,
        "scores",
        where,
        (1,),
        (grads, *parts),
        [INSIDE] * (1 + len(parts)),
        [pl.BlockSpec(shape, lambda j, where: (0, 0))],
        [jax.ShapeDtypeStruct(shape, jnp.float32)],
        [],
        LIMIT,
    )
    return scores


def pieces(a):
    high = a.astype(jnp.bfloat16)
    rest = a - high.astype(jnp.float32)
    middle = rest.astype(jnp.bfloat16)
    low = (rest - middle.astype(jnp.float32)).astype(jnp.bfloat16)
    return high, middle, low


def update_body(scale, where, grads, hessian, out, new, out_sems):
    parts, _, width = new.shape
    high, middle, low = pieces(grads[:, columns(where, FIRST_PART, new.shape[1])])
    left = jnp.concatenate([high, high, middle, middle, high, low], axis=0).T
    writes = []
    for t in range(parts):
        span = pl.ds(t * width, width)
        high, middle, low = pieces(grads[:, span])
        right = jnp.concatenate([high, middle, high, middle, low, high], axis=0)
        new[t] = hessian[:, span] + dot(left, right) * scale
        writes.append(pltpu.make_async_copy(new.at[t], out.at[:, span], out_sems.at[t]))
        writes[t].start()
    for write in writes:
        write.wait()


def update(where, grads, hessian):
    rows, length = hessian.shape
    count = grads.shape[0]
    parts = 8
    width = length // parts
    (updated,) = call(
        functools.partial(update_body, 1.0 / count),
        "hessian_update",
        where,
        (1,),
        (grads, hessian),
        [INSIDE, INSIDE],
        [ANYWHERE],
        [jax.ShapeDtypeStruct((rows, length), jnp.float32)],
        [pltpu.VMEM((parts, rows, width), jnp.float32), pltpu.SemaphoreType.DMA((parts,))],
        LIMIT,
        flops=1000,
    )
    return updated


def line_of_four(where, inputs, gate_pre, grad_out, w_down, proj_in, proj_out, early, late):
    send = functools.partial(lax.ppermute, axis_name="tensor")
    pairs = [(0, 1), (1, 0), (2, 3), (3, 2)]
    inner = [(1, 2), (2, 1)]
    outward = [(1, 0), (2, 3)]
    inward = [(0, 1), (3, 2)]
    tokens = grad_out.shape[0]
    halves = [slice(0, tokens // 2), slice(tokens // 2, tokens)]
    pair = send(grad_out, perm=pairs)
    own = [grad_out[half] for half in halves]
    mid_inner = [send(a, perm=inner) for a in own]
    in_part = input_block(where, inputs, proj_in.T)
    from_end = send(after(in_part, mid_inner[0]), perm=inward)
    acc, kept, begun = own_block(where, after(grad_out, in_part, *early), w_down)
    mid_outer = [send(after(a, begun), perm=outward) for a in mid_inner]
    side = small_kernel(sum_body, "side", where, in_part, after(from_end, begun, pair))
    end_inner = [send(pair[halves[0]], perm=inner)]
    end_inner.append(send(after(pair[halves[1]], mid_outer[0], side), perm=inner))
    total = small_kernel(sum_body, "total", where, side, send(side, perm=inner))
    sent = send(total.astype(jnp.bfloat16), perm=outward)

    acc, first = add_block(where, 1, [pair], w_down, after(acc, mid_outer[0]), begun, 2 * grad_out.size * w_down.shape[0])
    acc, second = add_block(where, 2, mid_inner + mid_outer, w_down, acc, first, 1000)

    sizes = [256] * (tokens // 256 - 1) + [128, 128]
    arrived, done = [total, total, total], [first, first, second]
    rights = []
    start = 0
    for n, size in enumerate(sizes):
        h, at = divmod(start, tokens // 2)
        ahead = arrived[n + 1] if n < 4 else arrived[n]
        end_outer = send(after(end_inner[h][at : at + size], ahead, done[n]), perm=outward)
        arrived.append(end_outer)
        bring = []
        if n + 1 < len(sizes):
            bring.append((gate_pre, start + size, sizes[n + 1]))
        if n == 0:
            bring.append((proj_out.T, 0, PROJ))
        if n == len(sizes) - 3:
            bring += [(a, 0, a.shape[0]) for a in (*early, late)]
        place = where, end_inner[h], at, end_outer, start, kept, acc
        if n == 0:
            kept, acc, right, *brought = last_block(*place, gate_pre, proj_out.T, second, bring)
            po_near = brought[1]
        else:
            kept, acc, right, *brought = near_block(*place, gate_near, po_near, bring)
        if n == len(sizes) - 3:
            *early, late = brought[1:]
        if bring:
            gate_near = brought[0]
        rights.append(right)
        done.append(right)
        start += size
    return outer_products(where, total, sent, rights), early, late


def any_line(where, inputs, gate_pre, grad_out, w_down, proj_in, proj_out, early, late):
    in_part = jnp.dot(inputs, proj_in, preferred_element_type=jnp.float32)
    in_proj = lax.psum(in_part, "tensor").reshape(-1, LEN, PROJ)
    gathered = lax.all_gather(grad_out, "tensor", axis=1, tiled=True)
    up_grad = (dot_nt(gathered, w_down) * silu(gate_pre.astype(jnp.float32))).astype(jnp.bfloat16)
    out_part = jnp.dot(up_grad, proj_out, preferred_element_type=jnp.float32).reshape(-1, LEN, PROJ)
    grads = jnp.einsum("sti,stj->sij", in_proj, out_part, precision=HIGHEST)
    return grads.reshape(-1, PROJ * PROJ), early, late


def swap(a, axis, bit):
    return lax.ppermute(a, axis, [(i, i ^ bit) for i in range(lax.axis_size(axis))])


def bits(axis):
    return [1 << b for b in range(lax.axis_size(axis).bit_length() - 1)]


def xor_sum(a, axis):
    for bit in bits(axis):
        a = a + swap(a, axis, bit)
    return a


def positions():
    z, me, count = lax.axis_index("tensor"), lax.axis_index("dp"), lax.axis_size("dp")
    low = z < 2
    middle = jnp.logical_and(z > 0, z < 3)
    blocks = [z, z + 1 - 2 * (z % 2), jnp.where(low, 2, 1), jnp.where(low, 3, 0), middle]
    parts = [z * count + (me ^ s) for s in range(count)]
    return jnp.stack([a.astype(jnp.int32) for a in blocks + parts])


def on_device(inputs, gate_pre, grad_out, w_down, proj_in, proj_out, hessian, queries):
    where = positions()
    count = lax.axis_size("dp")
    parts = [queries] + [swap(queries, "dp", s) for s in range(1, count)]
    line = line_of_four if lax.axis_size("tensor") == 4 else any_line
    grads, parts, hessian = line(where, inputs, gate_pre, grad_out, w_down, proj_in, proj_out, parts, hessian)
    grads = xor_sum(grads, "tensor")

    scores = score_parts(where, grads, parts)
    all_grads = after(grads, scores)
    *first, last = bits("tensor")
    for bit in bits("dp"):
        all_grads = jnp.concatenate([all_grads, swap(all_grads, "dp", bit)], axis=0)
    for bit in first:
        scores = score_sum(where, scores, swap(scores, "tensor", bit))
    others = swap(scores, "tensor", last)
    all_grads = after(all_grads, scores)
    row_count = hessian.shape[0]
    if row_count % 128:
        mine = lax.dynamic_slice_in_dim(all_grads, where[FIRST_PART] * row_count, row_count, 1)
        updated = hessian + jnp.dot(mine.T, all_grads, precision=HIGHEST) / all_grads.shape[0]
    else:
        updated = update(where, all_grads, hessian)
    updated, others = lax.optimization_barrier((updated, others))
    return (updated, scores + others)


def solution(mesh):
    return jax.shard_map(
        on_device,
        mesh=mesh,
        in_specs=(
            P(("groups", "dp"), "tensor"),
            P(("groups", "dp"), "tensor"),
            P(("groups", "dp"), "tensor"),
            P("tensor", None),
            P("tensor", None),
            P("tensor", None),
            P(("groups", "tensor", "dp"), None),
            P("groups", ("tensor", "dp")),
        ),
        out_specs=(P(("groups", "tensor", "dp"), None), P(("groups", "dp"), None)),
        check_vma=False,
    )
```

```python
import functools

import jax
import jax.numpy as jnp
from jax import lax
from jax.experimental import pallas as pl
from jax.experimental.pallas import tpu as pltpu
from jax.sharding import PartitionSpec as P

PROJ = 64
LEN = 512
HIGHEST = lax.Precision.HIGHEST
NT = (((1,), (1,)), ((), ()))
TILE = 512
LIMIT = 16
FIRST_PART = 5
ANYWHERE = pl.BlockSpec(memory_space=pl.ANY)
INSIDE = pl.BlockSpec(memory_space=pltpu.VMEM)
OUTSIDE = pl.BlockSpec(memory_space=pltpu.HBM)


def silu(v):
    return 0.5 * v * (1.0 + jnp.tanh(0.5 * v))


def dot(a, b):
    return jnp.dot(a, b, preferred_element_type=jnp.float32)


def dot_nt(a, b):
    return lax.dot_general(a, b, NT, preferred_element_type=jnp.float32)


def placed(a, spec):
    if spec is INSIDE or spec is OUTSIDE:
        return pltpu.with_memory_space_constraint(a, spec.memory_space)
    return a


def call(body, name, where, grid, operands, in_specs, out_specs, out_shapes, scratch, mib, aliases=None, flops=1000):
    scalars = [] if where is None else [where]
    return pl.pallas_call(
        body,
        grid_spec=pltpu.PrefetchScalarGridSpec(
            num_scalar_prefetch=len(scalars), grid=grid, in_specs=in_specs, out_specs=out_specs, scratch_shapes=scratch
        ),
        out_shape=out_shapes,
        compiler_params=pltpu.CompilerParams(vmem_limit_bytes=mib * 2**20),
        cost_estimate=pl.CostEstimate(flops=flops, bytes_accessed=1000, transcendentals=0),
        name=name,
        input_output_aliases=aliases or {},
    )(*scalars, *[placed(a, spec) for a, spec in zip(operands, in_specs)])


def after(a, *others):
    return lax.optimization_barrier((a, *others))[0]


def fixed(shape):
    return pl.BlockSpec(shape, lambda j, where: (0, 0), pipeline_mode=pl.Buffered(1))


def tile_rows(t, size=TILE):
    return pl.ds(pl.multiple_of(t * size, size), size)


def columns(where, i, width):
    return pl.ds(pl.multiple_of(where[i] * width, width), width)


def input_body(where, inputs, pi_t, in_t):
    in_t[...] = dot_nt(pi_t[...], inputs[...])


def input_block(where, inputs, pi_t):
    shape = (pi_t.shape[0], inputs.shape[0])
    (in_t,) = call(
        input_body,
        "input_block",
        where,
        (1,),
        (inputs, pi_t),
        [fixed(inputs.shape), fixed(pi_t.shape)],
        [pl.BlockSpec(shape, lambda j, where: (0, 0))],
        [jax.ShapeDtypeStruct(shape, jnp.float32)],
        [],
        LIMIT,
    )
    return in_t


def own_body(where, own, w, w_last, acc, kept, token):
    here = tile_rows(pl.program_id(0))
    token[...] = jnp.zeros_like(token)
    kept[:, here] = w_last[...].T
    acc[:, here] = dot_nt(own[...], w[...])


def own_block(where, own, w):
    tokens, feats = own.shape
    hidden = w.shape[0]
    return call(
        own_body,
        "own_block",
        where,
        (hidden // TILE,),
        (own, w, w),
        [
            fixed(own.shape),
            pl.BlockSpec((TILE, feats), lambda j, where: (j, where[0])),
            pl.BlockSpec((TILE, feats), lambda j, where: (j, where[3])),
        ],
        [INSIDE, INSIDE, pl.BlockSpec((8, 128), lambda j, where: (0, 0))],
        [
            pltpu.VMEM((tokens, hidden), jnp.float32),
            pltpu.VMEM((feats, hidden), w.dtype),
            jax.ShapeDtypeStruct((8, 128), jnp.float32),
        ],
        [],
        LIMIT,
    )


def select(where, inner, outer):
    return jnp.where(where[4] == 1, inner[...], outer[...])


def add_body(where, *refs):
    *blocks, w, old, _, acc, token, block = refs
    step = pl.program_id(0)

    @pl.when(step == 0)
    def _():
        token[...] = jnp.zeros_like(token)
        if len(blocks) == 1:
            block[...] = blocks[0][...]
        else:
            half = len(blocks) // 2
            size = blocks[0].shape[0]
            for h in range(half):
                block[h * size : (h + 1) * size, :] = select(where, blocks[h], blocks[half + h])

    here = tile_rows(step)
    acc[:, here] = old[:, here] + dot_nt(block[...], w[...])


def add_block(where, which, blocks, w, old, token, flops):
    tokens, feats = old.shape[0], blocks[0].shape[1]
    return call(
        add_body,
        f"add_block_{which}",
        where,
        (w.shape[0] // TILE,),
        (*blocks, w, old, token),
        [fixed(a.shape) for a in blocks]
        + [pl.BlockSpec((TILE, feats), lambda j, where: (j, where[which])), INSIDE, ANYWHERE],
        [INSIDE, pl.BlockSpec((8, 128), lambda j, where: (0, 0))],
        [pltpu.VMEM(old.shape, old.dtype), jax.ShapeDtypeStruct((8, 128), jnp.float32)],
        [pltpu.VMEM((tokens, feats), blocks[0].dtype)],
        LIMIT,
        aliases={len(blocks) + 2: 0},
        flops=flops,
    )


def last_body(start, inner_at, bring, inner, outer, kept, old, gate, po_t, _, *rest):
    count = len(bring)
    far, rest = rest[:count], rest[count:]
    _, _, right, *near = rest[: 3 + count]
    gates, po, gate_sems, po_sem, near_sems = rest[3 + count :]
    size = outer.shape[0]
    hidden = kept.shape[1]
    tokens = pl.ds(start, size)
    spans = [pl.ds(t * TILE, TILE) for t in range(hidden // TILE)]
    po_read = pltpu.make_async_copy(po_t, po, po_sem)
    reads = [
        pltpu.make_async_copy(gate.at[tokens, span], gates.at[t], gate_sems.at[t]) for t, span in enumerate(spans)
    ]
    reads[0].start()
    po_read.start()
    for read in reads[1:]:
        read.start()
    brought = [
        pltpu.make_async_copy(a.at[pl.ds(first, b.shape[0])], b, near_sems.at[i])
        for i, (a, b, first) in enumerate(zip(far, near, bring))
    ]
    for copy in brought:
        copy.start()
    block = inner[pl.ds(inner_at, size), :] + outer[...]
    total = jnp.zeros((size, PROJ), jnp.float32)
    for t, span in enumerate(spans):
        hidden_grad = old[tokens, span] + dot(block, kept[:, span])
        reads[t].wait()
        up_grad = (hidden_grad * silu(gates[t].astype(jnp.float32))).astype(jnp.bfloat16)
        if t == 0:
            po_read.wait()
        total = total + dot_nt(up_grad, po[:, span])
    right[...] = total
    for copy in brought:
        copy.wait()


def last_block(inner, inner_at, outer, start, kept, old, gate, po_t, token, bring):
    size = outer.shape[0]
    tiles = kept.shape[1] // TILE
    return call(
        functools.partial(last_body, start, inner_at, [first for _, first, _ in bring]),
        "last_block",
        None,
        (1,),
        (inner, outer, kept, old, gate, po_t, token, *[a for a, _, _ in bring]),
        [INSIDE, INSIDE, INSIDE, INSIDE, OUTSIDE, ANYWHERE, ANYWHERE] + [OUTSIDE] * len(bring),
        [INSIDE] * (3 + len(bring)),
        [
            pltpu.VMEM(kept.shape, kept.dtype),
            pltpu.VMEM(old.shape, old.dtype),
            pltpu.VMEM((size, PROJ), jnp.float32),
            *[pltpu.VMEM((rows, a.shape[1]), a.dtype) for a, _, rows in bring],
        ],
        [
            pltpu.VMEM((tiles, size, TILE), gate.dtype),
            pltpu.VMEM(po_t.shape, po_t.dtype),
            pltpu.SemaphoreType.DMA((tiles,)),
            pltpu.SemaphoreType.DMA,
            pltpu.SemaphoreType.DMA((max(len(bring), 1),)),
        ],
        LIMIT,
        aliases={2: 0, 3: 1},
    )


def near_body(start, inner_at, bring, inner, outer, kept, old, gate, po, *rest):
    far, rest = rest[: len(bring)], rest[len(bring) :]
    _, _, right, *near = rest[: 3 + len(bring)]
    near_sems = rest[-1]
    size = outer.shape[0]
    brought = [
        pltpu.make_async_copy(a.at[pl.ds(first, b.shape[0])], b, near_sems.at[i])
        for i, (a, b, first) in enumerate(zip(far, near, bring))
    ]
    for copy in brought:
        copy.start()
    block = inner[pl.ds(inner_at, size), :] + outer[...]
    total = jnp.zeros((size, PROJ), jnp.float32)
    for t in range(kept.shape[1] // TILE):
        span = pl.ds(t * TILE, TILE)
        hidden_grad = old[pl.ds(start, size), span] + dot(block, kept[:, span])
        up_grad = (hidden_grad * silu(gate[:, span].astype(jnp.float32))).astype(jnp.bfloat16)
        total = total + dot_nt(up_grad, po[:, span])
    right[...] = total
    for copy in brought:
        copy.wait()


def near_block(inner, inner_at, outer, start, kept, old, gate, po, bring):
    return call(
        functools.partial(near_body, start, inner_at, [first for _, first, _ in bring]),
        "near_block",
        None,
        (1,),
        (inner, outer, kept, old, gate, po, *[a for a, _, _ in bring]),
        [INSIDE] * 6 + [OUTSIDE] * len(bring),
        [INSIDE] * (3 + len(bring)),
        [
            pltpu.VMEM(kept.shape, kept.dtype),
            pltpu.VMEM(old.shape, old.dtype),
            pltpu.VMEM((outer.shape[0], PROJ), jnp.float32),
            *[pltpu.VMEM((rows, a.shape[1]), a.dtype) for a, _, rows in bring],
        ],
        [pltpu.SemaphoreType.DMA((max(len(bring), 1),))],
        LIMIT,
        aliases={2: 0, 3: 1},
    )


def outer_body(masked, sent, *refs):
    *rights, grads, wide = refs
    left_t = masked[...] + sent[...].astype(jnp.float32)
    wide[...] = jnp.zeros_like(wide)
    start = 0
    terms = [None] * grads.shape[0]
    for right in rights:
        size = right.shape[0]
        s = start // LEN
        term = jnp.dot(
            left_t[:, start : start + size], right[...], precision=HIGHEST, preferred_element_type=jnp.float32
        )
        terms[s] = term if terms[s] is None else terms[s] + term
        start += size
    for s, term in enumerate(terms):
        wide[:, :PROJ] = term
        even = wide[pl.ds(0, PROJ // 2, stride=2), :]
        odd = wide[pl.ds(1, PROJ // 2, stride=2), :]
        rows = even + pltpu.roll(odd, PROJ, 1)
        for i in range(PROJ // 2):
            grads[s : s + 1, i * 2 * PROJ : (i + 1) * 2 * PROJ] = rows[i : i + 1, :]


def outer_products(masked, sent, rights):
    shape = (masked.shape[1] // LEN, PROJ * PROJ)
    (grads,) = call(
        outer_body,
        "outer_products",
        None,
        (1,),
        (masked, sent, *rights),
        [INSIDE] * (2 + len(rights)),
        [INSIDE],
        [pltpu.VMEM(shape, jnp.float32)],
        [pltpu.VMEM((PROJ, 2 * PROJ), jnp.float32)],
        LIMIT,
    )
    return grads


def small_kernel(body, name, where, *operands):
    (out,) = call(
        body,
        name,
        where,
        (1,),
        operands,
        [fixed(a.shape) for a in operands],
        [pl.BlockSpec(operands[0].shape, lambda j, where: (0, 0))],
        [jax.ShapeDtypeStruct(operands[0].shape, operands[0].dtype)],
        [],
        LIMIT,
    )
    return out


def score_sum(a, b):
    out = pltpu.VMEM(a.shape, a.dtype)
    (total,) = call(
        sum_body, "score_sum", None, (1,), (a, b), [INSIDE, INSIDE], [INSIDE], [out], [], LIMIT, flops=3 * 10**9
    )
    return total


def sum_body(*refs):
    a, b, out = refs[-3:]
    out[...] = a[...] + b[...]


def mask_body(where, a, out):
    out[...] = jnp.where(where[4] == 1, a[...], 0.0)


def score_body(where, grads, *rest):
    *parts, out = rest
    rows, width = parts[0].shape
    count = grads.shape[0]
    lane = lax.broadcasted_iota(jnp.int32, (rows, 128), 1)
    total = jnp.zeros((rows, 128), jnp.float32)
    for s in range(count):
        products = None
        for p, part in enumerate(parts):
            term = part[...] * grads[s : s + 1, columns(where, FIRST_PART + p, width)]
            products = term if products is None else products + term
        total = jnp.where(lane == s, jnp.sum(products, axis=1, keepdims=True), total)
    out[...] = total.T[:count, :]


def score_parts(where, grads, parts):
    width = parts[0].shape[1]
    shape = (grads.shape[0], parts[0].shape[0])
    if width % 128:
        slices = [
            lax.dynamic_slice_in_dim(grads, where[FIRST_PART + p] * width, width, 1) for p in range(len(parts))
        ]
        return jnp.dot(jnp.concatenate(slices, axis=1), jnp.concatenate(parts, axis=1).T, precision=HIGHEST)
    (scores,) = call(
        score_body,
        "scores",
        where,
        (1,),
        (grads, *parts),
        [INSIDE] * (1 + len(parts)),
        [pl.BlockSpec(shape, lambda j, where: (0, 0))],
        [jax.ShapeDtypeStruct(shape, jnp.float32)],
        [],
        LIMIT,
    )
    return scores


def pieces(a):
    high = a.astype(jnp.bfloat16)
    rest = a - high.astype(jnp.float32)
    middle = rest.astype(jnp.bfloat16)
    low = (rest - middle.astype(jnp.float32)).astype(jnp.bfloat16)
    return high, middle, low


def update_body(scale, where, grads, hessian, out, new, out_sems):
    parts, _, width = new.shape
    high, middle, low = pieces(grads[:, columns(where, FIRST_PART, new.shape[1])])
    left = jnp.concatenate([high, high, middle, middle, high, low], axis=0).T
    writes = []
    for t in range(parts):
        span = pl.ds(t * width, width)
        high, middle, low = pieces(grads[:, span])
        right = jnp.concatenate([high, middle, high, middle, low, high], axis=0)
        new[t] = hessian[:, span] + dot(left, right) * scale
        writes.append(pltpu.make_async_copy(new.at[t], out.at[:, span], out_sems.at[t]))
        writes[t].start()
    for write in writes:
        write.wait()


def update(where, grads, hessian):
    rows, length = hessian.shape
    count = grads.shape[0]
    parts = 8
    width = length // parts
    (updated,) = call(
        functools.partial(update_body, 1.0 / count),
        "hessian_update",
        where,
        (1,),
        (grads, hessian),
        [INSIDE, INSIDE],
        [ANYWHERE],
        [jax.ShapeDtypeStruct((rows, length), jnp.float32)],
        [pltpu.VMEM((parts, rows, width), jnp.float32), pltpu.SemaphoreType.DMA((parts,))],
        LIMIT,
        flops=1000,
    )
    return updated


def line_of_four(where, inputs, gate_pre, grad_out, w_down, proj_in, proj_out, early, late):
    send = functools.partial(lax.ppermute, axis_name="tensor")
    pairs = [(0, 1), (1, 0), (2, 3), (3, 2)]
    inner = [(1, 2), (2, 1)]
    outward = [(1, 0), (2, 3)]
    inward = [(0, 1), (3, 2)]
    tokens = grad_out.shape[0]
    halves = [slice(0, tokens // 2), slice(tokens // 2, tokens)]
    pair = send(grad_out, perm=pairs)
    own = [grad_out[half] for half in halves]
    mid_inner = [send(a, perm=inner) for a in own]
    in_part = input_block(where, inputs, proj_in.T)
    from_end = send(after(in_part, mid_inner[0]), perm=inward)
    acc, kept, begun = own_block(where, after(grad_out, in_part, *early), w_down)
    mid_outer = [send(after(a, begun), perm=outward) for a in mid_inner]
    side = small_kernel(sum_body, "side", where, in_part, after(from_end, begun, pair))
    end_inner = [send(pair[halves[0]], perm=inner)]
    end_inner.append(send(after(pair[halves[1]], mid_outer[0], side), perm=inner))
    total = small_kernel(sum_body, "total", where, side, send(side, perm=inner))
    masked = small_kernel(mask_body, "masked", where, total)
    sent = send(total.astype(jnp.bfloat16), perm=outward)

    acc, first = add_block(where, 1, [pair], w_down, after(acc, mid_outer[0]), begun, 2 * grad_out.size * w_down.shape[0])
    acc, second = add_block(where, 2, mid_inner + mid_outer, w_down, acc, first, 1000)

    sizes = [256] * (tokens // 256 - 1) + [128, 128]
    arrived, done = [total, total, total], [first, first, second]
    rights = []
    start = 0
    for n, size in enumerate(sizes):
        h, at = divmod(start, tokens // 2)
        ahead = arrived[n + 1] if n < 4 else arrived[n]
        end_outer = send(after(end_inner[h][at : at + size], ahead, done[n]), perm=outward)
        arrived.append(end_outer)
        bring = []
        if n + 1 < len(sizes):
            bring.append((gate_pre, start + size, sizes[n + 1]))
        if n == 0:
            bring.append((proj_out.T, 0, PROJ))
        if n == len(sizes) - 3:
            bring += [(a, 0, a.shape[0]) for a in (*early, late)]
        place = end_inner[h], at, end_outer, start, kept, acc
        if n == 0:
            kept, acc, right, *brought = last_block(*place, gate_pre, proj_out.T, second, bring)
            po_near = brought[1]
        else:
            kept, acc, right, *brought = near_block(*place, gate_near, po_near, bring)
        if n == len(sizes) - 3:
            *early, late = brought[1:]
        if bring:
            gate_near = brought[0]
        rights.append(right)
        done.append(right)
        start += size
    return outer_products(masked, sent, rights), early, late


def any_line(where, inputs, gate_pre, grad_out, w_down, proj_in, proj_out, early, late):
    in_part = jnp.dot(inputs, proj_in, preferred_element_type=jnp.float32)
    in_proj = lax.psum(in_part, "tensor").reshape(-1, LEN, PROJ)
    gathered = lax.all_gather(grad_out, "tensor", axis=1, tiled=True)
    up_grad = (dot_nt(gathered, w_down) * silu(gate_pre.astype(jnp.float32))).astype(jnp.bfloat16)
    out_part = jnp.dot(up_grad, proj_out, preferred_element_type=jnp.float32).reshape(-1, LEN, PROJ)
    grads = jnp.einsum("sti,stj->sij", in_proj, out_part, precision=HIGHEST)
    return grads.reshape(-1, PROJ * PROJ), early, late


def swap(a, axis, bit):
    return lax.ppermute(a, axis, [(i, i ^ bit) for i in range(lax.axis_size(axis))])


def bits(axis):
    return [1 << b for b in range(lax.axis_size(axis).bit_length() - 1)]


def xor_sum(a, axis):
    for bit in bits(axis):
        a = a + swap(a, axis, bit)
    return a


def positions():
    z, me, count = lax.axis_index("tensor"), lax.axis_index("dp"), lax.axis_size("dp")
    low = z < 2
    middle = jnp.logical_and(z > 0, z < 3)
    blocks = [z, z + 1 - 2 * (z % 2), jnp.where(low, 2, 1), jnp.where(low, 3, 0), middle]
    parts = [z * count + (me ^ s) for s in range(count)]
    return jnp.stack([a.astype(jnp.int32) for a in blocks + parts])


def on_device(inputs, gate_pre, grad_out, w_down, proj_in, proj_out, hessian, queries):
    where = positions()
    count = lax.axis_size("dp")
    parts = [queries] + [swap(queries, "dp", s) for s in range(1, count)]
    line = line_of_four if lax.axis_size("tensor") == 4 else any_line
    grads, parts, hessian = line(where, inputs, gate_pre, grad_out, w_down, proj_in, proj_out, parts, hessian)
    grads = xor_sum(grads, "tensor")

    scores = score_parts(where, grads, parts)
    all_grads = after(grads, scores)
    *first, last = bits("tensor")
    for bit in bits("dp"):
        all_grads = jnp.concatenate([all_grads, swap(all_grads, "dp", bit)], axis=0)
    for bit in first:
        scores = score_sum(scores, swap(scores, "tensor", bit))
    others = swap(scores, "tensor", last)
    all_grads = after(all_grads, scores)
    row_count = hessian.shape[0]
    if row_count % 128:
        mine = lax.dynamic_slice_in_dim(all_grads, where[FIRST_PART] * row_count, row_count, 1)
        updated = hessian + jnp.dot(mine.T, all_grads, precision=HIGHEST) / all_grads.shape[0]
    else:
        updated = update(where, all_grads, hessian)
    updated, others = lax.optimization_barrier((updated, others))
    return (updated, scores + others)


def solution(mesh):
    return jax.shard_map(
        on_device,
        mesh=mesh,
        in_specs=(
            P(("groups", "dp"), "tensor"),
            P(("groups", "dp"), "tensor"),
            P(("groups", "dp"), "tensor"),
            P("tensor", None),
            P("tensor", None),
            P("tensor", None),
            P(("groups", "tensor", "dp"), None),
            P("groups", ("tensor", "dp")),
        ),
        out_specs=(P(("groups", "tensor", "dp"), None), P(("groups", "dp"), None)),
        check_vma=False,
    )
```

```python
import functools

import jax
import jax.numpy as jnp
from jax import lax
from jax.experimental import pallas as pl
from jax.experimental.pallas import tpu as pltpu
from jax.sharding import PartitionSpec as P

PROJ = 64
LEN = 512
HIGHEST = lax.Precision.HIGHEST
NT = (((1,), (1,)), ((), ()))
TILE = 512
LIMIT = 16
FIRST_PART = 5
ANYWHERE = pl.BlockSpec(memory_space=pl.ANY)
INSIDE = pl.BlockSpec(memory_space=pltpu.VMEM)
OUTSIDE = pl.BlockSpec(memory_space=pltpu.HBM)


def silu(v):
    return 0.5 * v * (1.0 + jnp.tanh(0.5 * v))


def dot(a, b):
    return jnp.dot(a, b, preferred_element_type=jnp.float32)


def dot_nt(a, b):
    return lax.dot_general(a, b, NT, preferred_element_type=jnp.float32)


def placed(a, spec):
    if spec is INSIDE or spec is OUTSIDE:
        return pltpu.with_memory_space_constraint(a, spec.memory_space)
    return a


def call(body, name, where, grid, operands, in_specs, out_specs, out_shapes, scratch, mib, aliases=None, flops=1000):
    scalars = [] if where is None else [where]
    return pl.pallas_call(
        body,
        grid_spec=pltpu.PrefetchScalarGridSpec(
            num_scalar_prefetch=len(scalars), grid=grid, in_specs=in_specs, out_specs=out_specs, scratch_shapes=scratch
        ),
        out_shape=out_shapes,
        compiler_params=pltpu.CompilerParams(vmem_limit_bytes=mib * 2**20),
        cost_estimate=pl.CostEstimate(flops=flops, bytes_accessed=1000, transcendentals=0),
        name=name,
        input_output_aliases=aliases or {},
    )(*scalars, *[placed(a, spec) for a, spec in zip(operands, in_specs)])


def after(a, *others):
    return lax.optimization_barrier((a, *others))[0]


def fixed(shape):
    return pl.BlockSpec(shape, lambda j, where: (0, 0), pipeline_mode=pl.Buffered(1))


def my_part(p, width):
    at = lax.axis_index("tensor") * lax.axis_size("dp") + (lax.axis_index("dp") ^ p)
    return pl.ds(pl.multiple_of(at * width, width), width)


def tile_rows(t, size=TILE):
    return pl.ds(pl.multiple_of(t * size, size), size)


def columns(where, i, width):
    return pl.ds(pl.multiple_of(where[i] * width, width), width)


def input_body(where, inputs, pi_t, in_t):
    in_t[...] = dot_nt(pi_t[...], inputs[...])


def input_block(where, inputs, pi_t):
    shape = (pi_t.shape[0], inputs.shape[0])
    (in_t,) = call(
        input_body,
        "input_block",
        where,
        (1,),
        (inputs, pi_t),
        [fixed(inputs.shape), fixed(pi_t.shape)],
        [pl.BlockSpec(shape, lambda j, where: (0, 0))],
        [jax.ShapeDtypeStruct(shape, jnp.float32)],
        [],
        LIMIT,
    )
    return in_t


def own_body(where, own, w, w_last, acc, kept, token):
    here = tile_rows(pl.program_id(0))
    token[...] = jnp.zeros_like(token)
    kept[:, here] = w_last[...].T
    acc[:, here] = dot_nt(own[...], w[...])


def own_block(where, own, w):
    tokens, feats = own.shape
    hidden = w.shape[0]
    return call(
        own_body,
        "own_block",
        where,
        (hidden // TILE,),
        (own, w, w),
        [
            fixed(own.shape),
            pl.BlockSpec((TILE, feats), lambda j, where: (j, where[0])),
            pl.BlockSpec((TILE, feats), lambda j, where: (j, where[3])),
        ],
        [INSIDE, INSIDE, pl.BlockSpec((8, 128), lambda j, where: (0, 0))],
        [
            pltpu.VMEM((tokens, hidden), jnp.float32),
            pltpu.VMEM((feats, hidden), w.dtype),
            jax.ShapeDtypeStruct((8, 128), jnp.float32),
        ],
        [],
        LIMIT,
    )


def select(where, inner, outer):
    return jnp.where(where[4] == 1, inner[...], outer[...])


def add_body(where, *refs):
    *blocks, w, old, _, acc, token, block = refs
    step = pl.program_id(0)

    @pl.when(step == 0)
    def _():
        token[...] = jnp.zeros_like(token)
        if len(blocks) == 1:
            block[...] = blocks[0][...]
        else:
            half = len(blocks) // 2
            size = blocks[0].shape[0]
            for h in range(half):
                block[h * size : (h + 1) * size, :] = select(where, blocks[h], blocks[half + h])

    here = tile_rows(step)
    acc[:, here] = old[:, here] + dot_nt(block[...], w[...])


def add_block(where, which, blocks, w, old, token, flops):
    tokens, feats = old.shape[0], blocks[0].shape[1]
    return call(
        add_body,
        f"add_block_{which}",
        where,
        (w.shape[0] // TILE,),
        (*blocks, w, old, token),
        [fixed(a.shape) for a in blocks]
        + [pl.BlockSpec((TILE, feats), lambda j, where: (j, where[which])), INSIDE, ANYWHERE],
        [INSIDE, pl.BlockSpec((8, 128), lambda j, where: (0, 0))],
        [pltpu.VMEM(old.shape, old.dtype), jax.ShapeDtypeStruct((8, 128), jnp.float32)],
        [pltpu.VMEM((tokens, feats), blocks[0].dtype)],
        LIMIT,
        aliases={len(blocks) + 2: 0},
        flops=flops,
    )


def last_body(start, inner_at, bring, inner, outer, kept, old, gate, po_t, _, *rest):
    count = len(bring)
    far, rest = rest[:count], rest[count:]
    _, _, right, *near = rest[: 3 + count]
    gates, po, gate_sems, po_sem, near_sems = rest[3 + count :]
    size = outer.shape[0]
    hidden = kept.shape[1]
    tokens = pl.ds(start, size)
    spans = [pl.ds(t * TILE, TILE) for t in range(hidden // TILE)]
    po_read = pltpu.make_async_copy(po_t, po, po_sem)
    reads = [
        pltpu.make_async_copy(gate.at[tokens, span], gates.at[t], gate_sems.at[t]) for t, span in enumerate(spans)
    ]
    reads[0].start()
    po_read.start()
    for read in reads[1:]:
        read.start()
    brought = [
        pltpu.make_async_copy(a.at[pl.ds(first, b.shape[0])], b, near_sems.at[i])
        for i, (a, b, first) in enumerate(zip(far, near, bring))
    ]
    for copy in brought:
        copy.start()
    block = inner[pl.ds(inner_at, size), :] + outer[...]
    total = jnp.zeros((size, PROJ), jnp.float32)
    for t, span in enumerate(spans):
        hidden_grad = old[tokens, span] + dot(block, kept[:, span])
        reads[t].wait()
        up_grad = (hidden_grad * silu(gates[t].astype(jnp.float32))).astype(jnp.bfloat16)
        if t == 0:
            po_read.wait()
        total = total + dot_nt(up_grad, po[:, span])
    right[...] = total
    for copy in brought:
        copy.wait()


def last_block(inner, inner_at, outer, start, kept, old, gate, po_t, token, bring):
    size = outer.shape[0]
    tiles = kept.shape[1] // TILE
    return call(
        functools.partial(last_body, start, inner_at, [first for _, first, _ in bring]),
        "last_block",
        None,
        (1,),
        (inner, outer, kept, old, gate, po_t, token, *[a for a, _, _ in bring]),
        [INSIDE, INSIDE, INSIDE, INSIDE, OUTSIDE, ANYWHERE, ANYWHERE] + [OUTSIDE] * len(bring),
        [INSIDE] * (3 + len(bring)),
        [
            pltpu.VMEM(kept.shape, kept.dtype),
            pltpu.VMEM(old.shape, old.dtype),
            pltpu.VMEM((size, PROJ), jnp.float32),
            *[pltpu.VMEM((rows, a.shape[1]), a.dtype) for a, _, rows in bring],
        ],
        [
            pltpu.VMEM((tiles, size, TILE), gate.dtype),
            pltpu.VMEM(po_t.shape, po_t.dtype),
            pltpu.SemaphoreType.DMA((tiles,)),
            pltpu.SemaphoreType.DMA,
            pltpu.SemaphoreType.DMA((max(len(bring), 1),)),
        ],
        LIMIT,
        aliases={2: 0, 3: 1},
    )


def near_body(start, inner_at, bring, inner, outer, kept, old, gate, po, *rest):
    far, rest = rest[: len(bring)], rest[len(bring) :]
    _, _, right, *near = rest[: 3 + len(bring)]
    near_sems = rest[-1]
    size = outer.shape[0]
    brought = [
        pltpu.make_async_copy(a.at[pl.ds(first, b.shape[0])], b, near_sems.at[i])
        for i, (a, b, first) in enumerate(zip(far, near, bring))
    ]
    for copy in brought:
        copy.start()
    block = inner[pl.ds(inner_at, size), :] + outer[...]
    total = jnp.zeros((size, PROJ), jnp.float32)
    for t in range(kept.shape[1] // TILE):
        span = pl.ds(t * TILE, TILE)
        hidden_grad = old[pl.ds(start, size), span] + dot(block, kept[:, span])
        up_grad = (hidden_grad * silu(gate[:, span].astype(jnp.float32))).astype(jnp.bfloat16)
        total = total + dot_nt(up_grad, po[:, span])
    right[...] = total
    for copy in brought:
        copy.wait()


def near_block(inner, inner_at, outer, start, kept, old, gate, po, bring):
    return call(
        functools.partial(near_body, start, inner_at, [first for _, first, _ in bring]),
        "near_block",
        None,
        (1,),
        (inner, outer, kept, old, gate, po, *[a for a, _, _ in bring]),
        [INSIDE] * 6 + [OUTSIDE] * len(bring),
        [INSIDE] * (3 + len(bring)),
        [
            pltpu.VMEM(kept.shape, kept.dtype),
            pltpu.VMEM(old.shape, old.dtype),
            pltpu.VMEM((outer.shape[0], PROJ), jnp.float32),
            *[pltpu.VMEM((rows, a.shape[1]), a.dtype) for a, _, rows in bring],
        ],
        [pltpu.SemaphoreType.DMA((max(len(bring), 1),))],
        LIMIT,
        aliases={2: 0, 3: 1},
    )


def outer_body(masked, sent, *refs):
    *rights, grads, wide = refs
    left_t = masked[...] + sent[...].astype(jnp.float32)
    wide[...] = jnp.zeros_like(wide)
    start = 0
    terms = [None] * grads.shape[0]
    for right in rights:
        size = right.shape[0]
        s = start // LEN
        term = jnp.dot(
            left_t[:, start : start + size], right[...], precision=HIGHEST, preferred_element_type=jnp.float32
        )
        terms[s] = term if terms[s] is None else terms[s] + term
        start += size
    for s, term in enumerate(terms):
        wide[:, :PROJ] = term
        even = wide[pl.ds(0, PROJ // 2, stride=2), :]
        odd = wide[pl.ds(1, PROJ // 2, stride=2), :]
        rows = even + pltpu.roll(odd, PROJ, 1)
        for i in range(PROJ // 2):
            grads[s : s + 1, i * 2 * PROJ : (i + 1) * 2 * PROJ] = rows[i : i + 1, :]


def outer_products(masked, sent, rights):
    shape = (masked.shape[1] // LEN, PROJ * PROJ)
    (grads,) = call(
        outer_body,
        "outer_products",
        None,
        (1,),
        (masked, sent, *rights),
        [INSIDE] * (2 + len(rights)),
        [INSIDE],
        [pltpu.VMEM(shape, jnp.float32)],
        [pltpu.VMEM((PROJ, 2 * PROJ), jnp.float32)],
        LIMIT,
    )
    return grads


def small_kernel(body, name, where, *operands):
    (out,) = call(
        body,
        name,
        where,
        (1,),
        operands,
        [fixed(a.shape) for a in operands],
        [pl.BlockSpec(operands[0].shape, lambda j, where: (0, 0))],
        [jax.ShapeDtypeStruct(operands[0].shape, operands[0].dtype)],
        [],
        LIMIT,
    )
    return out


def score_sum(a, b):
    out = pltpu.VMEM(a.shape, a.dtype)
    (total,) = call(
        sum_body, "score_sum", None, (1,), (a, b), [INSIDE, INSIDE], [INSIDE], [out], [], LIMIT, flops=3 * 10**9
    )
    return total


def sum_body(*refs):
    a, b, out = refs[-3:]
    out[...] = a[...] + b[...]


def mask_body(where, a, out):
    out[...] = jnp.where(where[4] == 1, a[...], 0.0)


def score_body(grads, *rest):
    *parts, out = rest
    rows, width = parts[0].shape
    count = grads.shape[0]
    lane = lax.broadcasted_iota(jnp.int32, (rows, 128), 1)
    total = jnp.zeros((rows, 128), jnp.float32)
    for s in range(count):
        products = None
        for p, part in enumerate(parts):
            term = part[...] * grads[s : s + 1, my_part(p, width)]
            products = term if products is None else products + term
        total = jnp.where(lane == s, jnp.sum(products, axis=1, keepdims=True), total)
    out[...] = total.T[:count, :]


def score_parts(where, grads, parts):
    width = parts[0].shape[1]
    shape = (grads.shape[0], parts[0].shape[0])
    if width % 128:
        slices = [
            lax.dynamic_slice_in_dim(grads, where[FIRST_PART + p] * width, width, 1) for p in range(len(parts))
        ]
        return jnp.dot(jnp.concatenate(slices, axis=1), jnp.concatenate(parts, axis=1).T, precision=HIGHEST)
    (scores,) = call(
        score_body,
        "scores",
        None,
        (1,),
        (grads, *parts),
        [INSIDE] * (1 + len(parts)),
        [pl.BlockSpec(shape, lambda j: (0, 0))],
        [jax.ShapeDtypeStruct(shape, jnp.float32)],
        [],
        LIMIT,
    )
    return scores


def pieces(a):
    high = a.astype(jnp.bfloat16)
    rest = a - high.astype(jnp.float32)
    middle = rest.astype(jnp.bfloat16)
    low = (rest - middle.astype(jnp.float32)).astype(jnp.bfloat16)
    return high, middle, low


def update_body(scale, grads, hessian, out, new, out_sems):
    parts, _, width = new.shape
    high, middle, low = pieces(grads[:, my_part(0, new.shape[1])])
    left = jnp.concatenate([high, high, middle, middle, high, low], axis=0).T
    writes = []
    for t in range(parts):
        span = pl.ds(t * width, width)
        high, middle, low = pieces(grads[:, span])
        right = jnp.concatenate([high, middle, high, middle, low, high], axis=0)
        new[t] = hessian[:, span] + dot(left, right) * scale
        writes.append(pltpu.make_async_copy(new.at[t], out.at[:, span], out_sems.at[t]))
        writes[t].start()
    for write in writes:
        write.wait()


def update(grads, hessian):
    rows, length = hessian.shape
    count = grads.shape[0]
    parts = 8
    width = length // parts
    (updated,) = call(
        functools.partial(update_body, 1.0 / count),
        "hessian_update",
        None,
        (1,),
        (grads, hessian),
        [INSIDE, INSIDE],
        [ANYWHERE],
        [jax.ShapeDtypeStruct((rows, length), jnp.float32)],
        [pltpu.VMEM((parts, rows, width), jnp.float32), pltpu.SemaphoreType.DMA((parts,))],
        LIMIT,
        flops=1000,
    )
    return updated


def line_of_four(where, inputs, gate_pre, grad_out, w_down, proj_in, proj_out, early, late):
    send = functools.partial(lax.ppermute, axis_name="tensor")
    pairs = [(0, 1), (1, 0), (2, 3), (3, 2)]
    inner = [(1, 2), (2, 1)]
    outward = [(1, 0), (2, 3)]
    inward = [(0, 1), (3, 2)]
    tokens = grad_out.shape[0]
    halves = [slice(0, tokens // 2), slice(tokens // 2, tokens)]
    pair = send(grad_out, perm=pairs)
    own = [grad_out[half] for half in halves]
    mid_inner = [send(a, perm=inner) for a in own]
    in_part = input_block(where, inputs, proj_in.T)
    from_end = send(after(in_part, mid_inner[0]), perm=inward)
    acc, kept, begun = own_block(where, after(grad_out, in_part, *early), w_down)
    mid_outer = [send(after(a, begun), perm=outward) for a in mid_inner]
    side = small_kernel(sum_body, "side", where, in_part, after(from_end, begun, pair))
    end_inner = [send(pair[halves[0]], perm=inner)]
    end_inner.append(send(after(pair[halves[1]], mid_outer[0], side), perm=inner))
    total = small_kernel(sum_body, "total", where, side, send(side, perm=inner))
    masked = small_kernel(mask_body, "masked", where, total)
    sent = send(total.astype(jnp.bfloat16), perm=outward)

    acc, first = add_block(where, 1, [pair], w_down, after(acc, mid_outer[0]), begun, 2 * grad_out.size * w_down.shape[0])
    acc, second = add_block(where, 2, mid_inner + mid_outer, w_down, acc, first, 1000)

    sizes = [256] * (tokens // 256 - 1) + [128, 128]
    arrived, done = [total, total, total], [first, first, second]
    rights = []
    start = 0
    for n, size in enumerate(sizes):
        h, at = divmod(start, tokens // 2)
        ahead = arrived[n + 1] if n < 4 else arrived[n]
        end_outer = send(after(end_inner[h][at : at + size], ahead, done[n]), perm=outward)
        arrived.append(end_outer)
        bring = []
        if n + 1 < len(sizes):
            bring.append((gate_pre, start + size, sizes[n + 1]))
        if n == 0:
            bring.append((proj_out.T, 0, PROJ))
        if n == len(sizes) - 3:
            bring += [(a, 0, a.shape[0]) for a in (*early, late)]
        place = end_inner[h], at, end_outer, start, kept, acc
        if n == 0:
            kept, acc, right, *brought = last_block(*place, gate_pre, proj_out.T, second, bring)
            po_near = brought[1]
        else:
            kept, acc, right, *brought = near_block(*place, gate_near, po_near, bring)
        if n == len(sizes) - 3:
            *early, late = brought[1:]
        if bring:
            gate_near = brought[0]
        rights.append(right)
        done.append(right)
        start += size
    return outer_products(masked, sent, rights), early, late


def any_line(where, inputs, gate_pre, grad_out, w_down, proj_in, proj_out, early, late):
    in_part = jnp.dot(inputs, proj_in, preferred_element_type=jnp.float32)
    in_proj = lax.psum(in_part, "tensor").reshape(-1, LEN, PROJ)
    gathered = lax.all_gather(grad_out, "tensor", axis=1, tiled=True)
    up_grad = (dot_nt(gathered, w_down) * silu(gate_pre.astype(jnp.float32))).astype(jnp.bfloat16)
    out_part = jnp.dot(up_grad, proj_out, preferred_element_type=jnp.float32).reshape(-1, LEN, PROJ)
    grads = jnp.einsum("sti,stj->sij", in_proj, out_part, precision=HIGHEST)
    return grads.reshape(-1, PROJ * PROJ), early, late


def swap(a, axis, bit):
    return lax.ppermute(a, axis, [(i, i ^ bit) for i in range(lax.axis_size(axis))])


def bits(axis):
    return [1 << b for b in range(lax.axis_size(axis).bit_length() - 1)]


def xor_sum(a, axis):
    for bit in bits(axis):
        a = a + swap(a, axis, bit)
    return a


def positions():
    z, me, count = lax.axis_index("tensor"), lax.axis_index("dp"), lax.axis_size("dp")
    low = z < 2
    middle = jnp.logical_and(z > 0, z < 3)
    blocks = [z, z + 1 - 2 * (z % 2), jnp.where(low, 2, 1), jnp.where(low, 3, 0), middle]
    parts = [z * count + (me ^ s) for s in range(count)]
    return jnp.stack([a.astype(jnp.int32) for a in blocks + parts])


def on_device(inputs, gate_pre, grad_out, w_down, proj_in, proj_out, hessian, queries):
    where = positions()
    count = lax.axis_size("dp")
    parts = [queries] + [swap(queries, "dp", s) for s in range(1, count)]
    line = line_of_four if lax.axis_size("tensor") == 4 else any_line
    grads, parts, hessian = line(where, inputs, gate_pre, grad_out, w_down, proj_in, proj_out, parts, hessian)
    grads = xor_sum(grads, "tensor")

    scores = score_parts(where, grads, parts)
    all_grads = after(grads, scores)
    *first, last = bits("tensor")
    for bit in bits("dp"):
        all_grads = jnp.concatenate([all_grads, swap(all_grads, "dp", bit)], axis=0)
    for bit in first:
        scores = score_sum(scores, swap(scores, "tensor", bit))
    others = swap(scores, "tensor", last)
    all_grads = after(all_grads, scores)
    row_count = hessian.shape[0]
    if row_count % 128:
        mine = lax.dynamic_slice_in_dim(all_grads, where[FIRST_PART] * row_count, row_count, 1)
        updated = hessian + jnp.dot(mine.T, all_grads, precision=HIGHEST) / all_grads.shape[0]
    else:
        updated = update(all_grads, hessian)
    updated, others = lax.optimization_barrier((updated, others))
    return (updated, scores + others)


def solution(mesh):
    return jax.shard_map(
        on_device,
        mesh=mesh,
        in_specs=(
            P(("groups", "dp"), "tensor"),
            P(("groups", "dp"), "tensor"),
            P(("groups", "dp"), "tensor"),
            P("tensor", None),
            P("tensor", None),
            P("tensor", None),
            P(("groups", "tensor", "dp"), None),
            P("groups", ("tensor", "dp")),
        ),
        out_specs=(P(("groups", "tensor", "dp"), None), P(("groups", "dp"), None)),
        check_vma=False,
    )
```

```python
import functools

import jax
import jax.numpy as jnp
from jax import lax
from jax.experimental import pallas as pl
from jax.experimental.pallas import tpu as pltpu
from jax.sharding import PartitionSpec as P

PROJ = 64
LEN = 512
HIGHEST = lax.Precision.HIGHEST
NT = (((1,), (1,)), ((), ()))
TILE = 512
LIMIT = 16
FIRST_PART = 5
ANYWHERE = pl.BlockSpec(memory_space=pl.ANY)
INSIDE = pl.BlockSpec(memory_space=pltpu.VMEM)
OUTSIDE = pl.BlockSpec(memory_space=pltpu.HBM)


def silu(v):
    return 0.5 * v * (1.0 + jnp.tanh(0.5 * v))


def dot(a, b):
    return jnp.dot(a, b, preferred_element_type=jnp.float32)


def dot_nt(a, b):
    return lax.dot_general(a, b, NT, preferred_element_type=jnp.float32)


def placed(a, spec):
    if spec is INSIDE or spec is OUTSIDE:
        return pltpu.with_memory_space_constraint(a, spec.memory_space)
    return a


def call(body, name, where, grid, operands, in_specs, out_specs, out_shapes, scratch, mib, aliases=None, flops=1000):
    scalars = [] if where is None else [where]
    return pl.pallas_call(
        body,
        grid_spec=pltpu.PrefetchScalarGridSpec(
            num_scalar_prefetch=len(scalars), grid=grid, in_specs=in_specs, out_specs=out_specs, scratch_shapes=scratch
        ),
        out_shape=out_shapes,
        compiler_params=pltpu.CompilerParams(vmem_limit_bytes=mib * 2**20),
        cost_estimate=pl.CostEstimate(flops=flops, bytes_accessed=1000, transcendentals=0),
        name=name,
        input_output_aliases=aliases or {},
    )(*scalars, *[placed(a, spec) for a, spec in zip(operands, in_specs)])


def after(a, *others):
    return lax.optimization_barrier((a, *others))[0]


def fixed(shape):
    return pl.BlockSpec(shape, lambda j, where: (0, 0), pipeline_mode=pl.Buffered(1))


def my_part(p, width):
    at = lax.axis_index("tensor") * lax.axis_size("dp") + (lax.axis_index("dp") ^ p)
    return pl.ds(pl.multiple_of(at * width, width), width)


def tile_rows(t, size=TILE):
    return pl.ds(pl.multiple_of(t * size, size), size)


def columns(where, i, width):
    return pl.ds(pl.multiple_of(where[i] * width, width), width)


def input_body(where, inputs, pi_t, in_t):
    in_t[...] = dot_nt(pi_t[...], inputs[...])


def input_block(where, inputs, pi_t):
    shape = (pi_t.shape[0], inputs.shape[0])
    (in_t,) = call(
        input_body,
        "input_block",
        where,
        (1,),
        (inputs, pi_t),
        [fixed(inputs.shape), fixed(pi_t.shape)],
        [pl.BlockSpec(shape, lambda j, where: (0, 0))],
        [jax.ShapeDtypeStruct(shape, jnp.float32)],
        [],
        LIMIT,
    )
    return in_t


def own_body(where, own, w, w_last, acc, kept, token):
    here = tile_rows(pl.program_id(0))
    token[...] = jnp.zeros_like(token)
    kept[:, here] = w_last[...].T
    acc[:, here] = dot_nt(own[...], w[...])


def own_block(where, own, w):
    tokens, feats = own.shape
    hidden = w.shape[0]
    return call(
        own_body,
        "own_block",
        where,
        (hidden // TILE,),
        (own, w, w),
        [
            fixed(own.shape),
            pl.BlockSpec((TILE, feats), lambda j, where: (j, where[0])),
            pl.BlockSpec((TILE, feats), lambda j, where: (j, where[3])),
        ],
        [INSIDE, INSIDE, pl.BlockSpec((8, 128), lambda j, where: (0, 0))],
        [
            pltpu.VMEM((tokens, hidden), jnp.float32),
            pltpu.VMEM((feats, hidden), w.dtype),
            jax.ShapeDtypeStruct((8, 128), jnp.float32),
        ],
        [],
        LIMIT,
    )


def select(where, inner, outer):
    return jnp.where(where[4] == 1, inner[...], outer[...])


def add_body(where, *refs):
    *blocks, w, old, _, acc, token, block = refs
    step = pl.program_id(0)

    @pl.when(step == 0)
    def _():
        token[...] = jnp.zeros_like(token)
        if len(blocks) == 1:
            block[...] = blocks[0][...]
        else:
            half = len(blocks) // 2
            size = blocks[0].shape[0]
            for h in range(half):
                block[h * size : (h + 1) * size, :] = select(where, blocks[h], blocks[half + h])

    here = tile_rows(step)
    acc[:, here] = old[:, here] + dot_nt(block[...], w[...])


def add_block(where, which, blocks, w, old, token, flops):
    tokens, feats = old.shape[0], blocks[0].shape[1]
    return call(
        add_body,
        f"add_block_{which}",
        where,
        (w.shape[0] // TILE,),
        (*blocks, w, old, token),
        [fixed(a.shape) for a in blocks]
        + [pl.BlockSpec((TILE, feats), lambda j, where: (j, where[which])), INSIDE, ANYWHERE],
        [INSIDE, pl.BlockSpec((8, 128), lambda j, where: (0, 0))],
        [pltpu.VMEM(old.shape, old.dtype), jax.ShapeDtypeStruct((8, 128), jnp.float32)],
        [pltpu.VMEM((tokens, feats), blocks[0].dtype)],
        LIMIT,
        aliases={len(blocks) + 2: 0},
        flops=flops,
    )


def last_body(start, inner_at, bring, inner, outer, kept, old, gate, po_t, _, *rest):
    count = len(bring)
    far, rest = rest[:count], rest[count:]
    _, _, right, *near = rest[: 3 + count]
    gates, po, gate_sems, po_sem, near_sems = rest[3 + count :]
    size = outer.shape[0]
    hidden = kept.shape[1]
    tokens = pl.ds(start, size)
    spans = [pl.ds(t * TILE, TILE) for t in range(hidden // TILE)]
    po_read = pltpu.make_async_copy(po_t, po, po_sem)
    reads = [
        pltpu.make_async_copy(gate.at[tokens, span], gates.at[t], gate_sems.at[t]) for t, span in enumerate(spans)
    ]
    reads[0].start()
    po_read.start()
    for read in reads[1:]:
        read.start()
    brought = [
        pltpu.make_async_copy(a.at[pl.ds(first, b.shape[0])], b, near_sems.at[i])
        for i, (a, b, first) in enumerate(zip(far, near, bring))
    ]
    for copy in brought:
        copy.start()
    block = inner[pl.ds(inner_at, size), :] + outer[...]
    total = jnp.zeros((size, PROJ), jnp.float32)
    for t, span in enumerate(spans):
        hidden_grad = old[tokens, span] + dot(block, kept[:, span])
        reads[t].wait()
        up_grad = (hidden_grad * silu(gates[t].astype(jnp.float32))).astype(jnp.bfloat16)
        if t == 0:
            po_read.wait()
        total = total + dot_nt(up_grad, po[:, span])
    right[...] = total
    for copy in brought:
        copy.wait()


def last_block(inner, inner_at, outer, start, kept, old, gate, po_t, token, bring):
    size = outer.shape[0]
    tiles = kept.shape[1] // TILE
    return call(
        functools.partial(last_body, start, inner_at, [first for _, first, _ in bring]),
        "last_block",
        None,
        (1,),
        (inner, outer, kept, old, gate, po_t, token, *[a for a, _, _ in bring]),
        [INSIDE, INSIDE, INSIDE, INSIDE, OUTSIDE, ANYWHERE, ANYWHERE] + [OUTSIDE] * len(bring),
        [INSIDE] * (3 + len(bring)),
        [
            pltpu.VMEM(kept.shape, kept.dtype),
            pltpu.VMEM(old.shape, old.dtype),
            pltpu.VMEM((size, PROJ), jnp.float32),
            *[pltpu.VMEM((rows, a.shape[1]), a.dtype) for a, _, rows in bring],
        ],
        [
            pltpu.VMEM((tiles, size, TILE), gate.dtype),
            pltpu.VMEM(po_t.shape, po_t.dtype),
            pltpu.SemaphoreType.DMA((tiles,)),
            pltpu.SemaphoreType.DMA,
            pltpu.SemaphoreType.DMA((max(len(bring), 1),)),
        ],
        LIMIT,
        aliases={2: 0, 3: 1},
    )


def near_body(start, inner_at, bring, inner, outer, kept, old, gate, po, *rest):
    far, rest = rest[: len(bring)], rest[len(bring) :]
    _, _, right, *near = rest[: 3 + len(bring)]
    near_sems = rest[-1]
    size = outer.shape[0]
    brought = [
        pltpu.make_async_copy(a.at[pl.ds(first, b.shape[0])], b, near_sems.at[i])
        for i, (a, b, first) in enumerate(zip(far, near, bring))
    ]
    for copy in brought:
        copy.start()
    block = inner[pl.ds(inner_at, size), :] + outer[...]
    total = jnp.zeros((size, PROJ), jnp.float32)
    for t in range(kept.shape[1] // TILE):
        span = pl.ds(t * TILE, TILE)
        hidden_grad = old[pl.ds(start, size), span] + dot(block, kept[:, span])
        up_grad = (hidden_grad * silu(gate[:, span].astype(jnp.float32))).astype(jnp.bfloat16)
        total = total + dot_nt(up_grad, po[:, span])
    right[...] = total
    for copy in brought:
        copy.wait()


def near_block(inner, inner_at, outer, start, kept, old, gate, po, bring):
    return call(
        functools.partial(near_body, start, inner_at, [first for _, first, _ in bring]),
        "near_block",
        None,
        (1,),
        (inner, outer, kept, old, gate, po, *[a for a, _, _ in bring]),
        [INSIDE] * 6 + [OUTSIDE] * len(bring),
        [INSIDE] * (3 + len(bring)),
        [
            pltpu.VMEM(kept.shape, kept.dtype),
            pltpu.VMEM(old.shape, old.dtype),
            pltpu.VMEM((outer.shape[0], PROJ), jnp.float32),
            *[pltpu.VMEM((rows, a.shape[1]), a.dtype) for a, _, rows in bring],
        ],
        [pltpu.SemaphoreType.DMA((max(len(bring), 1),))],
        LIMIT,
        aliases={2: 0, 3: 1},
    )


def outer_body(masked, sent, *refs):
    *rights, grads, wide = refs
    left_t = masked[...] + sent[...].astype(jnp.float32)
    wide[...] = jnp.zeros_like(wide)
    start = 0
    terms = [None] * grads.shape[0]
    for right in rights:
        size = right.shape[0]
        s = start // LEN
        term = jnp.dot(
            left_t[:, start : start + size], right[...], precision=HIGHEST, preferred_element_type=jnp.float32
        )
        terms[s] = term if terms[s] is None else terms[s] + term
        start += size
    for s, term in enumerate(terms):
        wide[:, :PROJ] = term
        even = wide[pl.ds(0, PROJ // 2, stride=2), :]
        odd = wide[pl.ds(1, PROJ // 2, stride=2), :]
        rows = even + pltpu.roll(odd, PROJ, 1)
        for i in range(PROJ // 2):
            grads[s : s + 1, i * 2 * PROJ : (i + 1) * 2 * PROJ] = rows[i : i + 1, :]


def outer_products(masked, sent, rights):
    shape = (masked.shape[1] // LEN, PROJ * PROJ)
    (grads,) = call(
        outer_body,
        "outer_products",
        None,
        (1,),
        (masked, sent, *rights),
        [INSIDE] * (2 + len(rights)),
        [INSIDE],
        [pltpu.VMEM(shape, jnp.float32)],
        [pltpu.VMEM((PROJ, 2 * PROJ), jnp.float32)],
        LIMIT,
    )
    return grads


def small_kernel(body, name, where, *operands):
    (out,) = call(
        body,
        name,
        where,
        (1,),
        operands,
        [fixed(a.shape) for a in operands],
        [pl.BlockSpec(operands[0].shape, lambda j, where: (0, 0))],
        [jax.ShapeDtypeStruct(operands[0].shape, operands[0].dtype)],
        [],
        LIMIT,
    )
    return out


def score_sum(a, b):
    out = pltpu.VMEM(a.shape, a.dtype)
    (total,) = call(
        sum_body, "score_sum", None, (1,), (a, b), [INSIDE, INSIDE], [INSIDE], [out], [], LIMIT, flops=3 * 10**9
    )
    return total


def sum_body(*refs):
    a, b, out = refs[-3:]
    out[...] = a[...] + b[...]


def mask_body(where, a, out):
    out[...] = jnp.where(where[4] == 1, a[...], 0.0)


def score_body(grads, *rest):
    *parts, out = rest
    rows, width = parts[0].shape
    count = grads.shape[0]
    lane = lax.broadcasted_iota(jnp.int32, (rows, 128), 1)
    total = jnp.zeros((rows, 128), jnp.float32)
    for s in range(count):
        products = None
        for p, part in enumerate(parts):
            term = part[...] * grads[s : s + 1, my_part(p, width)]
            products = term if products is None else products + term
        total = jnp.where(lane == s, jnp.sum(products, axis=1, keepdims=True), total)
    out[...] = total.T[:count, :]


def score_parts(where, grads, parts):
    width = parts[0].shape[1]
    shape = (grads.shape[0], parts[0].shape[0])
    if width % 128:
        slices = [
            lax.dynamic_slice_in_dim(grads, where[FIRST_PART + p] * width, width, 1) for p in range(len(parts))
        ]
        return jnp.dot(jnp.concatenate(slices, axis=1), jnp.concatenate(parts, axis=1).T, precision=HIGHEST)
    (scores,) = call(
        score_body,
        "scores",
        None,
        (1,),
        (grads, *parts),
        [INSIDE] * (1 + len(parts)),
        [pl.BlockSpec(shape, lambda j: (0, 0))],
        [jax.ShapeDtypeStruct(shape, jnp.float32)],
        [],
        LIMIT,
    )
    return scores


def pieces(a):
    high = a.astype(jnp.bfloat16)
    rest = a - high.astype(jnp.float32)
    middle = rest.astype(jnp.bfloat16)
    low = (rest - middle.astype(jnp.float32)).astype(jnp.bfloat16)
    return high, middle, low


def update_body(scale, grads, hessian, out, new, out_sems):
    parts, _, width = new.shape
    high, middle, low = pieces(grads[:, my_part(0, new.shape[1])])
    left = jnp.concatenate([high, high, middle, middle, high, low], axis=0).T
    writes = []
    for t in range(parts):
        span = pl.ds(t * width, width)
        high, middle, low = pieces(grads[:, span])
        right = jnp.concatenate([high, middle, high, middle, low, high], axis=0)
        new[t] = hessian[:, span] + dot(left, right) * scale
        writes.append(pltpu.make_async_copy(new.at[t], out.at[:, span], out_sems.at[t]))
        writes[t].start()
    for write in writes:
        write.wait()


def update(grads, hessian):
    rows, length = hessian.shape
    count = grads.shape[0]
    parts = 8
    width = length // parts
    (updated,) = call(
        functools.partial(update_body, 1.0 / count),
        "hessian_update",
        None,
        (1,),
        (grads, hessian),
        [INSIDE, INSIDE],
        [ANYWHERE],
        [jax.ShapeDtypeStruct((rows, length), jnp.float32)],
        [pltpu.VMEM((parts, rows, width), jnp.float32), pltpu.SemaphoreType.DMA((parts,))],
        LIMIT,
        flops=1000,
    )
    return updated


def line_of_four(where, inputs, gate_pre, grad_out, w_down, proj_in, proj_out, early, late):
    send = functools.partial(lax.ppermute, axis_name="tensor")
    pairs = [(0, 1), (1, 0), (2, 3), (3, 2)]
    inner = [(1, 2), (2, 1)]
    outward = [(1, 0), (2, 3)]
    inward = [(0, 1), (3, 2)]
    tokens = grad_out.shape[0]
    halves = [slice(0, tokens // 2), slice(tokens // 2, tokens)]
    pair = send(grad_out, perm=pairs)
    own = [grad_out[half] for half in halves]
    mid_inner = [send(a, perm=inner) for a in own]
    in_part = input_block(where, inputs, proj_in.T)
    from_end = send(after(in_part, mid_inner[0]), perm=inward)
    acc, kept, begun = own_block(where, after(grad_out, in_part, *early), w_down)
    mid_outer = [send(after(a, begun), perm=outward) for a in mid_inner]
    side = small_kernel(sum_body, "side", where, in_part, after(from_end, begun, pair))
    end_inner = [send(pair[halves[0]], perm=inner)]
    end_inner.append(send(after(pair[halves[1]], mid_outer[0], side), perm=inner))
    total = small_kernel(sum_body, "total", where, side, send(side, perm=inner))
    masked = small_kernel(mask_body, "masked", where, total)

    acc, first = add_block(where, 1, [pair], w_down, after(acc, mid_outer[0]), begun, 2 * grad_out.size * w_down.shape[0])
    acc, second = add_block(where, 2, mid_inner + mid_outer, w_down, acc, first, 1000)

    sizes = [256] * (tokens // 256 - 1) + [128, 64, 64]
    arrived, done = [total, total, total], [first, first, second]
    rights = []
    start = 0
    for n, size in enumerate(sizes):
        h, at = divmod(start, tokens // 2)
        ahead = arrived[min(n + 1, 4)]
        end_outer = send(after(end_inner[h][at : at + size], ahead, done[min(n, 4)]), perm=outward)
        arrived.append(end_outer)
        bring = []
        if n + 1 < len(sizes):
            bring.append((gate_pre, start + size, sizes[n + 1]))
        if n == 0:
            bring.append((proj_out.T, 0, PROJ))
        if n == len(sizes) - 4:
            bring += [(a, 0, a.shape[0]) for a in (*early, late)]
        place = end_inner[h], at, end_outer, start, kept, acc
        if n == 0:
            kept, acc, right, *brought = last_block(*place, gate_pre, proj_out.T, second, bring)
            po_near = brought[1]
        else:
            kept, acc, right, *brought = near_block(*place, gate_near, po_near, bring)
        if n == len(sizes) - 4:
            *early, late = brought[1:]
        if bring:
            gate_near = brought[0]
        rights.append(right)
        done.append(right)
        start += size
    sent = send(after(total.astype(jnp.bfloat16), arrived[5]), perm=outward)
    return outer_products(masked, sent, rights), early, late


def any_line(where, inputs, gate_pre, grad_out, w_down, proj_in, proj_out, early, late):
    in_part = jnp.dot(inputs, proj_in, preferred_element_type=jnp.float32)
    in_proj = lax.psum(in_part, "tensor").reshape(-1, LEN, PROJ)
    gathered = lax.all_gather(grad_out, "tensor", axis=1, tiled=True)
    up_grad = (dot_nt(gathered, w_down) * silu(gate_pre.astype(jnp.float32))).astype(jnp.bfloat16)
    out_part = jnp.dot(up_grad, proj_out, preferred_element_type=jnp.float32).reshape(-1, LEN, PROJ)
    grads = jnp.einsum("sti,stj->sij", in_proj, out_part, precision=HIGHEST)
    return grads.reshape(-1, PROJ * PROJ), early, late


def swap(a, axis, bit):
    return lax.ppermute(a, axis, [(i, i ^ bit) for i in range(lax.axis_size(axis))])


def bits(axis):
    return [1 << b for b in range(lax.axis_size(axis).bit_length() - 1)]


def xor_sum(a, axis):
    for bit in bits(axis):
        a = a + swap(a, axis, bit)
    return a


def positions():
    z, me, count = lax.axis_index("tensor"), lax.axis_index("dp"), lax.axis_size("dp")
    low = z < 2
    middle = jnp.logical_and(z > 0, z < 3)
    blocks = [z, z + 1 - 2 * (z % 2), jnp.where(low, 2, 1), jnp.where(low, 3, 0), middle]
    parts = [z * count + (me ^ s) for s in range(count)]
    return jnp.stack([a.astype(jnp.int32) for a in blocks + parts])


def on_device(inputs, gate_pre, grad_out, w_down, proj_in, proj_out, hessian, queries):
    where = positions()
    count = lax.axis_size("dp")
    parts = [queries] + [swap(queries, "dp", s) for s in range(1, count)]
    line = line_of_four if lax.axis_size("tensor") == 4 else any_line
    grads, parts, hessian = line(where, inputs, gate_pre, grad_out, w_down, proj_in, proj_out, parts, hessian)
    grads = xor_sum(grads, "tensor")

    scores = score_parts(where, grads, parts)
    all_grads = after(grads, scores)
    *first, last = bits("tensor")
    for bit in bits("dp"):
        all_grads = jnp.concatenate([all_grads, swap(all_grads, "dp", bit)], axis=0)
    for bit in first:
        scores = score_sum(scores, swap(scores, "tensor", bit))
    others = swap(scores, "tensor", last)
    all_grads = after(all_grads, scores)
    row_count = hessian.shape[0]
    if row_count % 128:
        mine = lax.dynamic_slice_in_dim(all_grads, where[FIRST_PART] * row_count, row_count, 1)
        updated = hessian + jnp.dot(mine.T, all_grads, precision=HIGHEST) / all_grads.shape[0]
    else:
        updated = update(all_grads, hessian)
    updated, others = lax.optimization_barrier((updated, others))
    return (updated, scores + others)


def solution(mesh):
    return jax.shard_map(
        on_device,
        mesh=mesh,
        in_specs=(
            P(("groups", "dp"), "tensor"),
            P(("groups", "dp"), "tensor"),
            P(("groups", "dp"), "tensor"),
            P("tensor", None),
            P("tensor", None),
            P("tensor", None),
            P(("groups", "tensor", "dp"), None),
            P("groups", ("tensor", "dp")),
        ),
        out_specs=(P(("groups", "tensor", "dp"), None), P(("groups", "dp"), None)),
        check_vma=False,
    )
```

```python
import functools

import jax
import jax.numpy as jnp
from jax import lax
from jax.experimental import pallas as pl
from jax.experimental.pallas import tpu as pltpu
from jax.sharding import PartitionSpec as P

PROJ = 64
LEN = 512
HIGHEST = lax.Precision.HIGHEST
NT = (((1,), (1,)), ((), ()))
TILE = 512
LIMIT = 16
FIRST_PART = 5
ANYWHERE = pl.BlockSpec(memory_space=pl.ANY)
INSIDE = pl.BlockSpec(memory_space=pltpu.VMEM)
OUTSIDE = pl.BlockSpec(memory_space=pltpu.HBM)


def silu(v):
    return 0.5 * v * (1.0 + jnp.tanh(0.5 * v))


def dot(a, b):
    return jnp.dot(a, b, preferred_element_type=jnp.float32)


def dot_nt(a, b):
    return lax.dot_general(a, b, NT, preferred_element_type=jnp.float32)


def placed(a, spec):
    if spec is INSIDE or spec is OUTSIDE:
        return pltpu.with_memory_space_constraint(a, spec.memory_space)
    return a


def call(body, name, where, grid, operands, in_specs, out_specs, out_shapes, scratch, mib, aliases=None, flops=1000):
    scalars = [] if where is None else [where]
    return pl.pallas_call(
        body,
        grid_spec=pltpu.PrefetchScalarGridSpec(
            num_scalar_prefetch=len(scalars), grid=grid, in_specs=in_specs, out_specs=out_specs, scratch_shapes=scratch
        ),
        out_shape=out_shapes,
        compiler_params=pltpu.CompilerParams(vmem_limit_bytes=mib * 2**20),
        cost_estimate=pl.CostEstimate(flops=flops, bytes_accessed=1000, transcendentals=0),
        name=name,
        input_output_aliases=aliases or {},
    )(*scalars, *[placed(a, spec) for a, spec in zip(operands, in_specs)])


def after(a, *others):
    return lax.optimization_barrier((a, *others))[0]


def fixed(shape):
    return pl.BlockSpec(shape, lambda j, where: (0, 0), pipeline_mode=pl.Buffered(1))


def my_part(p, width):
    at = lax.axis_index("tensor") * lax.axis_size("dp") + (lax.axis_index("dp") ^ p)
    return pl.ds(pl.multiple_of(at * width, width), width)


def tile_rows(t, size=TILE):
    return pl.ds(pl.multiple_of(t * size, size), size)


def columns(where, i, width):
    return pl.ds(pl.multiple_of(where[i] * width, width), width)


def input_body(where, inputs, pi_t, in_t):
    in_t[...] = dot_nt(pi_t[...], inputs[...])


def input_block(where, inputs, pi_t):
    shape = (pi_t.shape[0], inputs.shape[0])
    (in_t,) = call(
        input_body,
        "input_block",
        where,
        (1,),
        (inputs, pi_t),
        [fixed(inputs.shape), fixed(pi_t.shape)],
        [pl.BlockSpec(shape, lambda j, where: (0, 0))],
        [jax.ShapeDtypeStruct(shape, jnp.float32)],
        [],
        LIMIT,
    )
    return in_t


def own_body(where, own, w, w_last, acc, kept, token):
    here = tile_rows(pl.program_id(0))
    token[...] = jnp.zeros_like(token)
    kept[:, here] = w_last[...].T
    acc[:, here] = dot_nt(own[...], w[...])


def own_block(where, own, w):
    tokens, feats = own.shape
    hidden = w.shape[0]
    return call(
        own_body,
        "own_block",
        where,
        (hidden // TILE,),
        (own, w, w),
        [
            fixed(own.shape),
            pl.BlockSpec((TILE, feats), lambda j, where: (j, where[0])),
            pl.BlockSpec((TILE, feats), lambda j, where: (j, where[3])),
        ],
        [INSIDE, INSIDE, pl.BlockSpec((8, 128), lambda j, where: (0, 0))],
        [
            pltpu.VMEM((tokens, hidden), jnp.float32),
            pltpu.VMEM((feats, hidden), w.dtype),
            jax.ShapeDtypeStruct((8, 128), jnp.float32),
        ],
        [],
        LIMIT,
    )


def select(where, inner, outer):
    return jnp.where(where[4] == 1, inner[...], outer[...])


def add_body(where, *refs):
    *blocks, w, old, _, acc, token, block = refs
    step = pl.program_id(0)

    @pl.when(step == 0)
    def _():
        token[...] = jnp.zeros_like(token)
        if len(blocks) == 1:
            block[...] = blocks[0][...]
        else:
            half = len(blocks) // 2
            size = blocks[0].shape[0]
            for h in range(half):
                block[h * size : (h + 1) * size, :] = select(where, blocks[h], blocks[half + h])

    here = tile_rows(step)
    acc[:, here] = old[:, here] + dot_nt(block[...], w[...])


def add_block(where, which, blocks, w, old, token, flops):
    tokens, feats = old.shape[0], blocks[0].shape[1]
    return call(
        add_body,
        f"add_block_{which}",
        where,
        (w.shape[0] // TILE,),
        (*blocks, w, old, token),
        [fixed(a.shape) for a in blocks]
        + [pl.BlockSpec((TILE, feats), lambda j, where: (j, where[which])), INSIDE, ANYWHERE],
        [INSIDE, pl.BlockSpec((8, 128), lambda j, where: (0, 0))],
        [pltpu.VMEM(old.shape, old.dtype), jax.ShapeDtypeStruct((8, 128), jnp.float32)],
        [pltpu.VMEM((tokens, feats), blocks[0].dtype)],
        LIMIT,
        aliases={len(blocks) + 2: 0},
        flops=flops,
    )


def last_body(start, inner_at, bring, inner, outer, kept, old, gate, po_t, _, *rest):
    count = len(bring)
    far, rest = rest[:count], rest[count:]
    _, _, right, *near = rest[: 3 + count]
    gates, po, gate_sems, po_sem, near_sems = rest[3 + count :]
    size = outer.shape[0]
    hidden = kept.shape[1]
    tokens = pl.ds(start, size)
    spans = [pl.ds(t * TILE, TILE) for t in range(hidden // TILE)]
    po_read = pltpu.make_async_copy(po_t, po, po_sem)
    reads = [
        pltpu.make_async_copy(gate.at[tokens, span], gates.at[t], gate_sems.at[t]) for t, span in enumerate(spans)
    ]
    reads[0].start()
    po_read.start()
    for read in reads[1:]:
        read.start()
    brought = [
        pltpu.make_async_copy(a.at[pl.ds(first, b.shape[0])], b, near_sems.at[i])
        for i, (a, b, first) in enumerate(zip(far, near, bring))
    ]
    for copy in brought:
        copy.start()
    block = inner[pl.ds(inner_at, size), :] + outer[...]
    total = jnp.zeros((size, PROJ), jnp.float32)
    for t, span in enumerate(spans):
        hidden_grad = old[tokens, span] + dot(block, kept[:, span])
        reads[t].wait()
        up_grad = (hidden_grad * silu(gates[t].astype(jnp.float32))).astype(jnp.bfloat16)
        if t == 0:
            po_read.wait()
        total = total + dot_nt(up_grad, po[:, span])
    right[...] = total
    for copy in brought:
        copy.wait()


def last_block(inner, inner_at, outer, start, kept, old, gate, po_t, token, bring):
    size = outer.shape[0]
    tiles = kept.shape[1] // TILE
    return call(
        functools.partial(last_body, start, inner_at, [first for _, first, _ in bring]),
        "last_block",
        None,
        (1,),
        (inner, outer, kept, old, gate, po_t, token, *[a for a, _, _ in bring]),
        [INSIDE, INSIDE, INSIDE, INSIDE, OUTSIDE, ANYWHERE, ANYWHERE] + [OUTSIDE] * len(bring),
        [INSIDE] * (3 + len(bring)),
        [
            pltpu.VMEM(kept.shape, kept.dtype),
            pltpu.VMEM(old.shape, old.dtype),
            pltpu.VMEM((size, PROJ), jnp.float32),
            *[pltpu.VMEM((rows, a.shape[1]), a.dtype) for a, _, rows in bring],
        ],
        [
            pltpu.VMEM((tiles, size, TILE), gate.dtype),
            pltpu.VMEM(po_t.shape, po_t.dtype),
            pltpu.SemaphoreType.DMA((tiles,)),
            pltpu.SemaphoreType.DMA,
            pltpu.SemaphoreType.DMA((max(len(bring), 1),)),
        ],
        LIMIT,
        aliases={2: 0, 3: 1},
    )


def near_body(start, inner_at, bring, inner, outer, kept, old, gate, po, *rest):
    far, rest = rest[: len(bring)], rest[len(bring) :]
    _, _, right, *near = rest[: 3 + len(bring)]
    near_sems = rest[-1]
    size = outer.shape[0]
    brought = [
        pltpu.make_async_copy(a.at[pl.ds(first, b.shape[0])], b, near_sems.at[i])
        for i, (a, b, first) in enumerate(zip(far, near, bring))
    ]
    for copy in brought:
        copy.start()
    block = inner[pl.ds(inner_at, size), :] + outer[...]
    total = jnp.zeros((size, PROJ), jnp.float32)
    for t in range(kept.shape[1] // TILE):
        span = pl.ds(t * TILE, TILE)
        hidden_grad = old[pl.ds(start, size), span] + dot(block, kept[:, span])
        up_grad = (hidden_grad * silu(gate[:, span].astype(jnp.float32))).astype(jnp.bfloat16)
        total = total + dot_nt(up_grad, po[:, span])
    right[...] = total
    for copy in brought:
        copy.wait()


def near_block(inner, inner_at, outer, start, kept, old, gate, po, bring):
    return call(
        functools.partial(near_body, start, inner_at, [first for _, first, _ in bring]),
        "near_block",
        None,
        (1,),
        (inner, outer, kept, old, gate, po, *[a for a, _, _ in bring]),
        [INSIDE] * 6 + [OUTSIDE] * len(bring),
        [INSIDE] * (3 + len(bring)),
        [
            pltpu.VMEM(kept.shape, kept.dtype),
            pltpu.VMEM(old.shape, old.dtype),
            pltpu.VMEM((outer.shape[0], PROJ), jnp.float32),
            *[pltpu.VMEM((rows, a.shape[1]), a.dtype) for a, _, rows in bring],
        ],
        [pltpu.SemaphoreType.DMA((max(len(bring), 1),))],
        LIMIT,
        aliases={2: 0, 3: 1},
    )


def outer_body(masked, sent, *refs):
    *rights, grads, wide = refs
    left_t = masked[...] + sent[...].astype(jnp.float32)
    wide[...] = jnp.zeros_like(wide)
    start = 0
    terms = [None] * grads.shape[0]
    for right in rights:
        size = right.shape[0]
        s = start // LEN
        term = jnp.dot(
            left_t[:, start : start + size], right[...], precision=HIGHEST, preferred_element_type=jnp.float32
        )
        terms[s] = term if terms[s] is None else terms[s] + term
        start += size
    for s, term in enumerate(terms):
        wide[:, :PROJ] = term
        even = wide[pl.ds(0, PROJ // 2, stride=2), :]
        odd = wide[pl.ds(1, PROJ // 2, stride=2), :]
        rows = even + pltpu.roll(odd, PROJ, 1)
        for i in range(PROJ // 2):
            grads[s : s + 1, i * 2 * PROJ : (i + 1) * 2 * PROJ] = rows[i : i + 1, :]


def outer_products(masked, sent, rights):
    shape = (masked.shape[1] // LEN, PROJ * PROJ)
    (grads,) = call(
        outer_body,
        "outer_products",
        None,
        (1,),
        (masked, sent, *rights),
        [INSIDE] * (2 + len(rights)),
        [INSIDE],
        [pltpu.VMEM(shape, jnp.float32)],
        [pltpu.VMEM((PROJ, 2 * PROJ), jnp.float32)],
        LIMIT,
    )
    return grads


def small_kernel(body, name, where, *operands):
    (out,) = call(
        body,
        name,
        where,
        (1,),
        operands,
        [fixed(a.shape) for a in operands],
        [pl.BlockSpec(operands[0].shape, lambda j, where: (0, 0))],
        [jax.ShapeDtypeStruct(operands[0].shape, operands[0].dtype)],
        [],
        LIMIT,
    )
    return out


def score_sum(a, b):
    out = pltpu.VMEM(a.shape, a.dtype)
    (total,) = call(
        sum_body, "score_sum", None, (1,), (a, b), [INSIDE, INSIDE], [INSIDE], [out], [], LIMIT, flops=3 * 10**9
    )
    return total


def sum_body(*refs):
    a, b, out = refs[-3:]
    out[...] = a[...] + b[...]


def mask_body(where, a, out):
    out[...] = jnp.where(where[4] == 1, a[...], 0.0)


def score_body(grads, *rest):
    *parts, out = rest
    rows, width = parts[0].shape
    count = grads.shape[0]
    lane = lax.broadcasted_iota(jnp.int32, (rows, 128), 1)
    total = jnp.zeros((rows, 128), jnp.float32)
    for s in range(count):
        products = None
        for p, part in enumerate(parts):
            term = part[...] * grads[s : s + 1, my_part(p, width)]
            products = term if products is None else products + term
        total = jnp.where(lane == s, jnp.sum(products, axis=1, keepdims=True), total)
    out[...] = total.T[:count, :]


def score_parts(where, grads, parts):
    width = parts[0].shape[1]
    shape = (grads.shape[0], parts[0].shape[0])
    if width % 128:
        slices = [
            lax.dynamic_slice_in_dim(grads, where[FIRST_PART + p] * width, width, 1) for p in range(len(parts))
        ]
        return jnp.dot(jnp.concatenate(slices, axis=1), jnp.concatenate(parts, axis=1).T, precision=HIGHEST)
    (scores,) = call(
        score_body,
        "scores",
        None,
        (1,),
        (grads, *parts),
        [INSIDE] * (1 + len(parts)),
        [pl.BlockSpec(shape, lambda j: (0, 0))],
        [jax.ShapeDtypeStruct(shape, jnp.float32)],
        [],
        LIMIT,
    )
    return scores


def pieces(a):
    high = a.astype(jnp.bfloat16)
    rest = a - high.astype(jnp.float32)
    middle = rest.astype(jnp.bfloat16)
    low = (rest - middle.astype(jnp.float32)).astype(jnp.bfloat16)
    return high, middle, low


def update_body(scale, grads, hessian, out, new, out_sems):
    parts, _, width = new.shape
    high, middle, low = pieces(grads[:, my_part(0, new.shape[1])] * scale)
    left = jnp.concatenate([high, high, middle, middle, high, low], axis=0).T
    writes = []
    for t in range(parts):
        span = pl.ds(t * width, width)
        high, middle, low = pieces(grads[:, span])
        right = jnp.concatenate([high, middle, high, middle, low, high], axis=0)
        new[t] = hessian[:, span] + dot(left, right)
        writes.append(pltpu.make_async_copy(new.at[t], out.at[:, span], out_sems.at[t]))
        writes[t].start()
    for write in writes:
        write.wait()


def update(grads, hessian):
    rows, length = hessian.shape
    count = grads.shape[0]
    parts = 8
    width = length // parts
    (updated,) = call(
        functools.partial(update_body, 1.0 / count),
        "hessian_update",
        None,
        (1,),
        (grads, hessian),
        [INSIDE, INSIDE],
        [ANYWHERE],
        [jax.ShapeDtypeStruct((rows, length), jnp.float32)],
        [pltpu.VMEM((parts, rows, width), jnp.float32), pltpu.SemaphoreType.DMA((parts,))],
        LIMIT,
        flops=1000,
    )
    return updated


def line_of_four(where, inputs, gate_pre, grad_out, w_down, proj_in, proj_out, early, late):
    send = functools.partial(lax.ppermute, axis_name="tensor")
    pairs = [(0, 1), (1, 0), (2, 3), (3, 2)]
    inner = [(1, 2), (2, 1)]
    outward = [(1, 0), (2, 3)]
    inward = [(0, 1), (3, 2)]
    tokens = grad_out.shape[0]
    halves = [slice(0, tokens // 2), slice(tokens // 2, tokens)]
    pair = send(grad_out, perm=pairs)
    own = [grad_out[half] for half in halves]
    mid_inner = [send(a, perm=inner) for a in own]
    in_part = input_block(where, inputs, proj_in.T)
    from_end = send(after(in_part, mid_inner[0]), perm=inward)
    acc, kept, begun = own_block(where, after(grad_out, in_part, *early), w_down)
    mid_outer = [send(after(a, begun), perm=outward) for a in mid_inner]
    side = small_kernel(sum_body, "side", where, in_part, after(from_end, begun, pair))
    end_inner = [send(pair[halves[0]], perm=inner)]
    end_inner.append(send(after(pair[halves[1]], mid_outer[0], side), perm=inner))
    total = small_kernel(sum_body, "total", where, side, send(side, perm=inner))
    masked = small_kernel(mask_body, "masked", where, total)
    sent = send(total.astype(jnp.bfloat16), perm=outward)

    acc, first = add_block(where, 1, [pair], w_down, after(acc, mid_outer[0]), begun, 2 * grad_out.size * w_down.shape[0])
    acc, second = add_block(where, 2, mid_inner + mid_outer, w_down, acc, first, 1000)

    sizes = [256] * (tokens // 256 - 1) + [128, 128]
    arrived, done = [total, total, total], [first, first, second]
    rights = []
    start = 0
    for n, size in enumerate(sizes):
        h, at = divmod(start, tokens // 2)
        ahead = arrived[n + 1] if n < 4 else arrived[n]
        end_outer = send(after(end_inner[h][at : at + size], ahead, done[n]), perm=outward)
        arrived.append(end_outer)
        bring = []
        if n + 1 < len(sizes):
            bring.append((gate_pre, start + size, sizes[n + 1]))
        if n == 0:
            bring.append((proj_out.T, 0, PROJ))
        if n == len(sizes) - 3:
            bring += [(a, 0, a.shape[0]) for a in (*early, late)]
        place = end_inner[h], at, end_outer, start, kept, acc
        if n == 0:
            kept, acc, right, *brought = last_block(*place, gate_pre, proj_out.T, second, bring)
            po_near = brought[1]
        else:
            kept, acc, right, *brought = near_block(*place, gate_near, po_near, bring)
        if n == len(sizes) - 3:
            *early, late = brought[1:]
        if bring:
            gate_near = brought[0]
        rights.append(right)
        done.append(right)
        start += size
    return outer_products(masked, sent, rights), early, late


def any_line(where, inputs, gate_pre, grad_out, w_down, proj_in, proj_out, early, late):
    in_part = jnp.dot(inputs, proj_in, preferred_element_type=jnp.float32)
    in_proj = lax.psum(in_part, "tensor").reshape(-1, LEN, PROJ)
    gathered = lax.all_gather(grad_out, "tensor", axis=1, tiled=True)
    up_grad = (dot_nt(gathered, w_down) * silu(gate_pre.astype(jnp.float32))).astype(jnp.bfloat16)
    out_part = jnp.dot(up_grad, proj_out, preferred_element_type=jnp.float32).reshape(-1, LEN, PROJ)
    grads = jnp.einsum("sti,stj->sij", in_proj, out_part, precision=HIGHEST)
    return grads.reshape(-1, PROJ * PROJ), early, late


def swap(a, axis, bit):
    return lax.ppermute(a, axis, [(i, i ^ bit) for i in range(lax.axis_size(axis))])


def bits(axis):
    return [1 << b for b in range(lax.axis_size(axis).bit_length() - 1)]


def xor_sum(a, axis):
    for bit in reversed(bits(axis)):
        a = a + swap(a, axis, bit)
    return a


def positions():
    z, me, count = lax.axis_index("tensor"), lax.axis_index("dp"), lax.axis_size("dp")
    low = z < 2
    middle = jnp.logical_and(z > 0, z < 3)
    blocks = [z, z + 1 - 2 * (z % 2), jnp.where(low, 2, 1), jnp.where(low, 3, 0), middle]
    parts = [z * count + (me ^ s) for s in range(count)]
    return jnp.stack([a.astype(jnp.int32) for a in blocks + parts])


def on_device(inputs, gate_pre, grad_out, w_down, proj_in, proj_out, hessian, queries):
    where = positions()
    count = lax.axis_size("dp")
    parts = [queries] + [swap(queries, "dp", s) for s in range(1, count)]
    line = line_of_four if lax.axis_size("tensor") == 4 else any_line
    grads, parts, hessian = line(where, inputs, gate_pre, grad_out, w_down, proj_in, proj_out, parts, hessian)
    grads = xor_sum(grads, "tensor")

    scores = score_parts(where, grads, parts)
    all_grads = after(grads, scores)
    *first, last = bits("tensor")
    for bit in bits("dp"):
        all_grads = jnp.concatenate([all_grads, swap(all_grads, "dp", bit)], axis=0)
    for bit in first:
        scores = score_sum(scores, swap(scores, "tensor", bit))
    others = swap(scores, "tensor", last)
    all_grads = after(all_grads, scores)
    row_count = hessian.shape[0]
    if row_count % 128:
        mine = lax.dynamic_slice_in_dim(all_grads, where[FIRST_PART] * row_count, row_count, 1)
        updated = hessian + jnp.dot(mine.T, all_grads, precision=HIGHEST) / all_grads.shape[0]
    else:
        updated = update(all_grads, hessian)
    updated, others = lax.optimization_barrier((updated, others))
    return (updated, scores + others)


def solution(mesh):
    return jax.shard_map(
        on_device,
        mesh=mesh,
        in_specs=(
            P(("groups", "dp"), "tensor"),
            P(("groups", "dp"), "tensor"),
            P(("groups", "dp"), "tensor"),
            P("tensor", None),
            P("tensor", None),
            P("tensor", None),
            P(("groups", "tensor", "dp"), None),
            P("groups", ("tensor", "dp")),
        ),
        out_specs=(P(("groups", "tensor", "dp"), None), P(("groups", "dp"), None)),
        check_vma=False,
    )
```

```python
import functools

import jax
import jax.numpy as jnp
from jax import lax
from jax.experimental import pallas as pl
from jax.experimental.pallas import tpu as pltpu
from jax.sharding import PartitionSpec as P

PROJ = 64
LEN = 512
HIGHEST = lax.Precision.HIGHEST
NT = (((1,), (1,)), ((), ()))
TILE = 512
LIMIT = 16
FIRST_PART = 5
ANYWHERE = pl.BlockSpec(memory_space=pl.ANY)
INSIDE = pl.BlockSpec(memory_space=pltpu.VMEM)
OUTSIDE = pl.BlockSpec(memory_space=pltpu.HBM)


def silu(v):
    return 0.5 * v * (1.0 + jnp.tanh(0.5 * v))


def dot(a, b):
    return jnp.dot(a, b, preferred_element_type=jnp.float32)


def dot_nt(a, b):
    return lax.dot_general(a, b, NT, preferred_element_type=jnp.float32)


def placed(a, spec):
    if spec is INSIDE or spec is OUTSIDE:
        return pltpu.with_memory_space_constraint(a, spec.memory_space)
    return a


def call(body, name, where, grid, operands, in_specs, out_specs, out_shapes, scratch, mib, aliases=None, flops=1000):
    scalars = [] if where is None else [where]
    return pl.pallas_call(
        body,
        grid_spec=pltpu.PrefetchScalarGridSpec(
            num_scalar_prefetch=len(scalars), grid=grid, in_specs=in_specs, out_specs=out_specs, scratch_shapes=scratch
        ),
        out_shape=out_shapes,
        compiler_params=pltpu.CompilerParams(vmem_limit_bytes=mib * 2**20),
        cost_estimate=pl.CostEstimate(flops=flops, bytes_accessed=1000, transcendentals=0),
        name=name,
        input_output_aliases=aliases or {},
    )(*scalars, *[placed(a, spec) for a, spec in zip(operands, in_specs)])


def after(a, *others):
    return lax.optimization_barrier((a, *others))[0]


def fixed(shape):
    return pl.BlockSpec(shape, lambda j, where: (0, 0), pipeline_mode=pl.Buffered(1))


def my_part(p, width):
    at = lax.axis_index("tensor") * lax.axis_size("dp") + (lax.axis_index("dp") ^ p)
    return pl.ds(pl.multiple_of(at * width, width), width)


def tile_rows(t, size=TILE):
    return pl.ds(pl.multiple_of(t * size, size), size)


def columns(where, i, width):
    return pl.ds(pl.multiple_of(where[i] * width, width), width)


def input_body(where, inputs, pi_t, in_t):
    in_t[...] = dot_nt(pi_t[...], inputs[...])


def input_block(where, inputs, pi_t):
    shape = (pi_t.shape[0], inputs.shape[0])
    (in_t,) = call(
        input_body,
        "input_block",
        where,
        (1,),
        (inputs, pi_t),
        [fixed(inputs.shape), fixed(pi_t.shape)],
        [pl.BlockSpec(shape, lambda j, where: (0, 0))],
        [jax.ShapeDtypeStruct(shape, jnp.float32)],
        [],
        LIMIT,
    )
    return in_t


def own_body(where, own, w, w_last, acc, kept, token):
    here = tile_rows(pl.program_id(0))
    token[...] = jnp.zeros_like(token)
    kept[:, here] = w_last[...].T
    acc[:, here] = dot_nt(own[...], w[...])


def own_block(where, own, w):
    tokens, feats = own.shape
    hidden = w.shape[0]
    return call(
        own_body,
        "own_block",
        where,
        (hidden // TILE,),
        (own, w, w),
        [
            fixed(own.shape),
            pl.BlockSpec((TILE, feats), lambda j, where: (j, where[0])),
            pl.BlockSpec((TILE, feats), lambda j, where: (j, where[3])),
        ],
        [INSIDE, INSIDE, pl.BlockSpec((8, 128), lambda j, where: (0, 0))],
        [
            pltpu.VMEM((tokens, hidden), jnp.float32),
            pltpu.VMEM((feats, hidden), w.dtype),
            jax.ShapeDtypeStruct((8, 128), jnp.float32),
        ],
        [],
        LIMIT,
    )


def select(where, inner, outer):
    return jnp.where(where[4] == 1, inner[...], outer[...])


def add_body(where, *refs):
    *blocks, w, old, _, acc, token, block = refs
    step = pl.program_id(0)

    @pl.when(step == 0)
    def _():
        token[...] = jnp.zeros_like(token)
        if len(blocks) == 1:
            block[...] = blocks[0][...]
        else:
            half = len(blocks) // 2
            size = blocks[0].shape[0]
            for h in range(half):
                block[h * size : (h + 1) * size, :] = select(where, blocks[h], blocks[half + h])

    here = tile_rows(step)
    acc[:, here] = old[:, here] + dot_nt(block[...], w[...])


def add_block(where, which, blocks, w, old, token, flops):
    tokens, feats = old.shape[0], blocks[0].shape[1]
    return call(
        add_body,
        f"add_block_{which}",
        where,
        (w.shape[0] // TILE,),
        (*blocks, w, old, token),
        [fixed(a.shape) for a in blocks]
        + [pl.BlockSpec((TILE, feats), lambda j, where: (j, where[which])), INSIDE, ANYWHERE],
        [INSIDE, pl.BlockSpec((8, 128), lambda j, where: (0, 0))],
        [pltpu.VMEM(old.shape, old.dtype), jax.ShapeDtypeStruct((8, 128), jnp.float32)],
        [pltpu.VMEM((tokens, feats), blocks[0].dtype)],
        LIMIT,
        aliases={len(blocks) + 2: 0},
        flops=flops,
    )


def last_body(start, inner_at, bring, inner, outer, kept, old, gate, po_t, _, *rest):
    count = len(bring)
    far, rest = rest[:count], rest[count:]
    _, _, right, *near = rest[: 3 + count]
    gates, po, gate_sems, po_sem, near_sems = rest[3 + count :]
    size = outer.shape[0]
    hidden = kept.shape[1]
    tokens = pl.ds(start, size)
    spans = [pl.ds(t * TILE, TILE) for t in range(hidden // TILE)]
    po_read = pltpu.make_async_copy(po_t, po, po_sem)
    reads = [
        pltpu.make_async_copy(gate.at[tokens, span], gates.at[t], gate_sems.at[t]) for t, span in enumerate(spans)
    ]
    reads[0].start()
    po_read.start()
    for read in reads[1:]:
        read.start()
    brought = [
        pltpu.make_async_copy(a.at[pl.ds(first, b.shape[0])], b, near_sems.at[i])
        for i, (a, b, first) in enumerate(zip(far, near, bring))
    ]
    for copy in brought:
        copy.start()
    block = inner[pl.ds(inner_at, size), :] + outer[...]
    total = jnp.zeros((size, PROJ), jnp.float32)
    for t, span in enumerate(spans):
        hidden_grad = old[tokens, span] + dot(block, kept[:, span])
        reads[t].wait()
        up_grad = (hidden_grad * silu(gates[t].astype(jnp.float32))).astype(jnp.bfloat16)
        if t == 0:
            po_read.wait()
        total = total + dot_nt(up_grad, po[:, span])
    right[...] = total
    for copy in brought:
        copy.wait()


def last_block(inner, inner_at, outer, start, kept, old, gate, po_t, token, bring):
    size = outer.shape[0]
    tiles = kept.shape[1] // TILE
    return call(
        functools.partial(last_body, start, inner_at, [first for _, first, _ in bring]),
        "last_block",
        None,
        (1,),
        (inner, outer, kept, old, gate, po_t, token, *[a for a, _, _ in bring]),
        [INSIDE, INSIDE, INSIDE, INSIDE, OUTSIDE, ANYWHERE, ANYWHERE] + [OUTSIDE] * len(bring),
        [INSIDE] * (3 + len(bring)),
        [
            pltpu.VMEM(kept.shape, kept.dtype),
            pltpu.VMEM(old.shape, old.dtype),
            pltpu.VMEM((size, PROJ), jnp.float32),
            *[pltpu.VMEM((rows, a.shape[1]), a.dtype) for a, _, rows in bring],
        ],
        [
            pltpu.VMEM((tiles, size, TILE), gate.dtype),
            pltpu.VMEM(po_t.shape, po_t.dtype),
            pltpu.SemaphoreType.DMA((tiles,)),
            pltpu.SemaphoreType.DMA,
            pltpu.SemaphoreType.DMA((max(len(bring), 1),)),
        ],
        LIMIT,
        aliases={2: 0, 3: 1},
    )


def near_body(start, inner_at, bring, inner, outer, kept, old, gate, po, *rest):
    far, rest = rest[: len(bring)], rest[len(bring) :]
    _, _, right, *near = rest[: 3 + len(bring)]
    near_sems = rest[-1]
    size = outer.shape[0]
    brought = [
        pltpu.make_async_copy(a.at[pl.ds(first, b.shape[0])], b, near_sems.at[i])
        for i, (a, b, first) in enumerate(zip(far, near, bring))
    ]
    for copy in brought:
        copy.start()
    block = inner[pl.ds(inner_at, size), :] + outer[...]
    total = jnp.zeros((size, PROJ), jnp.float32)
    for t in range(kept.shape[1] // TILE):
        span = pl.ds(t * TILE, TILE)
        hidden_grad = old[pl.ds(start, size), span] + dot(block, kept[:, span])
        up_grad = (hidden_grad * silu(gate[:, span].astype(jnp.float32))).astype(jnp.bfloat16)
        total = total + dot_nt(up_grad, po[:, span])
    right[...] = total
    for copy in brought:
        copy.wait()


def near_block(inner, inner_at, outer, start, kept, old, gate, po, bring):
    return call(
        functools.partial(near_body, start, inner_at, [first for _, first, _ in bring]),
        "near_block",
        None,
        (1,),
        (inner, outer, kept, old, gate, po, *[a for a, _, _ in bring]),
        [INSIDE] * 6 + [OUTSIDE] * len(bring),
        [INSIDE] * (3 + len(bring)),
        [
            pltpu.VMEM(kept.shape, kept.dtype),
            pltpu.VMEM(old.shape, old.dtype),
            pltpu.VMEM((outer.shape[0], PROJ), jnp.float32),
            *[pltpu.VMEM((rows, a.shape[1]), a.dtype) for a, _, rows in bring],
        ],
        [pltpu.SemaphoreType.DMA((max(len(bring), 1),))],
        LIMIT,
        aliases={2: 0, 3: 1},
    )


def outer_body(masked, sent, *refs):
    *rights, grads, wide = refs
    left_t = masked[...] + sent[...].astype(jnp.float32)
    wide[...] = jnp.zeros_like(wide)
    start = 0
    terms = [None] * grads.shape[0]
    for right in rights:
        size = right.shape[0]
        s = start // LEN
        term = jnp.dot(
            left_t[:, start : start + size], right[...], precision=HIGHEST, preferred_element_type=jnp.float32
        )
        terms[s] = term if terms[s] is None else terms[s] + term
        start += size
    for s, term in enumerate(terms):
        wide[:, :PROJ] = term
        even = wide[pl.ds(0, PROJ // 2, stride=2), :]
        odd = wide[pl.ds(1, PROJ // 2, stride=2), :]
        rows = even + pltpu.roll(odd, PROJ, 1)
        for i in range(PROJ // 2):
            grads[s : s + 1, i * 2 * PROJ : (i + 1) * 2 * PROJ] = rows[i : i + 1, :]


def outer_products(masked, sent, rights):
    shape = (masked.shape[1] // LEN, PROJ * PROJ)
    (grads,) = call(
        outer_body,
        "outer_products",
        None,
        (1,),
        (masked, sent, *rights),
        [INSIDE] * (2 + len(rights)),
        [INSIDE],
        [pltpu.VMEM(shape, jnp.float32)],
        [pltpu.VMEM((PROJ, 2 * PROJ), jnp.float32)],
        LIMIT,
    )
    return grads


def small_kernel(body, name, where, *operands):
    (out,) = call(
        body,
        name,
        where,
        (1,),
        operands,
        [fixed(a.shape) for a in operands],
        [pl.BlockSpec(operands[0].shape, lambda j, where: (0, 0))],
        [jax.ShapeDtypeStruct(operands[0].shape, operands[0].dtype)],
        [],
        LIMIT,
    )
    return out


def score_sum(a, b):
    out = pltpu.VMEM(a.shape, a.dtype)
    (total,) = call(
        sum_body, "score_sum", None, (1,), (a, b), [INSIDE, INSIDE], [INSIDE], [out], [], LIMIT, flops=3 * 10**9
    )
    return total


def sum_body(*refs):
    a, b, out = refs[-3:]
    out[...] = a[...] + b[...]


def mask_body(where, a, out):
    out[...] = jnp.where(where[4] == 1, a[...], 0.0)


def score_body(grads, *rest):
    *parts, out = rest
    rows, width = parts[0].shape
    count = grads.shape[0]
    lane = lax.broadcasted_iota(jnp.int32, (rows, 128), 1)
    total = jnp.zeros((rows, 128), jnp.float32)
    for s in range(count):
        products = None
        for p, part in enumerate(parts):
            term = part[...] * grads[s : s + 1, my_part(p, width)]
            products = term if products is None else products + term
        total = jnp.where(lane == s, jnp.sum(products, axis=1, keepdims=True), total)
    out[...] = total.T[:count, :]


def score_parts(where, grads, parts):
    width = parts[0].shape[1]
    shape = (grads.shape[0], parts[0].shape[0])
    if width % 128:
        slices = [
            lax.dynamic_slice_in_dim(grads, where[FIRST_PART + p] * width, width, 1) for p in range(len(parts))
        ]
        return jnp.dot(jnp.concatenate(slices, axis=1), jnp.concatenate(parts, axis=1).T, precision=HIGHEST)
    (scores,) = call(
        score_body,
        "scores",
        None,
        (1,),
        (grads, *parts),
        [INSIDE] * (1 + len(parts)),
        [pl.BlockSpec(shape, lambda j: (0, 0))],
        [jax.ShapeDtypeStruct(shape, jnp.float32)],
        [],
        LIMIT,
    )
    return scores


def pieces(a):
    high = a.astype(jnp.bfloat16)
    rest = a - high.astype(jnp.float32)
    middle = rest.astype(jnp.bfloat16)
    low = (rest - middle.astype(jnp.float32)).astype(jnp.bfloat16)
    return high, middle, low


def update_body(scale, grads, hessian, out, new, out_sems):
    parts, _, width = new.shape
    high, middle, low = pieces(grads[:, my_part(0, new.shape[1])])
    left = jnp.concatenate([high, high, middle, middle, high, low], axis=0).T
    writes = []
    for t in range(parts):
        span = pl.ds(t * width, width)
        high, middle, low = pieces(grads[:, span])
        right = jnp.concatenate([high, middle, high, middle, low, high], axis=0)
        new[t] = hessian[:, span] + dot(left, right) * scale
        writes.append(pltpu.make_async_copy(new.at[t], out.at[:, span], out_sems.at[t]))
        writes[t].start()
    for write in writes:
        write.wait()


def update(grads, hessian):
    rows, length = hessian.shape
    count = grads.shape[0]
    parts = 8
    width = length // parts
    (updated,) = call(
        functools.partial(update_body, 1.0 / count),
        "hessian_update",
        None,
        (1,),
        (grads, hessian),
        [INSIDE, INSIDE],
        [ANYWHERE],
        [jax.ShapeDtypeStruct((rows, length), jnp.float32)],
        [pltpu.VMEM((parts, rows, width), jnp.float32), pltpu.SemaphoreType.DMA((parts,))],
        LIMIT,
        flops=1000,
    )
    return updated


def line_of_four(where, inputs, gate_pre, grad_out, w_down, proj_in, proj_out, early, late):
    send = functools.partial(lax.ppermute, axis_name="tensor")
    pairs = [(0, 1), (1, 0), (2, 3), (3, 2)]
    inner = [(1, 2), (2, 1)]
    outward = [(1, 0), (2, 3)]
    inward = [(0, 1), (3, 2)]
    tokens = grad_out.shape[0]
    halves = [slice(0, tokens // 2), slice(tokens // 2, tokens)]
    pair = send(grad_out, perm=pairs)
    own = [grad_out[half] for half in halves]
    mid_inner = [send(a, perm=inner) for a in own]
    in_part = input_block(where, inputs, proj_in.T)
    from_end = send(after(in_part, mid_inner[0]), perm=inward)
    acc, kept, begun = own_block(where, after(grad_out, in_part, *early), w_down)
    mid_outer = [send(after(a, begun), perm=outward) for a in mid_inner]
    side = small_kernel(sum_body, "side", where, in_part, after(from_end, begun, pair))
    end_inner = [send(pair[halves[0]], perm=inner)]
    end_inner.append(send(after(pair[halves[1]], mid_outer[0], side), perm=inner))
    total = small_kernel(sum_body, "total", where, side, send(side, perm=inner))
    masked = small_kernel(mask_body, "masked", where, total)
    sent = send(total.astype(jnp.bfloat16), perm=outward)

    acc, first = add_block(where, 1, [pair], w_down, after(acc, mid_outer[0]), begun, 2 * grad_out.size * w_down.shape[0])
    acc, second = add_block(where, 2, mid_inner + mid_outer, w_down, acc, first, 1000)

    sizes = [256] * (tokens // 256 - 1) + [128, 128]
    arrived, done = [total, total, total], [first, first, second]
    rights = []
    start = 0
    for n, size in enumerate(sizes):
        h, at = divmod(start, tokens // 2)
        ahead = arrived[n + 1] if n < 4 else arrived[n]
        end_outer = send(after(end_inner[h][at : at + size], ahead, done[n]), perm=outward)
        arrived.append(end_outer)
        bring = []
        if n + 1 < len(sizes):
            bring.append((gate_pre, start + size, sizes[n + 1]))
        if n == 0:
            bring.append((proj_out.T, 0, PROJ))
        if n == len(sizes) - 3:
            bring += [(a, 0, a.shape[0]) for a in (*early, late)]
        place = end_inner[h], at, end_outer, start, kept, acc
        if n == 0:
            kept, acc, right, *brought = last_block(*place, gate_pre, proj_out.T, second, bring)
            po_near = brought[1]
        else:
            kept, acc, right, *brought = near_block(*place, gate_near, po_near, bring)
        if n == len(sizes) - 3:
            *early, late = brought[1:]
        if bring:
            gate_near = brought[0]
        rights.append(right)
        done.append(right)
        start += size
    return outer_products(masked, sent, rights), early, late


def any_line(where, inputs, gate_pre, grad_out, w_down, proj_in, proj_out, early, late):
    in_part = jnp.dot(inputs, proj_in, preferred_element_type=jnp.float32)
    in_proj = lax.psum(in_part, "tensor").reshape(-1, LEN, PROJ)
    gathered = lax.all_gather(grad_out, "tensor", axis=1, tiled=True)
    up_grad = (dot_nt(gathered, w_down) * silu(gate_pre.astype(jnp.float32))).astype(jnp.bfloat16)
    out_part = jnp.dot(up_grad, proj_out, preferred_element_type=jnp.float32).reshape(-1, LEN, PROJ)
    grads = jnp.einsum("sti,stj->sij", in_proj, out_part, precision=HIGHEST)
    return grads.reshape(-1, PROJ * PROJ), early, late


def swap(a, axis, bit):
    return lax.ppermute(a, axis, [(i, i ^ bit) for i in range(lax.axis_size(axis))])


def bits(axis):
    return [1 << b for b in range(lax.axis_size(axis).bit_length() - 1)]


def xor_sum(a, axis):
    for bit in bits(axis):
        a = a + swap(a, axis, bit)
    return a


def positions():
    z, me, count = lax.axis_index("tensor"), lax.axis_index("dp"), lax.axis_size("dp")
    low = z < 2
    middle = jnp.logical_and(z > 0, z < 3)
    blocks = [z, z + 1 - 2 * (z % 2), jnp.where(low, 2, 1), jnp.where(low, 3, 0), middle]
    parts = [z * count + (me ^ s) for s in range(count)]
    return jnp.stack([a.astype(jnp.int32) for a in blocks + parts])


def on_device(inputs, gate_pre, grad_out, w_down, proj_in, proj_out, hessian, queries):
    where = positions()
    count = lax.axis_size("dp")
    parts = [queries] + [swap(queries, "dp", s) for s in range(1, count)]
    line = line_of_four if lax.axis_size("tensor") == 4 else any_line
    grads, parts, hessian = line(where, inputs, gate_pre, grad_out, w_down, proj_in, proj_out, parts, hessian)
    grads = xor_sum(grads, "tensor")

    scores = score_parts(where, grads, parts)
    all_grads = after(grads, scores)
    *first, last = reversed(bits("tensor"))
    for bit in bits("dp"):
        all_grads = jnp.concatenate([all_grads, swap(all_grads, "dp", bit)], axis=0)
    for bit in first:
        scores = score_sum(scores, swap(scores, "tensor", bit))
    others = swap(scores, "tensor", last)
    all_grads = after(all_grads, scores)
    row_count = hessian.shape[0]
    if row_count % 128:
        mine = lax.dynamic_slice_in_dim(all_grads, where[FIRST_PART] * row_count, row_count, 1)
        updated = hessian + jnp.dot(mine.T, all_grads, precision=HIGHEST) / all_grads.shape[0]
    else:
        updated = update(all_grads, hessian)
    updated, others = lax.optimization_barrier((updated, others))
    return (updated, scores + others)


def solution(mesh):
    return jax.shard_map(
        on_device,
        mesh=mesh,
        in_specs=(
            P(("groups", "dp"), "tensor"),
            P(("groups", "dp"), "tensor"),
            P(("groups", "dp"), "tensor"),
            P("tensor", None),
            P("tensor", None),
            P("tensor", None),
            P(("groups", "tensor", "dp"), None),
            P("groups", ("tensor", "dp")),
        ),
        out_specs=(P(("groups", "tensor", "dp"), None), P(("groups", "dp"), None)),
        check_vma=False,
    )
```
